256 devices in a mesh: seq: 64 (over z, y, core), head: 4 (over x).
Axes of the slice: x: 4, y: 4, z: 8, core: 2. Of those that a mesh axis runs over, the one named last changes fastest.
Arguments:
- inputs: float32 [8192, 1024], P('seq', 'head'), may hold values from -6 to 6
- proj_weights: float32 [1024, 3, 512], P(None, None, 'head'), may hold values from -0.1875 to 0.1875
- out_grads: float32 [8192, 512], P('seq', 'head'), may hold values from -6 to 6
Outputs:
- grad_inputs: float32 [8192, 1024], P('seq', 'head')
- grad_weights: float32 [1024, 3, 512], P('seq', None, 'head')
The draws below stay inside these ranges and needn't reach their ends.
All inputs are finite; a program needn't handle non-finite values.
Results may differ from the reference program's by a relative error of at most 0.0003.
Values sent between devices are 32-bit elements; how exact they have to be, the bound alone decides.
A program may use at most 128 MiB of HBM per device.

```python
import jax
import jax.numpy as jnp
import numpy as np
from jax import lax

D = 1024
HEADS = 8
HEAD_DIM = 64
T_DEV = 128
TOKENS = 8192


def steps_of(own_key, extent, shards, low, top_value):
    loudness, own = 1.0, jax.random.fold_in(own_key, 6)
    for position, parts in shards:
        heights = jnp.exp(jax.random.uniform(jax.random.fold_in(own, position), (parts,), jnp.float32, low / len(shards), top_value / len(shards)))
        loudness = loudness * jnp.repeat(heights, extent[position] // parts).reshape([-1 if axis == position else 1 for axis in range(len(extent))])
    return loudness


def scatter_about(key, extent, scale, bound, shards=(), held_as=jnp.bfloat16):
    result = scale * jax.random.normal(key, extent, jnp.float32)
    if shards:
        result = result * steps_of(key, extent, shards, -0.22, 0.18)
    return jnp.clip(result, -bound, bound).astype(held_as)


def setup_inputs(seed: int = 0) -> dict:
    key_of = jax.random.split(jax.random.key(seed), 4)
    inputs = scatter_about(key_of[0], (TOKENS, D), 1.0, 6.0, ((0, 64), (1, 4)), jnp.float32)
    proj_weights = scatter_about(key_of[1], (D, 3, HEADS * HEAD_DIM), D ** -0.5, 0.1875, ((2, 4),), jnp.float32)
    out_grads = scatter_about(key_of[2], (TOKENS, HEADS * HEAD_DIM), 1.0, 6.0, ((0, 64), (1, 4)), jnp.float32)
    return dict(inputs=inputs, proj_weights=proj_weights, out_grads=out_grads)


precise = lax.Precision.HIGHEST

def pair_tables(width):
    first_idx, second_idx = np.triu_indices(width)
    pair_scale = np.where(first_idx == second_idx, 1.0, np.sqrt(2.0))
    columns = np.arange(width)[:, None]
    table_one = jnp.asarray((columns == first_idx[None, :]) * pair_scale, jnp.float32)
    table_two = jnp.asarray((columns == second_idx[None, :]) * 1.0, jnp.float32)
    return (table_one, table_two)

def expand(vectors, table_one, table_two):
    part_one = jnp.einsum('hte,ef->htf', vectors, table_one, precision=precise)
    part_two = jnp.einsum('hte,ef->htf', vectors, table_two, precision=precise)
    return part_one * part_two

def forward(inputs, proj_weights):
    spans = TOKENS // T_DEV
    table_one, table_two = pair_tables(HEAD_DIM)
    pair_count = HEAD_DIM * (HEAD_DIM + 1) // 2

    def project(which_proj):
        flat = jnp.dot(inputs, proj_weights[:, which_proj, :], precision=precise)
        return flat.reshape(spans, T_DEV, HEADS, HEAD_DIM).transpose(0, 2, 1, 3)
    queries, keys_all, values = (project(0), project(1), project(2))
    causal = (jnp.arange(T_DEV)[:, None] >= jnp.arange(T_DEV)[None, :]).astype(jnp.float32)

    def span_step(carried, span_data):
        kv_state, kv_norms = carried
        query_blk, key_blk, value_blk = span_data
        query_feats = expand(query_blk, table_one, table_two) / HEAD_DIM
        key_feats = expand(key_blk, table_one, table_two)
        dots = jnp.einsum('hte,hse->hts', query_blk, key_blk, precision=precise)
        weights = dots * dots / HEAD_DIM * causal
        numerator = jnp.einsum('hts,hse->hte', weights, value_blk, precision=precise)
        numerator = numerator + jnp.einsum('htf,hfe->hte', query_feats, kv_state, precision=precise)
        denominator = 1.0 + lax.optimization_barrier(jnp.sum(weights, axis=-1)) + jnp.einsum('htf,hf->ht', query_feats, kv_norms, precision=precise)
        outputs = numerator / denominator[..., None]
        kv_state = kv_state + jnp.einsum('htf,hte->hfe', key_feats, value_blk, precision=precise)
        kv_norms = kv_norms + lax.optimization_barrier(jnp.sum(key_feats, axis=1))
        return ((kv_state, kv_norms), outputs)
    initial = (jnp.zeros((HEADS, pair_count, HEAD_DIM), jnp.float32), jnp.zeros((HEADS, pair_count), jnp.float32))
    _, outputs = lax.scan(jax.checkpoint(span_step), initial, (queries, keys_all, values))
    return outputs.transpose(0, 2, 1, 3).reshape(TOKENS, HEADS * HEAD_DIM)

def reference(inputs, proj_weights, out_grads):
    _, pullback = jax.vjp(forward, inputs, proj_weights)
    grad_inputs, grad_weights = pullback(out_grads)
    return (grad_inputs, grad_weights)
```

```python
import functools

import jax
import jax.numpy as jnp
from jax import lax
from jax.experimental import pallas as pl
from jax.experimental.pallas import tpu as pltpu
from jax.sharding import PartitionSpec as P

MESH = pl.DeviceIdType.MESH
F32, BF16 = jnp.float32, jnp.bfloat16
E = 64
L = 128
T = 256
NX, NY, NZ = 4, 4, 8
BLOCKS = 17
NORM_ROW = BLOCKS * E
ROWS = 1120
QUARTER = ROWS // NY
PIECE = 40
ZOWN = QUARTER // PIECE
VMEM = pl.BlockSpec(memory_space=pltpu.VMEM)
LIMIT = 56 * 2**20


def place():
    seq = lax.axis_index("seq")
    return lax.axis_index("head"), lax.rem(lax.div(seq, 2), NY), lax.div(seq, 2 * NY), lax.rem(seq, 2)


def device(x, y, z, c):
    return (z * (2 * NY) + y * 2 + c, x)


def greet(peers):
    barrier = pltpu.get_barrier_semaphore()
    for peer in peers:
        pl.semaphore_signal(barrier, inc=1, device_id=peer, device_id_type=MESH)
    pl.semaphore_wait(barrier, len(peers))


def remote(src, dst, send, recv, peer):
    return pltpu.make_async_remote_copy(
        src_ref=src, dst_ref=dst, send_sem=send, recv_sem=recv, device_id=peer, device_id_type=MESH
    )


def gather_kernel(x_ref, g_ref, xg, gg, xs, xr, fs, fr, cs, cr):
    x, y, z, c = place()
    sibling = device(x, y, z, 1 - c)
    peers = [device(lax.rem(x + d, NX), y, z, c) for d in range(1, NX)]
    greet([sibling] + peers)
    mine = pl.ds(pl.multiple_of(c * 128, 128), 128)
    over_x = [remote(x_ref, xg.at[x, mine], xs.at[d], xr.at[d], peers[d]) for d in range(NX - 1)]
    for copy in over_x:
        copy.start()
    own = remote(x_ref, xg.at[x, mine], cs.at[0], cr.at[0], sibling)
    own.start()
    grads = remote(g_ref, gg.at[mine], cs.at[1], cr.at[1], sibling)
    grads.start()
    xg[x, mine] = x_ref[...]
    gg[mine] = g_ref[...]
    forwards = []
    for d in (0, 2, 1):
        over_x[d].wait_recv()
        source = lax.rem(x + NX - 1 - d, NX)
        copy = remote(xg.at[source, mine], xg.at[source, mine], fs.at[d], fr.at[d], sibling)
        copy.start()
        forwards.append(copy)
    for copy in over_x:
        copy.wait_send()
    for copy in [own, grads] + forwards:
        copy.wait()


def gather(inputs, out_grads):
    dma = pltpu.SemaphoreType.DMA
    return pl.pallas_call(
        gather_kernel,
        out_shape=(jax.ShapeDtypeStruct((NX, T, 256), F32), jax.ShapeDtypeStruct((T, L), F32)),
        in_specs=[VMEM, VMEM],
        out_specs=(VMEM, VMEM),
        scratch_shapes=[dma((3,)), dma((3,)), dma((3,)), dma((3,)), dma((2,)), dma((2,))],
        compiler_params=pltpu.CompilerParams(collective_id=0, has_side_effects=True, vmem_limit_bytes=LIMIT),
        name="gather",
    )(inputs, out_grads)


def scan_kernel(reverse, st, out, ry, py, tot, rz, pz, ez, oy, s1, r1, s2, r2, s3, r3, s4, r4):
    x, y, z, c = place()
    py_peers = [device(x, lax.rem(y + d, NY), z, c) for d in range(1, NY)]
    pz_peers = [device(x, y, lax.rem(z + d, NZ), c) for d in range(1, NZ)]
    greet(py_peers + pz_peers)

    def quarter(index):
        return pl.ds(pl.multiple_of(index * QUARTER, 8), QUARTER)

    def piece(index):
        return pl.ds(pl.multiple_of(index * PIECE, 8), PIECE)

    def ordered(n):
        return range(n - 1, -1, -1) if reverse else range(n)

    first = [
        remote(st.at[quarter(lax.rem(y + d, NY))], ry.at[d], s1.at[d], r1.at[d], py_peers[d - 1]) for d in range(1, NY)
    ]
    for copy in first:
        copy.start()
    ry[0] = st[quarter(y)]
    for copy in first:
        copy.wait_recv()
    running = jnp.zeros((QUARTER, L), F32)
    for index in ordered(NY):
        py[index] = running
        running = running + ry[lax.rem(y + NY - index, NY)]
    tot[...] = running

    second, third = [], []
    for d in range(1, NZ):
        target = lax.rem(z + d, NZ)
        second.append(remote(tot.at[piece(lax.min(target, ZOWN - 1))], rz.at[d], s2.at[d], r2.at[d], pz_peers[d - 1]))
        third.append(remote(pz.at[target], ez.at[piece(lax.min(z, ZOWN - 1))], s3.at[d], r3.at[d], pz_peers[d - 1]))

        @pl.when(target < ZOWN)
        def _():
            second[-1].start()

    @pl.when(z < ZOWN)
    def _():
        rz[0] = tot[piece(z)]
        for copy in second:
            copy.wait_recv()
        running = jnp.zeros((PIECE, L), F32)
        for index in ordered(NZ):
            pz[index] = running
            running = running + rz[lax.rem(z + NZ - index, NZ)]
        for copy in third:
            copy.start()
        ez[piece(z)] = pz[z]

    for d in range(1, NZ):

        @pl.when(lax.rem(z + NZ - d, NZ) < ZOWN)
        def _():
            third[d - 1].wait_recv()

    fourth = []
    for d in range(1, NY):
        oy[d] = ez[...] + py[lax.rem(y + d, NY)]
        fourth.append(remote(oy.at[d], out.at[quarter(y)], s4.at[d], r4.at[d], py_peers[d - 1]))
        fourth[-1].start()
    out[quarter(y)] = ez[...] + py[y]
    for copy in first:
        copy.wait_send()
    for d in range(1, NZ):

        @pl.when(lax.rem(z + d, NZ) < ZOWN)
        def _():
            second[d - 1].wait_send()

    @pl.when(z < ZOWN)
    def _():
        for copy in third:
            copy.wait_send()

    for copy in fourth:
        copy.wait()


def scan(state, reverse):
    dma = pltpu.SemaphoreType.DMA
    return pl.pallas_call(
        functools.partial(scan_kernel, reverse),
        out_shape=jax.ShapeDtypeStruct((ROWS, L), F32),
        in_specs=[VMEM],
        out_specs=VMEM,
        scratch_shapes=[
            pltpu.VMEM((NY, QUARTER, L), F32),
            pltpu.VMEM((NY, QUARTER, L), F32),
            pltpu.VMEM((QUARTER, L), F32),
            pltpu.VMEM((NZ, PIECE, L), F32),
            pltpu.VMEM((NZ, PIECE, L), F32),
            pltpu.VMEM((QUARTER, L), F32),
            pltpu.VMEM((NY, QUARTER, L), F32),
        ]
        + [dma((NY,)), dma((NY,)), dma((NZ,)), dma((NZ,)), dma((NZ,)), dma((NZ,)), dma((NY,)), dma((NY,))],
        compiler_params=pltpu.CompilerParams(
            collective_id=2 if reverse else 1, has_side_effects=True, vmem_limit_bytes=LIMIT
        ),
        name="later" if reverse else "earlier",
    )(state)


def split(value):
    high = value.astype(BF16)
    return high, (value - high.astype(F32)).astype(BF16)


NN = (((1,), (0,)), ((), ()))
NT = (((1,), (1,)), ((), ()))
TN = (((0,), (0,)), ((), ()))


def dot(a, b, dims):
    return lax.dot_general(a, b, dims, preferred_element_type=F32)


def dot3(a, b, dims):
    return dot(a[0], b[0], dims) + (dot(a[0], b[1], dims) + dot(a[1], b[0], dims))


def lane():
    return lax.broadcasted_iota(jnp.int32, (1, L), 1)


def roll(value, shift):
    return pltpu.roll(value, shift, 1)


def shifted(double, block):
    return jnp.where(lane() < E, roll(double, E - 2 * block), roll(double, E - 1 - 2 * block))


def query_scale(block):
    distance = 2 * block + (lane() >= E).astype(jnp.int32)
    once = jnp.where(distance > 32, 0.0, 1.0 / E)
    return jnp.where((distance > 0) & (distance < 32), 2.0 / E, once)


def unshifted(term, block):
    low = lane() < E
    return roll(jnp.where(low, term, 0.0), 2 * block) + roll(jnp.where(low, 0.0, term), 2 * block + 1)


def folded(value):
    return value + roll(value, E)


def columns_of(vectors, extra):
    both = jnp.concatenate([vectors, jnp.broadcast_to(extra, (T, E))], axis=1).T
    high = both.astype(BF16).astype(F32)
    low = both - high
    return jnp.concatenate([high[:E], low[:E], high[E : E + 8], low[E : E + 8]], axis=0).astype(BF16)


def state_block(columns, feats):
    product = dot(columns, feats, NN)
    product = product[:, :L] + product[:, L:]
    return product[:E] + product[E : 2 * E], product[2 * E : 2 * E + 1] + product[2 * E + 8 : 2 * E + 9]


def feature_pair(features):
    return jnp.concatenate(split(features), axis=1)


def rows_of(vectors, extra):
    high, low = split(vectors)
    extra_high, extra_low = split(extra)
    at = lax.broadcasted_iota(jnp.int32, (1, 16), 1)
    tail = jnp.where((at == 0) | (at == 8), extra_high.astype(F32), jnp.where(at == 1, extra_low.astype(F32), 0.0))
    return jnp.concatenate([high, low, high, tail.astype(BF16)], axis=1)


def state_parts(state_ref, block):
    at = pl.multiple_of(block * E, E)
    high, low = split(state_ref[pl.ds(at, E), :])
    norm = jnp.broadcast_to(state_ref[pl.ds(NORM_ROW + block, 1), :], (8, L))
    norm_high = norm.astype(BF16).astype(F32)
    norms = jnp.concatenate([norm_high, norm - norm_high], axis=0).astype(BF16)
    return high, low, norms


def project_kernel(xg, w, qq_ref, kk_ref, v_ref, st):
    c = lax.rem(lax.axis_index("seq"), 2)
    sums = [jnp.zeros((T, L), F32) for _ in range(3)]
    for b in range(NX):
        feats = split(xg[b])
        for i in range(3):
            sums[i] = sums[i] + dot3(feats, split(w[i, b * 256 : (b + 1) * 256, :]), NN)

    def doubled(both):
        other = roll(both, E)
        low = lane() < E
        return jnp.where(low == (c == 0), both, other)

    kk = doubled(sums[1])
    v = doubled(sums[2])[:, :E]
    qq_ref[...] = doubled(sums[0])
    kk_ref[...] = kk
    v_ref[...] = v
    columns = columns_of(v, jnp.ones((T, 1), F32))
    st[NORM_ROW:, :] = jnp.zeros((ROWS - NORM_ROW, L), F32)

    def step(block, carry):
        state, norm = state_block(columns, feature_pair(kk * shifted(kk, block)))
        st[pl.ds(pl.multiple_of(block * E, E), E), :] = state
        st[pl.ds(NORM_ROW + block, 1), :] = norm
        return carry

    lax.fori_loop(0, BLOCKS, step, 0, unroll=True)


def local(kernel, outs, args, name, scratch=()):
    return pl.pallas_call(
        kernel,
        out_shape=tuple(jax.ShapeDtypeStruct(shape, F32) for shape in outs),
        in_specs=[VMEM] * len(args),
        out_specs=tuple(VMEM for _ in outs),
        scratch_shapes=list(scratch),
        compiler_params=pltpu.CompilerParams(vmem_limit_bytes=LIMIT),
        name=name,
    )(*args)


def query_kernel(qq_ref, kk_ref, v_ref, gg, sp, dq_ref, dk_ref, dv_ref, zt, feats):
    c = lax.rem(lax.axis_index("seq"), 2)
    qq = qq_ref[...]
    q, k, v = qq[:, :E], kk_ref[:, :E], v_ref[...]
    qs, ks, vs = split(q), split(k), split(v)
    both = gg[...]
    cot = jnp.where(c == 0, both, roll(both, E))[:, :E]
    causal = lax.broadcasted_iota(jnp.int32, (T, T), 0) >= lax.broadcasted_iota(jnp.int32, (T, T), 1)
    dots = dot3(qs, ks, NT)
    weights = jnp.where(causal, dots * dots * (1.0 / E), 0.0)
    ws = split(weights)

    def forward(block, total):
        pair = feature_pair(qq * shifted(qq, block) * query_scale(block))
        feats[block] = pair
        high, low, norms = state_parts(sp, block)
        rows = jnp.concatenate([high, low, norms], axis=0)
        return total + dot(pair, jnp.concatenate([rows, rows], axis=1), NT)

    total = lax.fori_loop(0, BLOCKS, forward, jnp.zeros((T, 2 * E + 16), F32), unroll=True)
    numer = dot3(ws, vs, NN) + total[:, :E] + total[:, E : 2 * E]
    denom = 1.0 + jnp.sum(weights, axis=1, keepdims=True) + total[:, L : L + 1] + total[:, L + 8 : L + 9]
    inverse = 1.0 / denom
    grad_numer = cot * inverse
    grad_denom = -jnp.sum(grad_numer * numer, axis=1, keepdims=True) * inverse
    gs = split(grad_numer)
    columns = columns_of(grad_numer, grad_denom)
    rows_g = rows_of(grad_numer, grad_denom)
    zt[NORM_ROW:, :] = jnp.zeros((ROWS - NORM_ROW, L), F32)

    def backward(block, carry):
        one, two = carry
        state, norm = state_block(columns, feats[block])
        zt[pl.ds(pl.multiple_of(block * E, E), E), :] = state
        zt[pl.ds(NORM_ROW + block, 1), :] = norm
        high, low, norms = state_parts(sp, block)
        grad = dot(rows_g, jnp.concatenate([high, high, low, norms], axis=0), NN) * query_scale(block)
        return one + grad * shifted(qq, block), two + unshifted(grad * qq, block)

    zero = jnp.zeros((T, L), F32)
    one, two = lax.fori_loop(0, BLOCKS, backward, (zero, zero), unroll=True)
    grad_scores = jnp.where(causal, dot3(gs, vs, NT) + grad_denom, 0.0)
    grad_dots = split(grad_scores * dots * (2.0 / E))
    dq_ref[...] = folded(one + two)[:, :E] + dot3(grad_dots, ks, NN)
    dk_ref[...] = dot3(grad_dots, qs, TN)
    dv_ref[...] = dot3(ws, gs, TN)


def key_kernel(kk_ref, v_ref, zp, dq_ref, dk_ref, dv_ref, xg, w, dx, dw):
    c = lax.rem(lax.axis_index("seq"), 2)
    kk, v = kk_ref[...], v_ref[...]
    rows_v = rows_of(v, jnp.ones((T, 1), F32))

    def step(block, carry):
        total, one, two = carry
        shift = shifted(kk, block)
        high, low, norms = state_parts(zp, block)
        rows = jnp.concatenate([high, low], axis=0)
        total = total + dot(feature_pair(kk * shift), jnp.concatenate([rows, rows], axis=1), NT)
        grad = dot(rows_v, jnp.concatenate([high, high, low, norms], axis=0), NN)
        return total, one + grad * shift, two + unshifted(grad * kk, block)

    zero = jnp.zeros((T, L), F32)
    total, one, two = lax.fori_loop(0, BLOCKS, step, (zero, zero, zero), unroll=True)
    dv = dv_ref[...] + total[:, :E] + total[:, E:]
    dk = dk_ref[...] + folded(one + two)[:, :E]
    dq = dq_ref[...]
    low = lane() < E
    qk = jnp.concatenate([dq, dk], axis=1)
    vv = jnp.concatenate([dv, dv], axis=1)
    grads = [jnp.concatenate([g, g], axis=1) for g in (dq, dk)] + [vv]
    padded = [split(jnp.where(low == (c == 0), g, 0.0)) for g in grads]
    qk_vv = split(jnp.concatenate([qk, vv], axis=1))
    for b in range(NX):
        part = jnp.zeros((T, 256), F32)
        for i in range(3):
            part = part + dot3(padded[i], split(w[i, b * 256 : (b + 1) * 256, :]), NT)
        dx[0, b] = part[:128]
        dx[1, b] = part[128:]
        grad = dot3(split(xg[b]), qk_vv, TN)
        for i in range(8):
            rows = grad[i * 32 : (i + 1) * 32]
            chip = b * 8 + i
            dw[chip % NY, chip // NY, :32] = rows[:, :L]
            dw[chip % NY, chip // NY, 32:] = jnp.where(low, rows[:16, L:], rows[16:, L:])


def reduce_kernel(dx, dw, gx, gw, rc, sx, rx, ry, ty, rz, own, other, cs, cr, xs, xr, s1, r1, s2, r2):
    x, y, z, c = place()
    sibling = device(x, y, z, 1 - c)
    px = [device(lax.rem(x + d, NX), y, z, c) for d in range(1, NX)]
    py = [device(x, lax.rem(y + d, NY), z, c) for d in range(1, NY)]
    pz = [device(x, y, lax.rem(z + d, NZ), c) for d in range(1, NZ)]
    greet([sibling] + px + py + pz)
    across = remote(dx.at[1 - c], rc, cs.at[0], cr.at[0], sibling)
    across.start()
    first = [remote(dw.at[lax.rem(y + d, NY)], ry.at[d], s1.at[d], r1.at[d], py[d - 1]) for d in range(1, NY)]
    for copy in first:
        copy.start()
    across.wait_recv()
    sx[...] = dx[c] + rc[...]
    over_x = [remote(sx.at[lax.rem(x + d, NX)], rx.at[d], xs.at[d], xr.at[d], px[d - 1]) for d in range(1, NX)]
    for copy in over_x:
        copy.start()
    for copy in first:
        copy.wait_recv()
    ty[...] = dw[y] + ry[1] + ry[2] + ry[3]
    second = [remote(ty.at[lax.rem(z + d, NZ)], rz.at[d], s2.at[d], r2.at[d], pz[d - 1]) for d in range(1, NZ)]
    for copy in second:
        copy.start()
    for copy in over_x:
        copy.wait_recv()
    gx[...] = sx[x] + rx[1] + rx[2] + rx[3]
    total = ty[z]
    for d in range(1, NZ):
        second[d - 1].wait_recv()
        total = total + rz[d]
    own[...] = total
    swap = remote(own, other, cs.at[1], cr.at[1], sibling)
    swap.start()
    for copy in first + second + over_x:
        copy.wait_send()
    across.wait_send()
    swap.wait()
    low = lane() < E
    mine = pl.ds(pl.multiple_of(c * 16, 16), 16)

    def halves(rows):
        a, b = own[rows], other[rows]
        return jnp.where(c == 0, a, b), jnp.where(c == 0, b, a)

    zero, one = halves(mine)
    gw[:, 0, :] = jnp.where(low, zero, roll(one, E))
    gw[:, 1, :] = jnp.where(low, roll(zero, E), one)
    zero, one = halves(pl.ds(32, 16))
    gw[:, 2, :] = jnp.where(c == 0, jnp.where(low, zero, roll(one, E)), jnp.where(low, roll(zero, E), one))


def reduce(dx, dw):
    dma = pltpu.SemaphoreType.DMA
    return pl.pallas_call(
        reduce_kernel,
        out_shape=(jax.ShapeDtypeStruct((128, 256), F32), jax.ShapeDtypeStruct((16, 3, L), F32)),
        in_specs=[VMEM, VMEM],
        out_specs=(VMEM, VMEM),
        scratch_shapes=[
            pltpu.VMEM((NX, 128, 256), F32),
            pltpu.VMEM((NX, 128, 256), F32),
            pltpu.VMEM((NX, 128, 256), F32),
            pltpu.VMEM((NY, NZ, 48, L), F32),
            pltpu.VMEM((NZ, 48, L), F32),
            pltpu.VMEM((NZ, 48, L), F32),
            pltpu.VMEM((48, L), F32),
            pltpu.VMEM((48, L), F32),
        ]
        + [dma((2,)), dma((2,)), dma((NX,)), dma((NX,)), dma((NY,)), dma((NY,)), dma((NZ,)), dma((NZ,))],
        compiler_params=pltpu.CompilerParams(collective_id=3, has_side_effects=True, vmem_limit_bytes=LIMIT),
        name="reduce",
    )(dx, dw)


def per_device(inputs, proj_weights, out_grads):
    xg, gg = gather(inputs, out_grads)
    w = proj_weights.transpose(1, 0, 2)
    qq, kk, v, st = local(project_kernel, [(T, L), (T, L), (T, E), (ROWS, L)], [xg, w], "project")
    sp = scan(st, False)
    dq, dk, dv, zt = local(
        query_kernel,
        [(T, E), (T, E), (T, E), (ROWS, L)],
        [qq, kk, v, gg, sp],
        "query",
        [pltpu.VMEM((BLOCKS, T, 2 * L), BF16)],
    )
    zp = scan(zt, True)
    dx, dw = local(
        key_kernel, [(2, NX, 128, 256), (NY, NZ, 48, L)], [kk, v, zp, dq, dk, dv, xg, w], "key"
    )
    return reduce(dx, dw)


def solution(mesh):
    return jax.shard_map(
        per_device,
        mesh=mesh,
        in_specs=(P("seq", "head"), P(None, None, "head"), P("seq", "head")),
        out_specs=(P("seq", "head"), P("seq", None, "head")),
        check_vma=False,
    )
```

```python
import functools
import types

import jax
import jax.numpy as jnp
from jax import lax
from jax.experimental import pallas as pl
from jax.experimental.pallas import tpu as pltpu
from jax.sharding import PartitionSpec as P

MESH = pl.DeviceIdType.MESH
F32, BF16 = jnp.float32, jnp.bfloat16
E = 64
L = 128
T = 256
NX, NY, NZ = 4, 4, 8
LAST = 16
CHUNKS = ((128, 16, 8), (144, 24, 6))
VMEM = pl.BlockSpec(memory_space=pltpu.VMEM)
LIMIT = 56 * 2**20


def place():
    seq = lax.axis_index("seq")
    return lax.axis_index("head"), lax.rem(lax.div(seq, 2), NY), lax.div(seq, 2 * NY), lax.rem(seq, 2)


def device(x, y, z, c):
    return (z * (2 * NY) + y * 2 + c, x)


def remote(src, dst, send, recv, peer):
    return pltpu.make_async_remote_copy(
        src_ref=src, dst_ref=dst, send_sem=send, recv_sem=recv, device_id=peer, device_id_type=MESH
    )


def split(value):
    high = value.astype(BF16)
    return high, (value - high.astype(F32)).astype(BF16)


NN = (((1,), (0,)), ((), ()))
NT = (((1,), (1,)), ((), ()))
TN = (((0,), (0,)), ((), ()))


def dot(a, b, dims):
    return lax.dot_general(a, b, dims, preferred_element_type=F32)


def dot3(a, b, dims):
    return dot(a[0], b[0], dims) + (dot(a[0], b[1], dims) + dot(a[1], b[0], dims))


def lower():
    return lax.broadcasted_iota(jnp.int32, (1, L), 1) < E


def roll(value, shift):
    return pltpu.roll(value, shift, 1)


def shifted(double, block):
    return jnp.where(lower(), roll(double, E - 2 * block), roll(double, E - 1 - 2 * block))


def query_scale(block):
    distance = 2 * block + jnp.where(lower(), 0, 1)
    once = jnp.where(distance > 32, 0.0, 1.0 / E)
    return jnp.where((distance > 0) & (distance < 32), 2.0 / E, once)


def unshifted(term, block):
    low = lower()
    return roll(jnp.where(low, term, 0.0), 2 * block) + roll(jnp.where(low, 0.0, term), 2 * block + 1)


def folded(value):
    return value + roll(value, E)


def columns_of(double):
    high, low = split(double.T)
    return jnp.concatenate([high[:E], low[:E]], axis=0)


def state_block(columns, feats):
    product = dot(columns, feats, NN)
    product = product[:, :L] + product[:, L:]
    return product[:E] + product[E:]


def feature_pair(features):
    return jnp.concatenate(split(features), axis=1)


def rows_of(double):
    high, low = split(double)
    return jnp.concatenate([high[:, :E], low[:, :E], high[:, :E]], axis=1)


def apply_state(pair, parts):
    rows = jnp.concatenate(parts, axis=0)
    return dot(pair, jnp.concatenate([rows, rows], axis=1), NT)


def apply_rows(rows, parts):
    high, low = parts
    return dot(rows, jnp.concatenate([high, high, low], axis=0), NN)


class Chunk:
    def __init__(self, at, chunk, reverse, bufs, sems):
        self.rows, self.piece, self.owners = CHUNKS[chunk]
        self.at, self.reverse = at, reverse
        self.st, self.ry, self.py, self.tot, self.rz, self.pz, self.ez, self.oy, self.out = bufs
        s1, r1, s2, r2, s3, r3, s4, r4 = [sem.at[int(reverse), chunk] for sem in sems]
        y, z = at.y, at.z
        self.first = [None] + [
            remote(self.st.at[lax.rem(y + d, NY)], self.ry.at[d], s1.at[d], r1.at[d], at.py[d]) for d in range(1, NY)
        ]
        self.second, self.third = [None], [None]
        for d in range(1, NZ):
            target = lax.rem(z + d, NZ)
            self.second.append(
                remote(self.tot.at[self.part(target)], self.rz.at[d], s2.at[d], r2.at[d], at.pz[d])
            )
            self.third.append(remote(self.pz.at[target], self.ez.at[self.part(z)], s3.at[d], r3.at[d], at.pz[d]))
        self.fourth = [None] + [
            remote(self.oy.at[d], self.out.at[y], s4.at[d], r4.at[d], at.py[d]) for d in range(1, NY)
        ]

    def part(self, index):
        return pl.ds(pl.multiple_of(lax.min(index, self.owners - 1) * self.piece, 8), self.piece)

    def owner(self, index, act):
        if self.owners == NZ:
            act()
        else:
            pl.when(index < self.owners)(act)

    def ordered(self, n):
        return range(n - 1, -1, -1) if self.reverse else range(n)

    def totals(self):
        y, z = self.at.y, self.at.z
        for d in (1, 3, 2):
            self.first[d].wait_recv()
        running = jnp.zeros((self.rows, L), F32)
        for index in self.ordered(NY):
            self.py[index] = running
            running = running + self.ry[lax.rem(y + NY - index, NY)]
        self.tot[...] = running
        for d in (4, 3, 5, 2, 6, 1, 7):
            self.owner(lax.rem(z + d, NZ), self.second[d].start)

    def prefixes(self):
        z = self.at.z

        def act():
            self.rz[0] = self.tot[self.part(z)]
            for copy in self.second[1:]:
                copy.wait_recv()
            running = jnp.zeros((self.piece, L), F32)
            for index in self.ordered(NZ):
                self.pz[index] = running
                running = running + self.rz[lax.rem(z + NZ - index, NZ)]
            for d in (4, 3, 5, 2, 6, 1, 7):
                self.third[d].start()
            self.ez[self.part(z)] = self.pz[z]

        self.owner(z, act)

    def spread(self):
        y, z = self.at.y, self.at.z
        for d in range(1, NZ):
            self.owner(lax.rem(z + NZ - d, NZ), self.third[d].wait_recv)
        for d in (2, 1, 3):
            self.oy[d] = self.ez[...] + self.py[lax.rem(y + d, NY)]
            self.fourth[d].start()
        self.out[y] = self.ez[...] + self.py[y]

    def close(self):
        for d in range(1, NY):
            self.first[d].wait_send()
            self.fourth[d].wait_send()
        for d in range(1, NZ):
            self.owner(lax.rem(self.at.z + d, NZ), self.second[d].wait_send)

        def act():
            for copy in self.third[1:]:
                copy.wait_send()

        self.owner(self.at.z, act)


def fill(at, chunks, make, tail):
    for h, chunk in enumerate(chunks):
        if h == 1:
            rows = tail()
            for q in range(NY):
                chunk.st[q, 2 * E :] = rows[q * 16 : (q + 1) * 16]
        for d in (2, 1, 3, 0):
            q = lax.rem(at.y + d, NY)

            def step(i, carry):
                rows = pl.ds(pl.multiple_of(i * E, E), E)
                block = make(8 * h + 2 * q + i)
                if d == 0:
                    chunk.ry[0, rows] = block
                else:
                    chunk.st[q, rows] = block
                return carry

            lax.fori_loop(0, 2, step, 0, unroll=True)
            if d:
                chunk.first[d].start()
        if h == 1:
            chunk.ry[0, 2 * E :] = chunk.st[at.y, 2 * E :]


def tail_of(chunk):
    return jnp.concatenate([chunk.out[q, 2 * E :] for q in range(NY)], axis=0)


def over_blocks(at, chunks, step, carry, wait):
    for h, chunk in enumerate(chunks):
        for d in (0, 1, 3, 2):
            if wait and d:
                chunk.fourth[d].wait_recv()
            q = lax.rem(at.y + NY - d, NY)

            def inner(i, carry):
                rows = pl.ds(pl.multiple_of(i * E, E), E)
                return step(8 * h + 2 * q + i, split(chunk.out[q, rows]), carry)

            carry = lax.fori_loop(0, 2, inner, carry, unroll=True)
    return carry


def fused_kernel(names, *refs):
    r = types.SimpleNamespace(**dict(zip(names, refs)))
    x, y, z, c = place()
    at = types.SimpleNamespace(x=x, y=y, z=z, c=c)
    sibling = device(x, y, z, 1 - c)
    at.px = [None] + [device(lax.rem(x + d, NX), y, z, c) for d in range(1, NX)]
    at.py = [None] + [device(x, lax.rem(y + d, NY), z, c) for d in range(1, NY)]
    at.pz = [None] + [device(x, y, lax.rem(z + d, NZ), c) for d in range(1, NZ)]
    low = lower()

    load = pltpu.make_async_copy(r.w_in, r.w, r.wsem)
    load.start()
    barrier = pltpu.get_barrier_semaphore()
    peers = [sibling] + at.px[1:] + at.py[1:] + at.pz[1:]
    for peer in peers:
        pl.semaphore_signal(barrier, inc=1, device_id=peer, device_id_type=MESH)
    pl.semaphore_wait(barrier, len(peers))

    mine = pl.ds(pl.multiple_of(c * 128, 128), 128)
    over_x = [None] + [remote(r.x_in, r.xg.at[x, mine], r.xs.at[d], r.xr.at[d], at.px[d]) for d in range(1, NX)]
    for d in (2, 1, 3):
        over_x[d].start()
    own = remote(r.x_in, r.xg.at[x, mine], r.cs.at[0], r.cr.at[0], sibling)
    own.start()
    grads = remote(r.g_in, r.gg.at[mine], r.cs.at[1], r.cr.at[1], sibling)
    grads.start()
    r.xg[x, mine] = r.x_in[...]
    r.gg[mine] = r.g_in[...]
    load.wait()

    def split_weights(b, carry):
        rows = pl.ds(pl.multiple_of(b * 256, 256), 256)
        for i in range(3):
            r.wh[i, rows], r.wl[i, rows] = split(r.w[i, rows])
        return carry

    lax.fori_loop(0, NX, split_weights, 0)

    def project(b, sums):
        rows = pl.ds(pl.multiple_of(b * 256, 256), 256)
        r.xh[b], r.xl[b] = split(r.xg[b])
        feats = (r.xh[b], r.xl[b])
        return [sums[i] + dot3(feats, (r.wh[i, rows], r.wl[i, rows]), NN) for i in range(3)]

    own.wait_recv()
    sums = project(x, [jnp.zeros((T, L), F32) for _ in range(3)])
    forwards = [None] * NX
    order = (1, 3, 2)
    for d in order:
        over_x[d].wait_recv()
        source = lax.rem(x + NX - d, NX)
        forwards[d] = remote(r.xg.at[source, mine], r.xg.at[source, mine], r.fs.at[d], r.fr.at[d], sibling)
        forwards[d].start()
        forwards[d].wait_recv()
        sums = project(source, sums)

    def doubled(both):
        return jnp.where(low == (c == 0), both, roll(both, E))

    r.qq[...] = doubled(sums[0])
    r.kk[...] = doubled(sums[1])
    r.vv[...] = doubled(sums[2])

    scans = []
    for reverse in (False, True):
        bufs = [[buf[int(reverse)][h] for buf in r.bufs] for h in range(2)]
        scans.append([Chunk(at, h, reverse, bufs[h], r.sems) for h in range(2)])
    earlier, later = scans

    r.cols[...] = columns_of(r.vv[...])

    def key_block(block):
        kk = r.kk[...]
        return state_block(r.cols[...], feature_pair(kk * shifted(kk, block)))

    def key_tail():
        ks = split(r.kk[...])
        norm = dot3([k[:, :E] for k in ks], ks, TN)
        return jnp.where(low, key_block(LAST), norm)

    fill(at, earlier, key_block, key_tail)
    earlier[0].totals()
    earlier[1].totals()

    def query_feature(block, carry):
        qq = r.qq[...]
        r.feats[block] = feature_pair(qq * shifted(qq, block) * query_scale(block))
        return carry

    lax.fori_loop(0, LAST + 1, query_feature, 0)
    earlier[0].prefixes()
    earlier[1].prefixes()
    grads.wait_recv()
    causal = lax.broadcasted_iota(jnp.int32, (T, T), 0) >= lax.broadcasted_iota(jnp.int32, (T, T), 1)
    qs, ks, vs = [split(ref[...]) for ref in (r.qq, r.kk, r.vv)]
    r.dots[...] = dot3([v[:, :E] for v in qs], [v[:, :E] for v in ks], NT)
    weights = jnp.where(causal, r.dots[...] * r.dots[...] * (1.0 / E), 0.0)
    r.wgh[...], r.wgl[...] = split(weights)
    r.numer[...] = dot3((r.wgh[...], r.wgl[...]), vs, NN)
    r.denom[...] = jnp.broadcast_to(1.0 + jnp.sum(weights, axis=1, keepdims=True), (T, L))
    earlier[0].spread()
    earlier[1].spread()

    def forward(block, parts, total):
        return total + apply_state(r.feats[block], parts)

    total = over_blocks(at, earlier, forward, jnp.zeros((T, L), F32), True)
    tail = split(tail_of(earlier[1]))
    total = total + apply_state(r.feats[LAST], tail)
    qs = split(r.qq[...])
    normed = jnp.where(low, 0.0, dot3([v[:, :E] for v in qs], tail, NN))
    denom = r.denom[...] + jnp.sum(normed * r.qq[...], axis=1, keepdims=True) * (1.0 / E)
    inverse = 1.0 / denom
    grad_numer = doubled(r.gg[...]) * inverse
    grad_denom = -0.5 * jnp.sum(grad_numer * (r.numer[...] + folded(total)), axis=1, keepdims=True) * inverse
    r.gn[...] = grad_numer
    r.gd[...] = grad_denom

    r.cols[...] = columns_of(grad_numer)

    def query_block(block):
        return state_block(r.cols[...], r.feats[block])

    def query_tail():
        qq = r.qq[...]
        norm = dot3(split((qq * r.gd[...])[:, :E]), split(qq), TN) * (1.0 / E)
        return jnp.where(low, query_block(LAST), norm)

    fill(at, later, query_block, query_tail)
    later[0].totals()
    later[1].totals()

    r.rows[...] = rows_of(r.gn[...])

    def backward(block, parts, carry):
        one, two = carry
        qq = r.qq[...]
        grad = apply_rows(r.rows[...], parts) * query_scale(block)
        return one + grad * shifted(qq, block), two + unshifted(grad * qq, block)

    r.one[...] = normed * r.gd[...] * (2.0 / E)
    tail = split(tail_of(earlier[1]))
    carry = backward(LAST, tail, (r.one[...], jnp.zeros((T, L), F32)))
    one, two = over_blocks(at, earlier, backward, carry, False)
    r.one[...] = folded(one + two)
    later[0].prefixes()
    later[1].prefixes()
    qs, ks, vs, gs = [split(ref[...]) for ref in (r.qq, r.kk, r.vv, r.gn)]
    grad_scores = dot3([v[:, :E] for v in gs], [v[:, :E] for v in vs], NT) + r.gd[:, :1]
    grad_dots = split(jnp.where(causal, grad_scores, 0.0) * r.dots[...] * (2.0 / E))
    r.dq[...] = r.one[...] + dot3(grad_dots, ks, NN)
    r.dk[...] = dot3(grad_dots, qs, TN)
    r.dv[...] = dot3((r.wgh[...], r.wgl[...]), gs, TN)
    r.rows[...] = rows_of(r.vv[...])
    later[0].spread()
    later[1].spread()

    def keys(block, parts, carry, mask=None):
        total, one, two = carry
        kk = r.kk[...]
        shift = shifted(kk, block)
        if mask is not None:
            shift, kk = jnp.where(mask, shift, 0.0), jnp.where(mask, kk, 0.0)
        total = total + apply_state(feature_pair(kk * shift), parts)
        grad = apply_rows(r.rows[...], parts)
        return total, one + grad * shift, two + unshifted(grad * kk, block)

    zero = jnp.zeros((T, L), F32)
    carry = over_blocks(at, later, keys, (zero, zero, zero), True)
    tail = split(tail_of(later[1]))
    total, one, two = keys(LAST, tail, carry, low)
    ks = split(r.kk[...])
    normed = jnp.where(low, 0.0, dot3([v[:, :E] for v in ks], tail, NN))
    dv = r.dv[...] + folded(total)
    dk = r.dk[...] + folded(one + two + 2.0 * normed)
    dq = r.dq[...]
    for i, g in enumerate((dq, dk, dv)):
        r.gh[i], r.gl[i] = split(jnp.where(low == (c == 0), g, 0.0))
    r.ph[...], r.pl[...] = split(jnp.concatenate([jnp.where(low, dq, dk), dv], axis=1))

    first, second = [], []
    for h in range(2):
        for b in (2 * h, 2 * h + 1):
            grad = dot3((r.xh[b], r.xl[b]), (r.ph[...], r.pl[...]), TN)
            for i in range(8):
                rows = grad[i * 32 : (i + 1) * 32]
                at_y, at_z = i % NY, (b % 2) * 2 + i // NY
                r.dw[h, at_y, at_z, :32] = rows[:, :L]
                r.dw[h, at_y, at_z, 32:] = jnp.where(low, rows[:16, L:], rows[16:, L:])
        first.append(
            [None]
            + [
                remote(r.dw.at[h, lax.rem(y + d, NY)], r.wry.at[h, d], r.ws1.at[h, d], r.wr1.at[h, d], at.py[d])
                for d in range(1, NY)
            ]
        )
        for d in (2, 1, 3):
            first[h][d].start()

    across = [None] * NX
    for d in (2, 1, 3, 0):
        b = lax.rem(x + d, NX)
        rows = pl.ds(pl.multiple_of(b * 256, 256), 256)
        part = jnp.zeros((T, 256), F32)
        for i in range(3):
            part = part + dot3((r.gh[i], r.gl[i]), (r.wh[i, rows], r.wl[i, rows]), NT)
        r.dx[d, 0] = part[:128]
        r.dx[d, 1] = part[128:]
        across[d] = remote(r.dx.at[d, 1 - c], r.rc.at[d], r.as_.at[d], r.ar.at[d], sibling)
        across[d].start()

    out_x = [None] * NX
    for d in (2, 1, 3, 0):
        across[d].wait_recv()
        total = r.dx[d, c] + r.rc[d]
        if d:
            r.sx[d] = total
            out_x[d] = remote(r.sx.at[d], r.gx.at[d], r.os.at[d], r.or_.at[d], at.px[d])
            out_x[d].start()
        else:
            r.gx[0] = total

    for h in range(2):
        for d in (1, 3, 2):
            first[h][d].wait_recv()
        r.wty[h] = r.dw[h, y] + r.wry[h, 1] + r.wry[h, 2] + r.wry[h, 3]
    for d in range(1, NZ):
        target = lax.rem(z + d, NZ)
        second.append(
            remote(
                r.wty.at[lax.div(target, 4), lax.rem(target, 4)], r.wrz.at[d], r.ws2.at[d], r.wr2.at[d], at.pz[d]
            )
        )
    for d in (4, 3, 5, 2, 6, 1, 7):
        second[d - 1].start()
    total = r.wty[lax.div(z, 4), lax.rem(z, 4)]
    for d in (1, 7, 2, 6, 3, 5, 4):
        second[d - 1].wait_recv()
        total = total + r.wrz[d]
    r.gw[0] = total
    swap = remote(r.gw.at[0], r.gw.at[1], r.cs.at[2], r.cr.at[2], sibling)
    swap.start()
    for d in range(1, NX):
        out_x[d].wait()
    for copy in [own, grads] + over_x[1:] + forwards[1:] + first[0][1:] + first[1][1:] + second + across:
        copy.wait_send()
    for chunk in earlier + later:
        chunk.close()
    swap.wait()


def fused(inputs, weights, out_grads):
    dma = pltpu.SemaphoreType.DMA

    def vm(*shape, dtype=F32):
        return pltpu.VMEM(shape, dtype)

    scratch = dict(
        w=vm(3, 1024, L),
        wh=vm(3, 1024, L, dtype=BF16),
        wl=vm(3, 1024, L, dtype=BF16),
        xg=vm(NX, T, 256),
        xh=vm(NX, T, 256, dtype=BF16),
        xl=vm(NX, T, 256, dtype=BF16),
        gg=vm(T, L),
        qq=vm(T, L),
        kk=vm(T, L),
        vv=vm(T, L),
        cols=vm(L, T, dtype=BF16),
        rows=vm(T, 3 * E, dtype=BF16),
        feats=vm(LAST + 1, T, 2 * L, dtype=BF16),
        dots=vm(T, T),
        wgh=vm(T, T, dtype=BF16),
        wgl=vm(T, T, dtype=BF16),
        numer=vm(T, L),
        denom=vm(T, L),
        gn=vm(T, L),
        gd=vm(T, L),
        one=vm(T, L),
        dq=vm(T, L),
        dk=vm(T, L),
        dv=vm(T, L),
        gh=vm(3, T, L, dtype=BF16),
        gl=vm(3, T, L, dtype=BF16),
        ph=vm(T, 2 * L, dtype=BF16),
        pl=vm(T, 2 * L, dtype=BF16),
        dw=vm(2, NY, 4, 48, L),
        wry=vm(2, NY, 4, 48, L),
        wty=vm(2, 4, 48, L),
        wrz=vm(NZ, 48, L),
        dx=vm(NX, 2, 128, 256),
        rc=vm(NX, 128, 256),
        sx=vm(NX, 128, 256),
    )
    sems = dict(
        wsem=dma,
        xs=dma((NX,)),
        xr=dma((NX,)),
        fs=dma((NX,)),
        fr=dma((NX,)),
        cs=dma((3,)),
        cr=dma((3,)),
        ws1=dma((2, NY)),
        wr1=dma((2, NY)),
        ws2=dma((NZ,)),
        wr2=dma((NZ,)),
        as_=dma((NX,)),
        ar=dma((NX,)),
        os=dma((NX,)),
        or_=dma((NX,)),
    )
    bufs = [
        [
            [
                vm(NY, rows, L),
                vm(NY, rows, L),
                vm(NY, rows, L),
                vm(rows, L),
                vm(NZ, piece, L),
                vm(NZ, piece, L),
                vm(rows, L),
                vm(NY, rows, L),
                vm(NY, rows, L),
            ]
            for rows, piece, _ in CHUNKS
        ]
        for _ in range(2)
    ]
    scan_sems = [dma((2, 2, n)) for n in (NY, NY, NZ, NZ, NZ, NZ, NY, NY)]
    flat = list(scratch.values()) + list(sems.values()) + [b for s in bufs for h in s for b in h] + scan_sems
    names = ["x_in", "w_in", "g_in", "gx", "gw"] + list(scratch) + list(sems)

    def kernel(*refs):
        named, rest = refs[: len(names)], refs[len(names) :]
        held = [[[rest[(s * 2 + h) * 9 + i] for h in range(2)] for s in range(2)] for i in range(9)]
        fused_kernel(names + ["bufs", "sems"], *named, held, rest[36:])

    return pl.pallas_call(
        kernel,
        out_shape=(jax.ShapeDtypeStruct((NX, 128, 256), F32), jax.ShapeDtypeStruct((2, 48, L), F32)),
        in_specs=[VMEM, pl.BlockSpec(memory_space=pl.ANY), VMEM],
        out_specs=(VMEM, VMEM),
        scratch_shapes=flat,
        compiler_params=pltpu.CompilerParams(collective_id=0, has_side_effects=True, vmem_limit_bytes=LIMIT),
        name="fused",
    )(inputs, weights, out_grads)


def finish_kernel(gx, gw, dx, dw):
    c = lax.rem(lax.axis_index("seq"), 2)
    dx[...] = gx[0] + gx[1] + gx[2] + gx[3]
    low = lower()
    mine = pl.ds(pl.multiple_of(c * 16, 16), 16)

    def halves(rows):
        a, b = gw[0, rows], gw[1, rows]
        return jnp.where(c == 0, a, b), jnp.where(c == 0, b, a)

    zero, one = halves(mine)
    dw[:, 0, :] = jnp.where(low, zero, roll(one, E))
    dw[:, 1, :] = jnp.where(low, roll(zero, E), one)
    zero, one = halves(pl.ds(32, 16))
    dw[:, 2, :] = jnp.where(c == 0, jnp.where(low, zero, roll(one, E)), jnp.where(low, roll(zero, E), one))


def per_device(inputs, proj_weights, out_grads):
    gx, gw = fused(inputs, proj_weights.transpose(1, 0, 2), out_grads)
    return pl.pallas_call(
        finish_kernel,
        out_shape=(jax.ShapeDtypeStruct((128, 256), F32), jax.ShapeDtypeStruct((16, 3, L), F32)),
        in_specs=[VMEM, VMEM],
        out_specs=(VMEM, VMEM),
        name="finish",
    )(gx, gw)


def solution(mesh):
    return jax.shard_map(
        per_device,
        mesh=mesh,
        in_specs=(P("seq", "head"), P(None, None, "head"), P("seq", "head")),
        out_specs=(P("seq", "head"), P("seq", None, "head")),
        check_vma=False,
    )
```

```python
import functools
import types

import jax
import jax.numpy as jnp
from jax import lax
from jax.experimental import pallas as pl
from jax.experimental.pallas import tpu as pltpu
from jax.sharding import PartitionSpec as P

MESH = pl.DeviceIdType.MESH
F32, BF16 = jnp.float32, jnp.bfloat16
E = 64
L = 128
T = 256
NX, NY, NZ = 4, 4, 8
LAST = 16
CHUNKS = ((64, 8, 8), (64, 8, 8), (80, 16, 5), (64, 8, 8))
WITH_LAST = 2
VMEM = pl.BlockSpec(memory_space=pltpu.VMEM)
LIMIT = 56 * 2**20


def place():
    seq = lax.axis_index("seq")
    return lax.axis_index("head"), lax.rem(lax.div(seq, 2), NY), lax.div(seq, 2 * NY), lax.rem(seq, 2)


def device(x, y, z, c):
    return (z * (2 * NY) + y * 2 + c, x)


def remote(src, dst, send, recv, peer):
    return pltpu.make_async_remote_copy(
        src_ref=src, dst_ref=dst, send_sem=send, recv_sem=recv, device_id=peer, device_id_type=MESH
    )


def split(value):
    high = value.astype(BF16)
    return high, (value - high.astype(F32)).astype(BF16)


NN = (((1,), (0,)), ((), ()))
NT = (((1,), (1,)), ((), ()))
TN = (((0,), (0,)), ((), ()))


def dot(a, b, dims):
    return lax.dot_general(a, b, dims, preferred_element_type=F32)


def dot3(a, b, dims):
    return dot(a[0], b[0], dims) + (dot(a[0], b[1], dims) + dot(a[1], b[0], dims))


def lower():
    return lax.broadcasted_iota(jnp.int32, (1, L), 1) < E


def roll(value, shift):
    return pltpu.roll(value, shift, 1)


def shifted(double, block):
    return jnp.where(lower(), roll(double, E - 2 * block), roll(double, E - 1 - 2 * block))


def query_scale(block):
    distance = 2 * block + jnp.where(lower(), 0, 1)
    once = jnp.where(distance > 32, 0.0, 1.0 / E)
    return jnp.where((distance > 0) & (distance < 32), 2.0 / E, once)


def unshifted(term, block):
    low = lower()
    return roll(jnp.where(low, term, 0.0), 2 * block) + roll(jnp.where(low, 0.0, term), 2 * block + 1)


def folded(value):
    return value + roll(value, E)


def columns_of(double):
    high, low = split(double.T)
    return jnp.concatenate([high[:E], low[:E]], axis=0)


def state_block(columns, feats):
    product = dot(columns, feats, NN)
    product = product[:, :L] + product[:, L:]
    return product[:E] + product[E:]


def feature_pair(features):
    return jnp.concatenate(split(features), axis=1)


def rows_of(double):
    high, low = split(double)
    return jnp.concatenate([high[:, :E], low[:, :E], high[:, :E]], axis=1)


def apply_state(pair, parts):
    rows = jnp.concatenate(parts, axis=0)
    return dot(pair, jnp.concatenate([rows, rows], axis=1), NT)


def apply_rows(rows, parts):
    high, low = parts
    return dot(rows, jnp.concatenate([high, high, low], axis=0), NN)


class Chunk:
    def __init__(self, at, chunk, reverse, bufs, sems):
        self.rows, self.piece, self.owners = CHUNKS[chunk]
        self.at, self.reverse = at, reverse
        self.st, self.ry, self.py, self.tot, self.rz, self.pz, self.ez, self.oy, self.out = bufs
        s1, r1, s2, r2, s3, r3, s4, r4 = [sem.at[int(reverse), chunk] for sem in sems]
        y, z = at.y, at.z
        self.first = [None] + [
            remote(self.st.at[lax.rem(y + d, NY)], self.ry.at[d], s1.at[d], r1.at[d], at.py[d]) for d in range(1, NY)
        ]
        self.second, self.third = [None], [None]
        for d in range(1, NZ):
            target = lax.rem(z + d, NZ)
            self.second.append(
                remote(self.tot.at[self.part(target)], self.rz.at[d], s2.at[d], r2.at[d], at.pz[d])
            )
            self.third.append(remote(self.pz.at[target], self.ez.at[self.part(z)], s3.at[d], r3.at[d], at.pz[d]))
        self.fourth = [None] + [
            remote(self.oy.at[d], self.out.at[y], s4.at[d], r4.at[d], at.py[d]) for d in range(1, NY)
        ]

    def part(self, index):
        return pl.ds(pl.multiple_of(lax.min(index, self.owners - 1) * self.piece, 8), self.piece)

    def owner(self, index, act):
        if self.owners == NZ:
            act()
        else:
            pl.when(index < self.owners)(act)

    def ordered(self, n):
        return range(n - 1, -1, -1) if self.reverse else range(n)

    def totals(self):
        y, z = self.at.y, self.at.z
        for d in (1, 3, 2):
            self.first[d].wait_recv()
        running = jnp.zeros((self.rows, L), F32)
        for index in self.ordered(NY):
            self.py[index] = running
            running = running + self.ry[lax.rem(y + NY - index, NY)]
        self.tot[...] = running
        for d in (4, 3, 5, 2, 6, 1, 7):
            self.owner(lax.rem(z + d, NZ), self.second[d].start)

    def prefixes(self):
        z = self.at.z

        def act():
            self.rz[0] = self.tot[self.part(z)]
            for copy in self.second[1:]:
                copy.wait_recv()
            running = jnp.zeros((self.piece, L), F32)
            for index in self.ordered(NZ):
                self.pz[index] = running
                running = running + self.rz[lax.rem(z + NZ - index, NZ)]
            for d in (4, 3, 5, 2, 6, 1, 7):
                self.third[d].start()
            self.ez[self.part(z)] = self.pz[z]

        self.owner(z, act)

    def spread(self):
        y, z = self.at.y, self.at.z
        for d in range(1, NZ):
            self.owner(lax.rem(z + NZ - d, NZ), self.third[d].wait_recv)
        for d in (2, 1, 3):
            self.oy[d] = self.ez[...] + self.py[lax.rem(y + d, NY)]
            self.fourth[d].start()
        self.out[y] = self.ez[...] + self.py[y]

    def close(self):
        for d in range(1, NY):
            self.first[d].wait_send()
            self.fourth[d].wait_send()
        for d in range(1, NZ):
            self.owner(lax.rem(self.at.z + d, NZ), self.second[d].wait_send)

        def act():
            for copy in self.third[1:]:
                copy.wait_send()

        self.owner(self.at.z, act)


def fill(at, chunks, make, tail):
    for h, chunk in enumerate(chunks):
        if h == WITH_LAST:
            rows = tail()
            for q in range(NY):
                chunk.st[q, E:] = rows[q * 16 : (q + 1) * 16]
            chunk.ry[0, E:] = chunk.st[at.y, E:]
        for d in (2, 1, 3, 0):
            q = lax.rem(at.y + d, NY)
            block = make(4 * h + q)
            if d == 0:
                chunk.ry[0, :E] = block
            else:
                chunk.st[q, :E] = block
                chunk.first[d].start()


def tail_of(chunks):
    return split(jnp.concatenate([chunks[WITH_LAST].out[q, E:] for q in range(NY)], axis=0))


def over_blocks(at, chunk, h, step, carry, wait):
    for d in (0, 1, 3, 2):
        if wait and d:
            chunk.fourth[d].wait_recv()
        q = lax.rem(at.y + NY - d, NY)
        carry = step(4 * h + q, split(chunk.out[q, :E]), carry)
    return carry


def fused_kernel(names, *refs):
    r = types.SimpleNamespace(**dict(zip(names, refs)))
    x, y, z, c = place()
    at = types.SimpleNamespace(x=x, y=y, z=z, c=c)
    sibling = device(x, y, z, 1 - c)
    at.px = [None] + [device(lax.rem(x + d, NX), y, z, c) for d in range(1, NX)]
    at.py = [None] + [device(x, lax.rem(y + d, NY), z, c) for d in range(1, NY)]
    at.pz = [None] + [device(x, y, lax.rem(z + d, NZ), c) for d in range(1, NZ)]
    low = lower()

    load = pltpu.make_async_copy(r.w_in, r.w, r.wsem)
    load.start()
    barrier = pltpu.get_barrier_semaphore()
    peers = [sibling] + at.px[1:] + at.py[1:] + at.pz[1:]
    for peer in peers:
        pl.semaphore_signal(barrier, inc=1, device_id=peer, device_id_type=MESH)
    mine = pl.ds(pl.multiple_of(c * 128, 128), 128)
    r.xg[x, mine] = r.x_in[...]
    r.gg[mine] = r.g_in[...]
    load.wait()

    def split_weights(b, carry):
        rows = pl.ds(pl.multiple_of(b * 256, 256), 256)
        for i in range(3):
            r.wh[i, rows], r.wl[i, rows] = split(r.w[i, rows])
        return carry

    lax.fori_loop(0, NX, split_weights, 0)
    pl.semaphore_wait(barrier, len(peers))

    over_x = [[None] * NX, [None] * NX]
    forwards = [[None] * NX, [None] * NX]
    halves = [pl.ds(pl.multiple_of(c * 128 + 64 * k, 64), 64) for k in range(2)]
    for k in range(2):
        for d in (2, 1, 3):
            over_x[k][d] = remote(
                r.x_in.at[pl.ds(64 * k, 64)], r.xg.at[x, halves[k]], r.xs.at[k, d], r.xr.at[k, d], at.px[d]
            )
            over_x[k][d].start()
    own = remote(r.x_in, r.xg.at[x, mine], r.cs.at[0], r.cr.at[0], sibling)
    own.start()
    grads = remote(r.g_in, r.gg.at[mine], r.cs.at[1], r.cr.at[1], sibling)
    grads.start()

    def project(b, sums):
        rows = pl.ds(pl.multiple_of(b * 256, 256), 256)
        r.xh[b], r.xl[b] = split(r.xg[b])
        feats = (r.xh[b], r.xl[b])
        return [sums[i] + dot3(feats, (r.wh[i, rows], r.wl[i, rows]), NN) for i in range(3)]

    own.wait_recv()
    sums = project(x, [jnp.zeros((T, L), F32) for _ in range(3)])
    for k in range(2):
        for d in (1, 3, 2):
            over_x[k][d].wait_recv()
            landed = r.xg.at[lax.rem(x + NX - d, NX), halves[k]]
            forwards[k][d] = remote(landed, landed, r.fs.at[k, d], r.fr.at[k, d], sibling)
            forwards[k][d].start()
    for d in (1, 3, 2):
        for k in range(2):
            forwards[k][d].wait_recv()
        sums = project(lax.rem(x + NX - d, NX), sums)

    def doubled(both):
        return jnp.where(low == (c == 0), both, roll(both, E))

    r.qq[...] = doubled(sums[0])
    r.kk[...] = doubled(sums[1])
    r.vv[...] = doubled(sums[2])

    scans = []
    for reverse in (False, True):
        bufs = [[buf[int(reverse)][h] for buf in r.bufs] for h in range(len(CHUNKS))]
        scans.append([Chunk(at, h, reverse, bufs[h], r.sems) for h in range(len(CHUNKS))])
    earlier, later = scans

    r.cols[...] = columns_of(r.vv[...])

    def key_block(block):
        kk = r.kk[...]
        return state_block(r.cols[...], feature_pair(kk * shifted(kk, block)))

    def key_tail():
        ks = split(r.kk[...])
        norm = dot3([k[:, :E] for k in ks], ks, TN)
        return jnp.where(low, key_block(LAST), norm)

    fill(at, earlier, key_block, key_tail)

    def query_feature(block, carry):
        qq = r.qq[...]
        r.feats[block] = feature_pair(qq * shifted(qq, block) * query_scale(block))
        return carry

    for h, chunk in enumerate(earlier):
        chunk.totals()
        lax.fori_loop(4 * h, 4 * h + 4, query_feature, 0)
    query_feature(LAST, 0)
    grads.wait_recv()
    causal = lax.broadcasted_iota(jnp.int32, (T, T), 0) >= lax.broadcasted_iota(jnp.int32, (T, T), 1)
    qs, ks, vs = [split(ref[...]) for ref in (r.qq, r.kk, r.vv)]
    r.dots[...] = dot3([v[:, :E] for v in qs], [v[:, :E] for v in ks], NT)
    weights = jnp.where(causal, r.dots[...] * r.dots[...] * (1.0 / E), 0.0)
    r.wgh[...], r.wgl[...] = split(weights)
    r.numer[...] = dot3((r.wgh[...], r.wgl[...]), vs, NN)
    r.denom[...] = jnp.broadcast_to(1.0 + jnp.sum(weights, axis=1, keepdims=True), (T, L))
    for chunk in earlier:
        chunk.prefixes()

    def transposed(b, carry):
        for to, value in ((r.xth, r.xh[b]), (r.xtl, r.xl[b])):
            r.turned[...] = value.T
            for i in range(8):
                rows = pl.ds(pl.multiple_of(i * 32 + c * 16, 16), 16)
                to[pl.ds(pl.multiple_of(b * 128 + i * 16, 16), 16)] = r.turned[rows]
        return carry

    lax.fori_loop(0, NX, transposed, 0)
    for chunk in earlier:
        chunk.spread()

    def forward(block, parts, total):
        return total + apply_state(r.feats[block], parts)

    total = jnp.zeros((T, L), F32)
    for h, chunk in enumerate(earlier):
        total = over_blocks(at, chunk, h, forward, total, True)
    tail = tail_of(earlier)
    total = total + apply_state(r.feats[LAST], tail)
    qs = split(r.qq[...])
    normed = jnp.where(low, 0.0, dot3([v[:, :E] for v in qs], tail, NN))
    denom = r.denom[...] + jnp.sum(normed * r.qq[...], axis=1, keepdims=True) * (1.0 / E)
    inverse = 1.0 / denom
    grad_numer = doubled(r.gg[...]) * inverse
    grad_denom = -0.5 * jnp.sum(grad_numer * (r.numer[...] + folded(total)), axis=1, keepdims=True) * inverse
    r.gn[...] = grad_numer
    r.gd[...] = grad_denom

    r.cols[...] = columns_of(grad_numer)

    def query_block(block):
        return state_block(r.cols[...], r.feats[block])

    def query_tail():
        qq = r.qq[...]
        norm = dot3(split((qq * r.gd[...])[:, :E]), split(qq), TN) * (1.0 / E)
        return jnp.where(low, query_block(LAST), norm)

    fill(at, later, query_block, query_tail)

    r.rows[...] = rows_of(r.gn[...])

    def backward(block, parts, carry):
        one, two = carry
        qq = r.qq[...]
        grad = apply_rows(r.rows[...], parts) * query_scale(block)
        return one + grad * shifted(qq, block), two + unshifted(grad * qq, block)

    r.one[...] = normed * r.gd[...] * (2.0 / E)
    r.two[...] = jnp.zeros((T, L), F32)
    for h, chunk in enumerate(later):
        chunk.totals()
        carry = (r.one[...], r.two[...])
        if h == 0:
            carry = backward(LAST, tail_of(earlier), carry)
        r.one[...], r.two[...] = over_blocks(at, earlier[h], h, backward, carry, False)
    qs, ks, vs, gs = [split(ref[...]) for ref in (r.qq, r.kk, r.vv, r.gn)]
    grad_scores = dot3([v[:, :E] for v in gs], [v[:, :E] for v in vs], NT) + r.gd[:, :1]
    r.gdh[...], r.gdl[...] = split(jnp.where(causal, grad_scores, 0.0) * r.dots[...] * (2.0 / E))
    r.dq[...] = folded(r.one[...] + r.two[...]) + dot3((r.gdh[...], r.gdl[...]), ks, NN)
    give_q = remote(r.dq, r.dqo, r.cs.at[2], r.cr.at[2], sibling)
    give_q.start()
    later[0].prefixes()
    later[1].prefixes()
    give_q.wait_recv()
    own_lanes = low == (c == 0)
    r.gh[0], r.gl[0] = split(jnp.where(own_lanes, r.dq[...], r.dqo[...]))
    for h in range(2):
        rows = pl.ds(h * 256, 256)
        grad = dot3((r.xth[rows], r.xtl[rows]), (r.gh[0], r.gl[0]), NN)
        for i in range(16):
            r.dwq[i % NY, 4 * h + i // NY] = grad[i * 16 : (i + 1) * 16]
    q_y = [None] + [
        remote(r.dwq.at[lax.rem(y + d, NY)], r.qry.at[d], r.qs1.at[d], r.qr1.at[d], at.py[d]) for d in range(1, NY)
    ]
    for d in (2, 1, 3):
        q_y[d].start()
    later[2].prefixes()
    later[3].prefixes()
    r.dk[...] = dot3((r.gdh[...], r.gdl[...]), qs, TN)
    r.dv[...] = dot3((r.wgh[...], r.wgl[...]), gs, TN)
    r.rows[...] = rows_of(r.vv[...])
    for chunk in later:
        chunk.spread()
    for d in (1, 3, 2):
        q_y[d].wait_recv()
    r.qty[...] = r.dwq[y] + r.qry[1] + r.qry[2] + r.qry[3]
    q_z = [None] + [
        remote(r.qty.at[lax.rem(z + d, NZ)], r.qrz.at[d], r.qs2.at[d], r.qr2.at[d], at.pz[d]) for d in range(1, NZ)
    ]
    for d in (4, 3, 5, 2, 6, 1, 7):
        q_z[d].start()

    def keys(block, parts, carry, mask=None):
        total, one, two = carry
        kk = r.kk[...]
        shift = shifted(kk, block)
        if mask is not None:
            shift, kk = jnp.where(mask, shift, 0.0), jnp.where(mask, kk, 0.0)
        total = total + apply_state(feature_pair(kk * shift), parts)
        grad = apply_rows(r.rows[...], parts)
        return total, one + grad * shift, two + unshifted(grad * kk, block)

    zero = jnp.zeros((T, L), F32)
    carry = (zero, zero, zero)
    for h, chunk in enumerate(later):
        carry = over_blocks(at, chunk, h, keys, carry, True)
    tail = tail_of(later)
    total, one, two = keys(LAST, tail, carry, low)
    ks = split(r.kk[...])
    normed = jnp.where(low, 0.0, dot3([v[:, :E] for v in ks], tail, NN))
    dv = r.dv[...] + folded(total)
    dk = r.dk[...] + folded(one + two + 2.0 * normed)
    r.kv[...] = jnp.where(low, dk, dv)
    give_kv = remote(r.kv, r.kvo, r.cs.at[3], r.cr.at[3], sibling)
    give_kv.start()
    give_kv.wait_recv()
    other = r.kvo[...]
    turned = roll(other, E)
    r.gh[1], r.gl[1] = split(jnp.where(own_lanes, dk, jnp.where(c == 0, turned, other)))
    r.gh[2], r.gl[2] = split(jnp.where(own_lanes, dv, jnp.where(c == 0, other, turned)))

    kv = [jnp.concatenate([g[1], g[2]], axis=1) for g in (r.gh, r.gl)]
    first = []
    for h in range(2):
        rows = pl.ds(h * 256, 256)
        grad = dot3((r.xth[rows], r.xtl[rows]), kv, NN)
        for i in range(16):
            r.dw[h, i % NY, i // NY] = grad[i * 16 : (i + 1) * 16]
        first.append(
            [None]
            + [
                remote(r.dw.at[h, lax.rem(y + d, NY)], r.wry.at[h, d], r.ws1.at[h, d], r.wr1.at[h, d], at.py[d])
                for d in range(1, NY)
            ]
        )
        for d in (2, 1, 3):
            first[h][d].start()

    out_x = [None] * NX
    for d in (2, 1, 3, 0):
        rows = pl.ds(pl.multiple_of(lax.rem(x + d, NX) * 256, 256), 256)
        part = jnp.zeros((128, 256), F32)
        for i in range(3):
            part = part + dot3((r.gh[i, mine], r.gl[i, mine]), (r.wh[i, rows], r.wl[i, rows]), NT)
        r.sx[d] = part
        if d:
            out_x[d] = remote(r.sx.at[d], r.rx.at[d], r.os.at[d], r.or_.at[d], at.px[d])
            out_x[d].start()

    for h in range(2):
        for d in (1, 3, 2):
            first[h][d].wait_recv()
        r.wty[h] = r.dw[h, y] + r.wry[h, 1] + r.wry[h, 2] + r.wry[h, 3]
        for j in (0, 3, 1, 2):
            target = 4 * h + j
            d = lax.rem(target - z + NZ, NZ)
            copy = remote(r.wty.at[h, j], r.wrz.at[d], r.ws2.at[d], r.wr2.at[d], device(x, y, target, c))
            pl.when(target != z)(copy.start)
    for d in (1, 3, 2):
        out_x[d].wait_recv()
    r.gx[...] = r.sx[0] + r.rx[1] + r.rx[2] + r.rx[3]
    total = r.qty[z]
    for d in range(1, NZ):
        q_z[d].wait_recv()
        total = total + r.qrz[d]
    r.gw[0] = total
    total = r.wty[lax.div(z, 4), lax.rem(z, 4)]
    second = [
        remote(
            r.wty.at[lax.div(lax.rem(z + d, NZ), 4), lax.rem(z + d, 4)], r.wrz.at[d], r.ws2.at[d], r.wr2.at[d], at.pz[d]
        )
        for d in range(1, NZ)
    ]
    for d in (1, 7, 2, 6, 3, 5, 4):
        second[d - 1].wait_recv()
        total = total + r.wrz[d]
    r.gw[1] = total[:, :L]
    r.gw[2] = total[:, L:]
    sent = [own, grads, give_q, give_kv] + second
    for group in over_x + forwards + first + [out_x, q_y, q_z]:
        sent += group[1:]
    for copy in sent:
        copy.wait_send()
    for chunk in earlier + later:
        chunk.close()


def fused(inputs, weights, out_grads):
    dma = pltpu.SemaphoreType.DMA

    def vm(*shape, dtype=F32):
        return pltpu.VMEM(shape, dtype)

    scratch = dict(
        w=vm(3, 1024, L),
        wh=vm(3, 1024, L, dtype=BF16),
        wl=vm(3, 1024, L, dtype=BF16),
        xg=vm(NX, T, 256),
        xh=vm(NX, T, 256, dtype=BF16),
        xl=vm(NX, T, 256, dtype=BF16),
        gg=vm(T, L),
        qq=vm(T, L),
        kk=vm(T, L),
        vv=vm(T, L),
        cols=vm(L, T, dtype=BF16),
        rows=vm(T, 3 * E, dtype=BF16),
        feats=vm(LAST + 1, T, 2 * L, dtype=BF16),
        dots=vm(T, T),
        wgh=vm(T, T, dtype=BF16),
        wgl=vm(T, T, dtype=BF16),
        numer=vm(T, L),
        denom=vm(T, L),
        gn=vm(T, L),
        gd=vm(T, L),
        one=vm(T, L),
        dq=vm(T, L),
        dk=vm(T, L),
        dv=vm(T, L),
        two=vm(T, L),
        gdh=vm(T, T, dtype=BF16),
        gdl=vm(T, T, dtype=BF16),
        dqo=vm(T, L),
        kv=vm(T, L),
        kvo=vm(T, L),
        gh=vm(3, T, L, dtype=BF16),
        gl=vm(3, T, L, dtype=BF16),
        turned=vm(256, T, dtype=BF16),
        xth=vm(512, T, dtype=BF16),
        xtl=vm(512, T, dtype=BF16),
        dwq=vm(NY, NZ, 16, L),
        qry=vm(NY, NZ, 16, L),
        qty=vm(NZ, 16, L),
        qrz=vm(NZ, 16, L),
        dw=vm(2, NY, 4, 16, 2 * L),
        wry=vm(2, NY, 4, 16, 2 * L),
        wty=vm(2, 4, 16, 2 * L),
        wrz=vm(NZ, 16, 2 * L),
        sx=vm(NX, 128, 256),
        rx=vm(NX, 128, 256),
    )
    sems = dict(
        wsem=dma,
        xs=dma((2, NX)),
        xr=dma((2, NX)),
        fs=dma((2, NX)),
        fr=dma((2, NX)),
        cs=dma((4,)),
        cr=dma((4,)),
        qs1=dma((NY,)),
        qr1=dma((NY,)),
        qs2=dma((NZ,)),
        qr2=dma((NZ,)),
        ws1=dma((2, NY)),
        wr1=dma((2, NY)),
        ws2=dma((NZ,)),
        wr2=dma((NZ,)),
        os=dma((NX,)),
        or_=dma((NX,)),
    )
    bufs = [
        [
            [
                vm(NY, rows, L),
                vm(NY, rows, L),
                vm(NY, rows, L),
                vm(rows, L),
                vm(NZ, piece, L),
                vm(NZ, piece, L),
                vm(rows, L),
                vm(NY, rows, L),
                vm(NY, rows, L),
            ]
            for rows, piece, _ in CHUNKS
        ]
        for _ in range(2)
    ]
    scan_sems = [dma((2, len(CHUNKS), n)) for n in (NY, NY, NZ, NZ, NZ, NZ, NY, NY)]
    flat = list(scratch.values()) + list(sems.values()) + [b for s in bufs for h in s for b in h] + scan_sems
    names = ["x_in", "w_in", "g_in", "gx", "gw"] + list(scratch) + list(sems)

    def kernel(*refs):
        named, rest = refs[: len(names)], refs[len(names) :]
        count = len(CHUNKS)
        held = [[[rest[(s * count + h) * 9 + i] for h in range(count)] for s in range(2)] for i in range(9)]
        fused_kernel(names + ["bufs", "sems"], *named, held, rest[18 * count :])

    return pl.pallas_call(
        kernel,
        out_shape=(jax.ShapeDtypeStruct((128, 256), F32), jax.ShapeDtypeStruct((3, 16, L), F32)),
        in_specs=[VMEM, pl.BlockSpec(memory_space=pl.ANY), VMEM],
        out_specs=(VMEM, VMEM),
        scratch_shapes=flat,
        compiler_params=pltpu.CompilerParams(collective_id=0, has_side_effects=True, vmem_limit_bytes=LIMIT),
        name="fused",
    )(inputs, weights, out_grads)


def finish_kernel(gx, gw, dx, dw):
    dx[...] = gx[...]
    dw[...] = gw[...]


def per_device(inputs, proj_weights, out_grads):
    gx, gw = fused(inputs, proj_weights.transpose(1, 0, 2), out_grads)
    dx, dw = pl.pallas_call(
        finish_kernel,
        out_shape=(jax.ShapeDtypeStruct((128, 256), F32), jax.ShapeDtypeStruct((3, 16, L), F32)),
        in_specs=[VMEM, VMEM],
        out_specs=(VMEM, VMEM),
        name="finish",
    )(gx, gw)
    return dx, dw.transpose(1, 0, 2)


def solution(mesh):
    return jax.shard_map(
        per_device,
        mesh=mesh,
        in_specs=(P("seq", "head"), P(None, None, "head"), P("seq", "head")),
        out_specs=(P("seq", "head"), P("seq", None, "head")),
        check_vma=False,
    )
```

```python
import functools
import types

import jax
import jax.numpy as jnp
from jax import lax
from jax.experimental import pallas as pl
from jax.experimental.pallas import tpu as pltpu
from jax.sharding import PartitionSpec as P

MESH = pl.DeviceIdType.MESH
F32, BF16 = jnp.float32, jnp.bfloat16
E = 64
L = 128
T = 256
NX, NY, NZ = 4, 4, 8
LAST = 16
CHUNKS = ((64, 8, 8), (64, 8, 8), (80, 16, 5), (64, 8, 8))
WITH_LAST = 2
VMEM = pl.BlockSpec(memory_space=pltpu.VMEM)
LIMIT = 56 * 2**20


def place():
    seq = lax.axis_index("seq")
    return lax.axis_index("head"), lax.rem(lax.div(seq, 2), NY), lax.div(seq, 2 * NY), lax.rem(seq, 2)


def device(x, y, z, c):
    return (z * (2 * NY) + y * 2 + c, x)


def remote(src, dst, send, recv, peer):
    return pltpu.make_async_remote_copy(
        src_ref=src, dst_ref=dst, send_sem=send, recv_sem=recv, device_id=peer, device_id_type=MESH
    )


def settle(ref, send, recv, peer):
    return remote(ref, ref, send, recv, peer)


def split(value):
    high = value.astype(BF16)
    return high, (value - high.astype(F32)).astype(BF16)


NN = (((1,), (0,)), ((), ()))
NT = (((1,), (1,)), ((), ()))
TN = (((0,), (0,)), ((), ()))


def dot(a, b, dims):
    return lax.dot_general(a, b, dims, preferred_element_type=F32)


def dot3(a, b, dims):
    return dot(a[0], b[0], dims) + (dot(a[0], b[1], dims) + dot(a[1], b[0], dims))


def lower():
    return lax.broadcasted_iota(jnp.int32, (1, L), 1) < E


def roll(value, shift):
    return pltpu.roll(value, shift, 1)


def shifted(double, block):
    return jnp.where(lower(), roll(double, E - 2 * block), roll(double, E - 1 - 2 * block))


def query_scale(block):
    distance = 2 * block + jnp.where(lower(), 0, 1)
    once = jnp.where(distance > 32, 0.0, 1.0 / E)
    return jnp.where((distance > 0) & (distance < 32), 2.0 / E, once)


def unshifted(term, block):
    low = lower()
    return roll(jnp.where(low, term, 0.0), 2 * block) + roll(jnp.where(low, 0.0, term), 2 * block + 1)


def folded(value):
    return value + roll(value, E)


def columns_of(double):
    high, low = split(double.T)
    return jnp.concatenate([high[:E], low[:E]], axis=0)


def state_block(columns, feats):
    product = dot(columns, feats, NN)
    product = product[:, :L] + product[:, L:]
    return product[:E] + product[E:]


def feature_pair(features):
    return jnp.concatenate(split(features), axis=1)


def rows_of(double):
    high, low = split(double)
    return jnp.concatenate([high[:, :E], low[:, :E], high[:, :E]], axis=1)


def apply_state(pair, parts):
    rows = jnp.concatenate(parts, axis=0)
    return dot(pair, jnp.concatenate([rows, rows], axis=1), NT)


def apply_rows(rows, parts):
    high, low = parts
    return dot(rows, jnp.concatenate([high, high, low], axis=0), NN)


class Chunk:
    def __init__(self, at, chunk, reverse, bufs, sems):
        self.rows, self.piece, self.owners = CHUNKS[chunk]
        self.at, self.reverse = at, reverse
        self.st, self.ry, self.py, self.tot, self.rz, self.pz, self.ez, self.oy, self.out = bufs
        send, recv = [[sem.at[int(reverse), chunk, stage] for stage in range(4)] for sem in sems]
        y, z = at.y, at.z
        self.first = [None] + [
            remote(self.st.at[lax.rem(y + d, NY)], self.ry.at[d], send[0], recv[0], at.py[d]) for d in range(1, NY)
        ]
        self.second, self.third = [None], [None]
        for d in range(1, NZ):
            target = lax.rem(z + d, NZ)
            self.second.append(remote(self.tot.at[self.part(target)], self.rz.at[d], send[1], recv[1], at.pz[d]))
            self.third.append(remote(self.pz.at[target], self.ez.at[self.part(z)], send[2], recv[2], at.pz[d]))
        self.fourth = [None] + [
            remote(self.oy.at[d], self.out.at[y], send[3], recv[3], at.py[d]) for d in range(1, NY)
        ]
        self.send, self.recv = send, recv

    def all_of(self, stage, pieces=NZ - 1):
        ref = self.ry.at[pl.ds(1, NY - 1)] if stage in (0, 3) else self.rz.at[pl.ds(0, pieces)]
        return settle(ref, self.send[stage], self.recv[stage], self.at.py[1])

    def part(self, index):
        return pl.ds(pl.multiple_of(lax.min(index, self.owners - 1) * self.piece, 8), self.piece)

    def owner(self, index, act, otherwise=None):
        if self.owners == NZ:
            act()
        else:
            pl.when(index < self.owners)(act)
            if otherwise is not None:
                pl.when(index >= self.owners)(otherwise)

    def ordered(self, n):
        return range(n - 1, -1, -1) if self.reverse else range(n)

    def totals(self):
        y, z = self.at.y, self.at.z
        self.all_of(0).wait_recv()
        running = jnp.zeros((self.rows, L), F32)
        for index in self.ordered(NY):
            self.py[index] = running
            running = running + self.ry[lax.rem(y + NY - index, NY)]
        self.tot[...] = running
        for d in (4, 3, 5, 2, 6, 1, 7):
            self.owner(lax.rem(z + d, NZ), self.second[d].start)

    def prefixes(self):
        z = self.at.z

        def act():
            self.rz[0] = self.tot[self.part(z)]
            self.all_of(1).wait_recv()
            running = jnp.zeros((self.piece, L), F32)
            for index in self.ordered(NZ):
                self.pz[index] = running
                running = running + self.rz[lax.rem(z + NZ - index, NZ)]
            for d in (4, 3, 5, 2, 6, 1, 7):
                self.third[d].start()
            self.ez[self.part(z)] = self.pz[z]

        self.owner(z, act)

    def spread(self):
        y, z = self.at.y, self.at.z
        self.owner(
            z,
            lambda: self.all_of(2, self.owners - 1).wait_recv(),
            lambda: self.all_of(2, self.owners).wait_recv(),
        )
        for d in (2, 1, 3):
            self.oy[d] = self.ez[...] + self.py[lax.rem(y + d, NY)]
            self.fourth[d].start()
        self.out[y] = self.ez[...] + self.py[y]

    def close(self):
        self.all_of(0).wait_send()
        self.owner(
            self.at.z,
            lambda: self.all_of(1, self.owners - 1).wait_send(),
            lambda: self.all_of(1, self.owners).wait_send(),
        )
        self.owner(self.at.z, lambda: self.all_of(2).wait_send())
        self.all_of(3).wait_send()


class Norms:
    def __init__(self, at, reverse, bufs, sems):
        self.at, self.reverse = at, reverse
        self.own, self.ry, self.tot, self.rz = bufs
        send, recv = [[sem.at[int(reverse), stage] for stage in range(2)] for sem in sems]
        self.first = [remote(self.own, self.ry.at[d], send[0], recv[0], at.py[d]) for d in (2, 1, 3)]
        self.second = [remote(self.tot, self.rz.at[d], send[1], recv[1], at.pz[d]) for d in (4, 3, 5, 2, 6, 1, 7)]
        self.all_first = settle(self.ry.at[pl.ds(1, NY - 1)], send[0], recv[0], at.py[1])
        self.all_second = settle(self.rz.at[pl.ds(1, NZ - 1)], send[1], recv[1], at.pz[1])

    def counts(self, d, index):
        return d > index if self.reverse else d <= index

    def start(self, matrix):
        self.own[...] = jnp.where(lower(), matrix[:32], matrix[32:])
        for copy in self.first:
            copy.start()

    def relay(self):
        self.all_first.wait_recv()
        self.tot[...] = self.own[...] + self.ry[1] + self.ry[2] + self.ry[3]
        for copy in self.second:
            copy.start()

    def result(self):
        self.all_second.wait_recv()
        total = jnp.zeros((32, L), F32)
        for d in range(1, NZ):
            total = total + jnp.where(self.counts(d, self.at.z), self.rz[d], 0.0)
        for d in range(1, NY):
            total = total + jnp.where(self.counts(d, self.at.y), self.ry[d], 0.0)
        turned = roll(total, E)
        low = lower()
        return split(jnp.concatenate([jnp.where(low, total, turned), jnp.where(low, turned, total)], axis=0))

    def close(self):
        self.all_first.wait_send()
        self.all_second.wait_send()


def fill(at, chunk, h, make):
    if h == WITH_LAST:
        rows = make(LAST)
        for q in range(NY):
            chunk.st[q, E:] = rows[q * 16 : (q + 1) * 16]
        chunk.ry[0, E:] = chunk.st[at.y, E:]
    for d in (2, 1, 3, 0):
        q = lax.rem(at.y + d, NY)
        block = make(4 * h + q)
        if d == 0:
            chunk.ry[0, :E] = block
        else:
            chunk.st[q, :E] = block
            chunk.first[d].start()


def tail_of(chunks):
    return split(jnp.concatenate([chunks[WITH_LAST].out[q, E:] for q in range(NY)], axis=0))


def over_blocks(at, chunk, h, step, carry, wait):
    for d in range(NY):
        if wait and d == 1:
            chunk.all_of(3).wait_recv()
        q = lax.rem(at.y + NY - d, NY)
        carry = step(4 * h + q, split(chunk.out[q, :E]), carry)
    return carry


def fused_kernel(names, *refs):
    r = types.SimpleNamespace(**dict(zip(names, refs)))
    x, y, z, c = place()
    at = types.SimpleNamespace(x=x, y=y, z=z, c=c)
    sibling = device(x, y, z, 1 - c)
    at.px = [None] + [device(lax.rem(x + d, NX), y, z, c) for d in range(1, NX)]
    at.py = [None] + [device(x, lax.rem(y + d, NY), z, c) for d in range(1, NY)]
    at.pz = [None] + [device(x, y, lax.rem(z + d, NZ), c) for d in range(1, NZ)]
    low = lower()

    load = pltpu.make_async_copy(r.w_in, r.w, r.wsem)
    load.start()
    barrier = pltpu.get_barrier_semaphore()
    peers = [sibling] + at.px[1:] + at.py[1:] + at.pz[1:]
    for peer in peers:
        pl.semaphore_signal(barrier, inc=1, device_id=peer, device_id_type=MESH)
    mine = pl.ds(pl.multiple_of(c * 128, 128), 128)
    r.xg[x, mine] = r.x_in[...]
    r.gg[mine] = r.g_in[...]
    load.wait()

    def split_weights(b, carry):
        rows = pl.ds(pl.multiple_of(b * 256, 256), 256)
        for i in range(3):
            r.wh[i, rows], r.wl[i, rows] = split(r.w[i, rows])
        return carry

    lax.fori_loop(0, NX, split_weights, 0)
    pl.semaphore_wait(barrier, len(peers))

    over_x = [[None] * NX, [None] * NX]
    forwards = [[None] * NX, [None] * NX]
    halves = [pl.ds(pl.multiple_of(c * 128 + 64 * k, 64), 64) for k in range(2)]
    for k in range(2):
        for d in (2, 1, 3):
            over_x[k][d] = remote(
                r.x_in.at[pl.ds(64 * k, 64)], r.xg.at[x, halves[k]], r.xs, r.xr.at[k, d], at.px[d]
            )
            over_x[k][d].start()
    own = remote(r.x_in, r.xg.at[x, mine], r.cs.at[0], r.cr.at[0], sibling)
    own.start()
    grads = remote(r.g_in, r.gg.at[mine], r.cs.at[1], r.cr.at[1], sibling)
    grads.start()

    def project(b, sums):
        rows = pl.ds(pl.multiple_of(b * 256, 256), 256)
        r.xh[b], r.xl[b] = split(r.xg[b])
        feats = (r.xh[b], r.xl[b])
        return [sums[i] + dot3(feats, (r.wh[i, rows], r.wl[i, rows]), NN) for i in range(3)]

    own.wait_recv()
    sums = project(x, [jnp.zeros((T, L), F32) for _ in range(3)])
    for k in range(2):
        for d in (1, 3, 2):
            over_x[k][d].wait_recv()
            landed = r.xg.at[lax.rem(x + NX - d, NX), halves[k]]
            forwards[k][d] = remote(landed, landed, r.fs, r.fr.at[k, d], sibling)
            forwards[k][d].start()
    for d in (1, 3, 2):
        for k in range(2):
            forwards[k][d].wait_recv()
        sums = project(lax.rem(x + NX - d, NX), sums)

    def doubled(both):
        return jnp.where(low == (c == 0), both, roll(both, E))

    r.qq[...] = doubled(sums[0])
    r.kk[...] = doubled(sums[1])
    r.vv[...] = doubled(sums[2])

    scans = []
    for reverse in (False, True):
        bufs = [[buf[int(reverse)][h] for buf in r.bufs] for h in range(len(CHUNKS))]
        scans.append([Chunk(at, h, reverse, bufs[h], r.sems) for h in range(len(CHUNKS))])
    earlier, later = scans

    norms, adjoint_norms = [Norms(at, v, r.small[int(v)], r.small_sems) for v in (False, True)]
    ks = split(r.kk[...])
    norms.start(dot3([v[:, :E] for v in ks], ks, TN))

    r.cols[...] = columns_of(r.vv[...])

    def key_block(block):
        kk = r.kk[...]
        return state_block(r.cols[...], feature_pair(kk * shifted(kk, block)))

    for h in range(4):
        if h == 3:
            norms.relay()
        fill(at, earlier[h], h, key_block)

    def query_feature(block, carry):
        qq = r.qq[...]
        r.feats[block] = feature_pair(qq * shifted(qq, block) * query_scale(block))
        return carry

    for h, chunk in enumerate(earlier):
        chunk.totals()
        lax.fori_loop(4 * h, 4 * h + 4, query_feature, 0)
    query_feature(LAST, 0)
    grads.wait_recv()
    causal = lax.broadcasted_iota(jnp.int32, (T, T), 0) >= lax.broadcasted_iota(jnp.int32, (T, T), 1)
    qs, ks, vs = [split(ref[...]) for ref in (r.qq, r.kk, r.vv)]
    r.dots[...] = dot3([v[:, :E] for v in qs], [v[:, :E] for v in ks], NT)
    weights = jnp.where(causal, r.dots[...] * r.dots[...] * (1.0 / E), 0.0)
    r.wgh[...], r.wgl[...] = split(weights)
    near = 1.0 + jnp.sum(weights, axis=1, keepdims=True)

    r.normed[...] = dot3([v[:, :E] for v in qs], norms.result(), NN)
    denom = near + jnp.sum(r.normed[...] * r.qq[...], axis=1, keepdims=True) * (0.5 / E)
    r.inverse[...] = jnp.broadcast_to(1.0 / denom, (T, L))
    r.gn[...] = doubled(r.gg[...]) * r.inverse[...]
    r.cols[...] = columns_of(r.gn[...])

    def query_block(block):
        return state_block(r.cols[...], r.feats[block])

    for h in range(4):
        earlier[h].prefixes()
        fill(at, later[h], h, query_block)

    def transposed(b, carry):
        for to, value in ((r.xth, r.xh[b]), (r.xtl, r.xl[b])):
            r.turned[...] = value.T
            for i in range(8):
                rows = pl.ds(pl.multiple_of(i * 32 + c * 16, 16), 16)
                to[pl.ds(pl.multiple_of(b * 128 + i * 16, 16), 16)] = r.turned[rows]
        return carry

    lax.fori_loop(0, NX, transposed, 0)
    for h in range(4):
        earlier[h].spread()
        later[h].totals()

    gs = split(r.gn[...])
    r.numer[...] = dot3((r.wgh[...], r.wgl[...]), vs, NN)
    r.dv[...] = dot3((r.wgh[...], r.wgl[...]), gs, TN)
    r.scores[...] = dot3([v[:, :E] for v in gs], [v[:, :E] for v in vs], NT)
    r.rows[...] = rows_of(r.gn[...])

    def forward(block, parts, total):
        return total + apply_state(r.feats[block], parts)

    total = jnp.zeros((T, L), F32)
    for h in range(4):
        total = over_blocks(at, earlier[h], h, forward, total, True)
        if h >= 2:
            later[h - 2].prefixes()
    total = total + apply_state(r.feats[LAST], tail_of(earlier))
    outputs = r.numer[...] + folded(total)
    r.gd[...] = jnp.sum(r.gn[...] * outputs, axis=1, keepdims=True) * r.inverse[...] * -0.5
    qq = r.qq[...]
    adjoint_norms.start(dot3(split((qq * r.gd[...])[:, :E]), split(qq), TN) * (1.0 / E))
    later[2].prefixes()
    later[3].prefixes()

    def backward(block, parts, carry):
        one, two = carry
        qq = r.qq[...]
        grad = apply_rows(r.rows[...], parts) * query_scale(block)
        return one + grad * shifted(qq, block), two + unshifted(grad * qq, block)

    r.one[...] = r.normed[...] * r.gd[...] * (1.0 / E)
    r.two[...] = jnp.zeros((T, L), F32)
    for h in range(4):
        carry = (r.one[...], r.two[...])
        if h == 0:
            carry = backward(LAST, tail_of(earlier), carry)
        r.one[...], r.two[...] = over_blocks(at, earlier[h], h, backward, carry, False)
        if h == 2:
            adjoint_norms.relay()
    qs, ks = [split(ref[...]) for ref in (r.qq, r.kk)]
    grad_scores = jnp.where(causal, r.scores[...] + r.gd[:, :1], 0.0)
    r.gdh[...], r.gdl[...] = split(grad_scores * r.dots[...] * (2.0 / E))
    r.dq[...] = folded(r.one[...] + r.two[...]) + dot3((r.gdh[...], r.gdl[...]), ks, NN)
    give_q = remote(r.dq, r.dqo, r.cs.at[2], r.cr.at[2], sibling)
    give_q.start()
    for chunk in later:
        chunk.spread()
    r.dk[...] = dot3((r.gdh[...], r.gdl[...]), qs, TN)
    r.rows[...] = rows_of(r.vv[...])
    give_q.wait_recv()
    own_lanes = low == (c == 0)
    r.gh[0], r.gl[0] = split(jnp.where(own_lanes, r.dq[...], r.dqo[...]))
    for h in range(2):
        rows = pl.ds(h * 256, 256)
        grad = dot3((r.xth[rows], r.xtl[rows]), (r.gh[0], r.gl[0]), NN)
        for i in range(16):
            r.dwq[i % NY, 4 * h + i // NY] = grad[i * 16 : (i + 1) * 16]
    q_y = [
        remote(r.dwq.at[lax.rem(y + d, NY)], r.qry.at[d], r.qs.at[0], r.qr.at[0], at.py[d]) for d in (2, 1, 3)
    ]
    for copy in q_y:
        copy.start()
    all_q_y = settle(r.qry.at[pl.ds(1, NY - 1)], r.qs.at[0], r.qr.at[0], at.py[1])
    all_q_z = settle(r.qrz.at[pl.ds(1, NZ - 1)], r.qs.at[1], r.qr.at[1], at.pz[1])

    def keys(block, parts, carry, mask=None):
        total, one, two = carry
        kk = r.kk[...]
        shift = shifted(kk, block)
        if mask is not None:
            shift, kk = jnp.where(mask, shift, 0.0), jnp.where(mask, kk, 0.0)
        total = total + apply_state(feature_pair(kk * shift), parts)
        grad = apply_rows(r.rows[...], parts)
        return total, one + grad * shift, two + unshifted(grad * kk, block)

    zero = jnp.zeros((T, L), F32)
    carry = (zero, zero, zero)
    for h in range(4):
        carry = over_blocks(at, later[h], h, keys, carry, True)
        if h == 2:
            all_q_y.wait_recv()
            r.qty[...] = r.dwq[y] + r.qry[1] + r.qry[2] + r.qry[3]
            for d in (4, 3, 5, 2, 6, 1, 7):
                remote(r.qty.at[lax.rem(z + d, NZ)], r.qrz.at[d], r.qs.at[1], r.qr.at[1], at.pz[d]).start()
    total, one, two = keys(LAST, tail_of(later), carry, low)
    ks = split(r.kk[...])
    normed = dot3([v[:, :E] for v in ks], adjoint_norms.result(), NN)
    dv = r.dv[...] + folded(total)
    dk = r.dk[...] + folded(one + two) + 2.0 * normed
    r.kv[...] = jnp.where(low, dk, dv)
    give_kv = remote(r.kv, r.kvo, r.cs.at[3], r.cr.at[3], sibling)
    give_kv.start()
    give_kv.wait_recv()
    other = r.kvo[...]
    turned = roll(other, E)
    r.gh[1], r.gl[1] = split(jnp.where(own_lanes, dk, jnp.where(c == 0, turned, other)))
    r.gh[2], r.gl[2] = split(jnp.where(own_lanes, dv, jnp.where(c == 0, other, turned)))

    kv = [jnp.concatenate([g[1], g[2]], axis=1) for g in (r.gh, r.gl)]
    first = []
    for h in range(2):
        rows = pl.ds(h * 256, 256)
        grad = dot3((r.xth[rows], r.xtl[rows]), kv, NN)
        for i in range(16):
            r.dw[h, i % NY, i // NY] = grad[i * 16 : (i + 1) * 16]
        for d in (2, 1, 3):
            remote(
                r.dw.at[h, lax.rem(y + d, NY)], r.wry.at[h, d], r.ws.at[h], r.wr.at[h], at.py[d]
            ).start()
        first.append(settle(r.wry.at[h, pl.ds(1, NY - 1)], r.ws.at[h], r.wr.at[h], at.py[1]))

    for d in (2, 1, 3, 0):
        rows = pl.ds(pl.multiple_of(lax.rem(x + d, NX) * 256, 256), 256)
        part = jnp.zeros((128, 256), F32)
        for i in range(3):
            part = part + dot3((r.gh[i, mine], r.gl[i, mine]), (r.wh[i, rows], r.wl[i, rows]), NT)
        r.sx[d] = part
        if d:
            remote(r.sx.at[d], r.rx.at[d], r.os.at[0], r.os.at[1], at.px[d]).start()
    all_x = settle(r.rx.at[pl.ds(1, NX - 1)], r.os.at[0], r.os.at[1], at.px[1])

    for h in range(2):
        first[h].wait_recv()
        r.wty[h] = r.dw[h, y] + r.wry[h, 1] + r.wry[h, 2] + r.wry[h, 3]
        for j in (0, 3, 1, 2):
            target = 4 * h + j
            d = lax.rem(target - z + NZ, NZ)
            copy = remote(r.wty.at[h, j], r.wrz.at[d], r.ws.at[2], r.wr.at[2], device(x, y, target, c))
            pl.when(target != z)(copy.start)
    all_x.wait_recv()
    r.gx[...] = r.sx[0] + r.rx[1] + r.rx[2] + r.rx[3]
    all_q_z.wait_recv()
    total = r.qty[z]
    for d in range(1, NZ):
        total = total + r.qrz[d]
    r.gw[0] = total
    for copy in [own, grads, give_q, give_kv, all_q_y, all_q_z, all_x] + first:
        copy.wait_send()
    settle(r.xg.at[pl.ds(0, 3), pl.ds(0, 128)], r.xs, r.xr.at[0, 0], at.px[1]).wait_send()
    settle(r.xg.at[pl.ds(0, 3), pl.ds(0, 128)], r.fs, r.fr.at[0, 0], sibling).wait_send()
    for group in earlier + later + [norms, adjoint_norms]:
        group.close()
    all_z = settle(r.wrz.at[pl.ds(1, NZ - 1)], r.ws.at[2], r.wr.at[2], at.pz[1])
    all_z.wait_recv()
    total = r.wty[lax.div(z, 4), lax.rem(z, 4)]
    for d in range(1, NZ):
        total = total + r.wrz[d]
    r.gw[1] = total[:, :L]
    r.gw[2] = total[:, L:]
    all_z.wait_send()


def fused(inputs, weights, out_grads):
    dma = pltpu.SemaphoreType.DMA

    def vm(*shape, dtype=F32):
        return pltpu.VMEM(shape, dtype)

    scratch = dict(
        w=vm(3, 1024, L),
        wh=vm(3, 1024, L, dtype=BF16),
        wl=vm(3, 1024, L, dtype=BF16),
        xg=vm(NX, T, 256),
        xh=vm(NX, T, 256, dtype=BF16),
        xl=vm(NX, T, 256, dtype=BF16),
        gg=vm(T, L),
        qq=vm(T, L),
        kk=vm(T, L),
        vv=vm(T, L),
        cols=vm(L, T, dtype=BF16),
        rows=vm(T, 3 * E, dtype=BF16),
        feats=vm(LAST + 1, T, 2 * L, dtype=BF16),
        dots=vm(T, T),
        wgh=vm(T, T, dtype=BF16),
        wgl=vm(T, T, dtype=BF16),
        numer=vm(T, L),
        inverse=vm(T, L),
        normed=vm(T, L),
        scores=vm(T, T),
        gn=vm(T, L),
        gd=vm(T, L),
        one=vm(T, L),
        dq=vm(T, L),
        dk=vm(T, L),
        dv=vm(T, L),
        two=vm(T, L),
        gdh=vm(T, T, dtype=BF16),
        gdl=vm(T, T, dtype=BF16),
        dqo=vm(T, L),
        kv=vm(T, L),
        kvo=vm(T, L),
        gh=vm(3, T, L, dtype=BF16),
        gl=vm(3, T, L, dtype=BF16),
        turned=vm(256, T, dtype=BF16),
        xth=vm(512, T, dtype=BF16),
        xtl=vm(512, T, dtype=BF16),
        dwq=vm(NY, NZ, 16, L),
        qry=vm(NY, NZ, 16, L),
        qty=vm(NZ, 16, L),
        qrz=vm(NZ, 16, L),
        dw=vm(2, NY, 4, 16, 2 * L),
        wry=vm(2, NY, 4, 16, 2 * L),
        wty=vm(2, 4, 16, 2 * L),
        wrz=vm(NZ, 16, 2 * L),
        sx=vm(NX, 128, 256),
        rx=vm(NX, 128, 256),
    )
    sems = dict(
        wsem=dma,
        xs=dma,
        xr=dma((2, NX)),
        fs=dma,
        fr=dma((2, NX)),
        cs=dma((4,)),
        cr=dma((4,)),
        qs=dma((2,)),
        qr=dma((2,)),
        ws=dma((3,)),
        wr=dma((3,)),
        os=dma((2,)),
    )
    bufs = [
        [
            [
                vm(NY, rows, L),
                vm(NY, rows, L),
                vm(NY, rows, L),
                vm(rows, L),
                vm(NZ, piece, L),
                vm(NZ, piece, L),
                vm(rows, L),
                vm(NY, rows, L),
                vm(NY, rows, L),
            ]
            for rows, piece, _ in CHUNKS
        ]
        for _ in range(2)
    ]
    small = [vm(*shape, 32, L) for _ in range(2) for shape in ((), (NY,), (), (NZ,))]
    scan_sems = [dma((2, len(CHUNKS), 4)), dma((2, len(CHUNKS), 4)), dma((2, 2)), dma((2, 2))]
    flat = list(scratch.values()) + list(sems.values()) + [b for s in bufs for h in s for b in h] + small + scan_sems
    names = ["x_in", "w_in", "g_in", "gx", "gw"] + list(scratch) + list(sems)

    def kernel(*refs):
        named, rest = refs[: len(names)], refs[len(names) :]
        count = len(CHUNKS)
        held = [[[rest[(s * count + h) * 9 + i] for h in range(count)] for s in range(2)] for i in range(9)]
        rest = rest[18 * count :]
        fused_kernel(
            names + ["bufs", "small", "sems", "small_sems"], *named, held, (rest[:4], rest[4:8]), rest[8:10], rest[10:]
        )

    return pl.pallas_call(
        kernel,
        out_shape=(jax.ShapeDtypeStruct((128, 256), F32), jax.ShapeDtypeStruct((3, 16, L), F32)),
        in_specs=[VMEM, pl.BlockSpec(memory_space=pl.ANY), VMEM],
        out_specs=(VMEM, VMEM),
        scratch_shapes=flat,
        compiler_params=pltpu.CompilerParams(collective_id=0, has_side_effects=True, vmem_limit_bytes=LIMIT),
        name="fused",
    )(inputs, weights, out_grads)


def finish_kernel(gx, gw, dx, dw):
    dx[...] = gx[...]
    dw[...] = gw[...]


def per_device(inputs, proj_weights, out_grads):
    gx, gw = fused(inputs, proj_weights.transpose(1, 0, 2), out_grads)
    dx, dw = pl.pallas_call(
        finish_kernel,
        out_shape=(jax.ShapeDtypeStruct((128, 256), F32), jax.ShapeDtypeStruct((3, 16, L), F32)),
        in_specs=[VMEM, VMEM],
        out_specs=(VMEM, VMEM),
        name="finish",
    )(gx, gw)
    return dx, dw.transpose(1, 0, 2)


def solution(mesh):
    return jax.shard_map(
        per_device,
        mesh=mesh,
        in_specs=(P("seq", "head"), P(None, None, "head"), P("seq", "head")),
        out_specs=(P("seq", "head"), P("seq", None, "head")),
        check_vma=False,
    )
```

```python
import functools
import types

import jax
import jax.numpy as jnp
from jax import lax
from jax.experimental import pallas as pl
from jax.experimental.pallas import tpu as pltpu
from jax.sharding import PartitionSpec as P

MESH = pl.DeviceIdType.MESH
F32, BF16 = jnp.float32, jnp.bfloat16
E = 64
L = 128
T = 256
NX, NY, NZ = 4, 4, 8
LAST = 16
CHUNKS = ((64, 8, 8), (64, 8, 8), (80, 16, 5), (64, 8, 8))
WITH_LAST = 2
VMEM = pl.BlockSpec(memory_space=pltpu.VMEM)
LIMIT = 56 * 2**20


def place():
    seq = lax.axis_index("seq")
    return lax.axis_index("head"), lax.rem(lax.div(seq, 2), NY), lax.div(seq, 2 * NY), lax.rem(seq, 2)


def device(x, y, z, c):
    return (z * (2 * NY) + y * 2 + c, x)


def remote(src, dst, send, recv, peer):
    return pltpu.make_async_remote_copy(
        src_ref=src, dst_ref=dst, send_sem=send, recv_sem=recv, device_id=peer, device_id_type=MESH
    )


def settle(ref, send, recv, peer):
    return remote(ref, ref, send, recv, peer)


def split(value):
    high = value.astype(BF16)
    return high, (value - high.astype(F32)).astype(BF16)


NN = (((1,), (0,)), ((), ()))
NT = (((1,), (1,)), ((), ()))
TN = (((0,), (0,)), ((), ()))


def dot(a, b, dims):
    return lax.dot_general(a, b, dims, preferred_element_type=F32)


def dot3(a, b, dims):
    return dot(a[0], b[0], dims) + (dot(a[0], b[1], dims) + dot(a[1], b[0], dims))


def lower():
    return lax.broadcasted_iota(jnp.int32, (1, L), 1) < E


def roll(value, shift):
    return pltpu.roll(value, shift, 1)


def shifted(double, block):
    return jnp.where(lower(), roll(double, E - 2 * block), roll(double, E - 1 - 2 * block))


def query_scale(block):
    distance = 2 * block + jnp.where(lower(), 0, 1)
    once = jnp.where(distance > 32, 0.0, 1.0 / E)
    return jnp.where((distance > 0) & (distance < 32), 2.0 / E, once)


def unshifted(term, block):
    low = lower()
    return roll(jnp.where(low, term, 0.0), 2 * block) + roll(jnp.where(low, 0.0, term), 2 * block + 1)


def folded(value):
    return value + roll(value, E)


def columns_of(double):
    high, low = split(double.T)
    return jnp.concatenate([high[:E], low[:E]], axis=0)


def state_block(columns, feats):
    product = dot(columns, feats, NN)
    product = product[:, :L] + product[:, L:]
    return product[:E] + product[E:]


def feature_pair(features):
    return jnp.concatenate(split(features), axis=1)


def rows_of(double):
    high, low = split(double)
    return jnp.concatenate([high[:, :E], low[:, :E], high[:, :E]], axis=1)


def apply_state(pair, parts):
    rows = jnp.concatenate(parts, axis=0)
    return dot(pair, jnp.concatenate([rows, rows], axis=1), NT)


def apply_rows(rows, parts):
    high, low = parts
    return dot(rows, jnp.concatenate([high, high, low], axis=0), NN)


class Chunk:
    def __init__(self, at, chunk, reverse, bufs, sems):
        self.rows, self.piece, self.owners = CHUNKS[chunk]
        self.at, self.reverse = at, reverse
        self.st, self.ry, self.py, self.tot, self.rz, self.pz, self.ez, self.oy, self.out = bufs
        send, recv = [[sem.at[int(reverse), chunk, stage] for stage in range(4)] for sem in sems]
        y, z = at.y, at.z
        self.first = [None] + [
            remote(self.st.at[lax.rem(y + d, NY)], self.ry.at[d], send[0], recv[0], at.py[d]) for d in range(1, NY)
        ]
        self.second, self.third = [None], [None]
        for d in range(1, NZ):
            target = lax.rem(z + d, NZ)
            self.second.append(remote(self.tot.at[self.part(target)], self.rz.at[d], send[1], recv[1], at.pz[d]))
            self.third.append(remote(self.pz.at[target], self.ez.at[self.part(z)], send[2], recv[2], at.pz[d]))
        self.fourth = [None] + [
            remote(self.oy.at[d], self.out.at[y], send[3], recv[3], at.py[d]) for d in range(1, NY)
        ]
        self.send, self.recv = send, recv

    def all_of(self, stage, pieces=NZ - 1):
        ref = self.ry.at[pl.ds(1, NY - 1)] if stage in (0, 3) else self.rz.at[pl.ds(0, pieces)]
        return settle(ref, self.send[stage], self.recv[stage], self.at.py[1])

    def part(self, index):
        return pl.ds(pl.multiple_of(lax.min(index, self.owners - 1) * self.piece, 8), self.piece)

    def owner(self, index, act, otherwise=None):
        if self.owners == NZ:
            act()
        else:
            pl.when(index < self.owners)(act)
            if otherwise is not None:
                pl.when(index >= self.owners)(otherwise)

    def ordered(self, n):
        return range(n - 1, -1, -1) if self.reverse else range(n)

    def totals(self):
        y, z = self.at.y, self.at.z
        self.all_of(0).wait_recv()
        running = jnp.zeros((self.rows, L), F32)
        for index in self.ordered(NY):
            self.py[index] = running
            running = running + self.ry[lax.rem(y + NY - index, NY)]
        self.tot[...] = running
        for d in (4, 3, 5, 2, 6, 1, 7):
            self.owner(lax.rem(z + d, NZ), self.second[d].start)

    def prefixes(self):
        z = self.at.z

        def act():
            self.rz[0] = self.tot[self.part(z)]
            self.all_of(1).wait_recv()
            running = jnp.zeros((self.piece, L), F32)
            for index in self.ordered(NZ):
                self.pz[index] = running
                running = running + self.rz[lax.rem(z + NZ - index, NZ)]
            for d in (4, 3, 5, 2, 6, 1, 7):
                self.third[d].start()
            self.ez[self.part(z)] = self.pz[z]

        self.owner(z, act)

    def spread(self):
        y, z = self.at.y, self.at.z
        self.owner(
            z,
            lambda: self.all_of(2, self.owners - 1).wait_recv(),
            lambda: self.all_of(2, self.owners).wait_recv(),
        )
        for d in (2, 1, 3):
            self.oy[d] = self.ez[...] + self.py[lax.rem(y + d, NY)]
            self.fourth[d].start()
        self.out[y] = self.ez[...] + self.py[y]

    def close(self):
        self.all_of(0).wait_send()
        self.owner(
            self.at.z,
            lambda: self.all_of(1, self.owners - 1).wait_send(),
            lambda: self.all_of(1, self.owners).wait_send(),
        )
        self.owner(self.at.z, lambda: self.all_of(2).wait_send())
        self.all_of(3).wait_send()


class Norms:
    def __init__(self, at, reverse, bufs, sems):
        self.at, self.reverse = at, reverse
        self.own, self.ry, self.tot, self.rz = bufs
        send, recv = [[sem.at[int(reverse), stage] for stage in range(2)] for sem in sems]
        self.first = [remote(self.own, self.ry.at[d], send[0], recv[0], at.py[d]) for d in (2, 1, 3)]
        self.second = [remote(self.tot, self.rz.at[d], send[1], recv[1], at.pz[d]) for d in (4, 3, 5, 2, 6, 1, 7)]
        self.all_first = settle(self.ry.at[pl.ds(1, NY - 1)], send[0], recv[0], at.py[1])
        self.all_second = settle(self.rz.at[pl.ds(1, NZ - 1)], send[1], recv[1], at.pz[1])

    def counts(self, d, index):
        return d > index if self.reverse else d <= index

    def start(self, matrix):
        self.own[...] = jnp.where(lower(), matrix[:32], matrix[32:])
        for copy in self.first:
            copy.start()

    def relay(self):
        self.all_first.wait_recv()
        self.tot[...] = self.own[...] + self.ry[1] + self.ry[2] + self.ry[3]
        for copy in self.second:
            copy.start()

    def result(self):
        self.all_second.wait_recv()
        total = jnp.zeros((32, L), F32)
        for d in range(1, NZ):
            total = total + jnp.where(self.counts(d, self.at.z), self.rz[d], 0.0)
        for d in range(1, NY):
            total = total + jnp.where(self.counts(d, self.at.y), self.ry[d], 0.0)
        turned = roll(total, E)
        low = lower()
        return split(jnp.concatenate([jnp.where(low, total, turned), jnp.where(low, turned, total)], axis=0))

    def close(self):
        self.all_first.wait_send()
        self.all_second.wait_send()


def fill(at, chunk, h, make):
    if h == WITH_LAST:
        rows = make(LAST)
        for q in range(NY):
            chunk.st[q, E:] = rows[q * 16 : (q + 1) * 16]
        chunk.ry[0, E:] = chunk.st[at.y, E:]
    for d in (2, 1, 3, 0):
        q = lax.rem(at.y + d, NY)
        block = make(4 * h + q)
        if d == 0:
            chunk.ry[0, :E] = block
        else:
            chunk.st[q, :E] = block
            chunk.first[d].start()


def tail_of(chunks):
    return split(jnp.concatenate([chunks[WITH_LAST].out[q, E:] for q in range(NY)], axis=0))


def over_blocks(at, chunk, h, step, carry, wait):
    for d in range(NY):
        if wait and d == 1:
            chunk.all_of(3).wait_recv()
        q = lax.rem(at.y + NY - d, NY)
        carry = step(4 * h + q, split(chunk.out[q, :E]), carry)
    return carry


def fused_kernel(names, *refs):
    r = types.SimpleNamespace(**dict(zip(names, refs)))
    x, y, z, c = place()
    at = types.SimpleNamespace(x=x, y=y, z=z, c=c)
    sibling = device(x, y, z, 1 - c)
    at.px = [None] + [device(lax.rem(x + d, NX), y, z, c) for d in range(1, NX)]
    at.py = [None] + [device(x, lax.rem(y + d, NY), z, c) for d in range(1, NY)]
    at.pz = [None] + [device(x, y, lax.rem(z + d, NZ), c) for d in range(1, NZ)]
    low = lower()

    load = pltpu.make_async_copy(r.w_in, r.w, r.wsem)
    load.start()
    barrier = pltpu.get_barrier_semaphore()
    peers = [sibling] + at.px[1:] + at.py[1:] + at.pz[1:]
    for peer in peers:
        pl.semaphore_signal(barrier, inc=1, device_id=peer, device_id_type=MESH)
    mine = pl.ds(pl.multiple_of(c * 128, 128), 128)
    r.xg[x, mine] = r.x_in[...]
    r.gg[mine] = r.g_in[...]
    load.wait()

    def split_weights(b, carry):
        rows = pl.ds(pl.multiple_of(b * 256, 256), 256)
        for i in range(3):
            r.wh[i, rows], r.wl[i, rows] = split(r.w[i, rows])
        return carry

    lax.fori_loop(0, NX, split_weights, 0)
    pl.semaphore_wait(barrier, len(peers))

    over_x = [[None] * NX, [None] * NX]
    forwards = [[None] * NX, [None] * NX]
    halves = [pl.ds(pl.multiple_of(c * 128 + 64 * k, 64), 64) for k in range(2)]
    for k in range(2):
        for d in (2, 1, 3):
            over_x[k][d] = remote(
                r.x_in.at[pl.ds(64 * k, 64)], r.xg.at[x, halves[k]], r.xs, r.xr.at[k, d], at.px[d]
            )
            over_x[k][d].start()
    own = remote(r.x_in, r.xg.at[x, mine], r.cs.at[0], r.cr.at[0], sibling)
    own.start()
    grads = remote(r.g_in, r.gg.at[mine], r.cs.at[1], r.cr.at[1], sibling)
    grads.start()

    def project(b, sums):
        rows = pl.ds(pl.multiple_of(b * 256, 256), 256)
        r.xh[b], r.xl[b] = split(r.xg[b])
        feats = (r.xh[b], r.xl[b])
        return [sums[i] + dot3(feats, (r.wh[i, rows], r.wl[i, rows]), NN) for i in range(3)]

    own.wait_recv()
    sums = project(x, [jnp.zeros((T, L), F32) for _ in range(3)])
    for k in range(2):
        for d in (1, 3, 2):
            over_x[k][d].wait_recv()
            landed = r.xg.at[lax.rem(x + NX - d, NX), halves[k]]
            forwards[k][d] = remote(landed, landed, r.fs, r.fr.at[k, d], sibling)
            forwards[k][d].start()
    for d in (1, 3, 2):
        for k in range(2):
            forwards[k][d].wait_recv()
        sums = project(lax.rem(x + NX - d, NX), sums)

    def doubled(both):
        return jnp.where(low == (c == 0), both, roll(both, E))

    r.qq[...] = doubled(sums[0])
    r.kk[...] = doubled(sums[1])
    r.vv[...] = doubled(sums[2])

    scans = []
    for reverse in (False, True):
        bufs = [[buf[int(reverse)][h] for buf in r.bufs] for h in range(len(CHUNKS))]
        scans.append([Chunk(at, h, reverse, bufs[h], r.sems) for h in range(len(CHUNKS))])
    earlier, later = scans

    norms, adjoint_norms = [Norms(at, v, r.small[int(v)], r.small_sems) for v in (False, True)]
    ks = split(r.kk[...])
    norms.start(dot3([v[:, :E] for v in ks], ks, TN))

    r.cols[...] = columns_of(r.vv[...])

    def key_block(block):
        kk = r.kk[...]
        return state_block(r.cols[...], feature_pair(kk * shifted(kk, block)))

    for h in range(4):
        if h == 2:
            norms.relay()
        fill(at, earlier[h], h, key_block)

    def query_feature(block, carry):
        qq = r.qq[...]
        r.feats[block] = feature_pair(qq * shifted(qq, block) * query_scale(block))
        return carry

    for h, chunk in enumerate(earlier):
        chunk.totals()
        lax.fori_loop(4 * h, 4 * h + 4, query_feature, 0)
    query_feature(LAST, 0)
    grads.wait_recv()
    causal = lax.broadcasted_iota(jnp.int32, (T, T), 0) >= lax.broadcasted_iota(jnp.int32, (T, T), 1)
    qs, ks, vs = [split(ref[...]) for ref in (r.qq, r.kk, r.vv)]
    r.dots[...] = dot3([v[:, :E] for v in qs], [v[:, :E] for v in ks], NT)
    weights = jnp.where(causal, r.dots[...] * r.dots[...] * (1.0 / E), 0.0)
    r.wgh[...], r.wgl[...] = split(weights)
    near = 1.0 + jnp.sum(weights, axis=1, keepdims=True)

    r.normed[...] = dot3([v[:, :E] for v in qs], norms.result(), NN)
    denom = near + jnp.sum(r.normed[...] * r.qq[...], axis=1, keepdims=True) * (0.5 / E)
    r.inverse[...] = jnp.broadcast_to(1.0 / denom, (T, L))
    r.gn[...] = doubled(r.gg[...]) * r.inverse[...]
    r.cols[...] = columns_of(r.gn[...])

    def query_block(block):
        return state_block(r.cols[...], r.feats[block])

    for h in range(4):
        fill(at, later[h], h, query_block)
    for chunk in earlier:
        chunk.prefixes()

    def transposed(b, carry):
        for to, value in ((r.xth, r.xh[b]), (r.xtl, r.xl[b])):
            r.turned[...] = value.T
            for i in range(8):
                rows = pl.ds(pl.multiple_of(i * 32 + c * 16, 16), 16)
                to[pl.ds(pl.multiple_of(b * 128 + i * 16, 16), 16)] = r.turned[rows]
        return carry

    lax.fori_loop(0, NX, transposed, 0)
    for h in range(4):
        earlier[h].spread()
        later[h].totals()

    gs = split(r.gn[...])
    r.numer[...] = dot3((r.wgh[...], r.wgl[...]), vs, NN)
    r.dv[...] = dot3((r.wgh[...], r.wgl[...]), gs, TN)
    r.scores[...] = dot3([v[:, :E] for v in gs], [v[:, :E] for v in vs], NT)
    r.rows[...] = rows_of(r.gn[...])

    def forward(block, parts, total):
        return total + apply_state(r.feats[block], parts)

    def backward(block, parts, carry):
        one, two = carry
        qq = r.qq[...]
        grad = apply_rows(r.rows[...], parts) * query_scale(block)
        return one + grad * shifted(qq, block), two + unshifted(grad * qq, block)

    r.one[...] = jnp.zeros((T, L), F32)
    r.two[...] = jnp.zeros((T, L), F32)

    def query_gradient(h):
        carry = (r.one[...], r.two[...])
        r.one[...], r.two[...] = over_blocks(at, earlier[h], h, backward, carry, False)

    r.total[...] = jnp.zeros((T, L), F32)
    for h in range(4):
        r.total[...] = over_blocks(at, earlier[h], h, forward, r.total[...], True)
        if h < 3:
            query_gradient(h)
        if h in (1, 2):
            later[h - 1].prefixes()
    total = r.total[...] + apply_state(r.feats[LAST], tail_of(earlier))
    outputs = r.numer[...] + folded(total)
    r.gd[...] = jnp.sum(r.gn[...] * outputs, axis=1, keepdims=True) * r.inverse[...] * -0.5
    qq = r.qq[...]
    adjoint_norms.start(dot3(split((qq * r.gd[...])[:, :E]), split(qq), TN) * (1.0 / E))
    later[2].prefixes()
    later[3].prefixes()

    query_gradient(3)
    carry = backward(LAST, tail_of(earlier), (r.one[...] + r.normed[...] * r.gd[...] * (1.0 / E), r.two[...]))
    r.one[...], r.two[...] = carry
    qs, ks = [split(ref[...]) for ref in (r.qq, r.kk)]
    grad_scores = jnp.where(causal, r.scores[...] + r.gd[:, :1], 0.0)
    r.gdh[...], r.gdl[...] = split(grad_scores * r.dots[...] * (2.0 / E))
    r.dq[...] = folded(r.one[...] + r.two[...]) + dot3((r.gdh[...], r.gdl[...]), ks, NN)
    give_q = remote(r.dq, r.dqo, r.cs.at[2], r.cr.at[2], sibling)
    give_q.start()
    adjoint_norms.relay()
    for chunk in later:
        chunk.spread()
    r.dk[...] = dot3((r.gdh[...], r.gdl[...]), qs, TN)
    r.rows[...] = rows_of(r.vv[...])
    give_q.wait_recv()
    own_lanes = low == (c == 0)
    r.gh[0], r.gl[0] = split(jnp.where(own_lanes, r.dq[...], r.dqo[...]))
    for h in range(2):
        rows = pl.ds(h * 256, 256)
        grad = dot3((r.xth[rows], r.xtl[rows]), (r.gh[0], r.gl[0]), NN)
        for i in range(16):
            r.dwq[i % NY, 4 * h + i // NY] = grad[i * 16 : (i + 1) * 16]
    q_y = [
        remote(r.dwq.at[lax.rem(y + d, NY)], r.qry.at[d], r.qs.at[0], r.qr.at[0], at.py[d]) for d in (2, 1, 3)
    ]
    all_q_y = settle(r.qry.at[pl.ds(1, NY - 1)], r.qs.at[0], r.qr.at[0], at.py[1])
    all_q_z = settle(r.qrz.at[pl.ds(1, NZ - 1)], r.qs.at[1], r.qr.at[1], at.pz[1])

    def keys(block, parts, carry, mask=None):
        total, one, two = carry
        kk = r.kk[...]
        shift = shifted(kk, block)
        if mask is not None:
            shift, kk = jnp.where(mask, shift, 0.0), jnp.where(mask, kk, 0.0)
        total = total + apply_state(feature_pair(kk * shift), parts)
        grad = apply_rows(r.rows[...], parts)
        return total, one + grad * shift, two + unshifted(grad * kk, block)

    zero = jnp.zeros((T, L), F32)
    carry = (zero, zero, zero)
    for h in range(4):
        if h == 3:
            later[3].all_of(3).wait_recv()
            for copy in q_y:
                copy.start()
        carry = over_blocks(at, later[h], h, keys, carry, h < 3)
    total, one, two = keys(LAST, tail_of(later), carry, low)
    ks = split(r.kk[...])
    normed = dot3([v[:, :E] for v in ks], adjoint_norms.result(), NN)
    dv = r.dv[...] + folded(total)
    dk = r.dk[...] + folded(one + two) + 2.0 * normed
    r.kv[...] = jnp.where(low, dk, dv)
    give_kv = remote(r.kv, r.kvo, r.cs.at[3], r.cr.at[3], sibling)
    give_kv.start()
    give_kv.wait_recv()
    other = r.kvo[...]
    turned = roll(other, E)
    r.gh[1], r.gl[1] = split(jnp.where(own_lanes, dk, jnp.where(c == 0, turned, other)))
    r.gh[2], r.gl[2] = split(jnp.where(own_lanes, dv, jnp.where(c == 0, other, turned)))

    kv = [jnp.concatenate([g[1], g[2]], axis=1) for g in (r.gh, r.gl)]
    first = []
    for h in range(2):
        rows = pl.ds(h * 256, 256)
        grad = dot3((r.xth[rows], r.xtl[rows]), kv, NN)
        for i in range(16):
            r.dw[h, i % NY, i // NY] = grad[i * 16 : (i + 1) * 16]
        for d in (2, 1, 3):
            remote(
                r.dw.at[h, lax.rem(y + d, NY)], r.wry.at[h, d], r.ws.at[h], r.wr.at[h], at.py[d]
            ).start()
        first.append(settle(r.wry.at[h, pl.ds(1, NY - 1)], r.ws.at[h], r.wr.at[h], at.py[1]))

    all_q_y.wait_recv()
    r.qty[...] = r.dwq[y] + r.qry[1] + r.qry[2] + r.qry[3]
    for d in (4, 3, 5, 2, 6, 1, 7):
        remote(r.qty.at[lax.rem(z + d, NZ)], r.qrz.at[d], r.qs.at[1], r.qr.at[1], at.pz[d]).start()

    for d in (2, 1, 3, 0):
        rows = pl.ds(pl.multiple_of(lax.rem(x + d, NX) * 256, 256), 256)
        part = jnp.zeros((128, 256), F32)
        for i in range(3):
            part = part + dot3((r.gh[i, mine], r.gl[i, mine]), (r.wh[i, rows], r.wl[i, rows]), NT)
        r.sx[d] = part
        if d:
            remote(r.sx.at[d], r.rx.at[d], r.os.at[0], r.os.at[1], at.px[d]).start()
    all_x = settle(r.rx.at[pl.ds(1, NX - 1)], r.os.at[0], r.os.at[1], at.px[1])

    for h in range(2):
        first[h].wait_recv()
        r.wty[h] = r.dw[h, y] + r.wry[h, 1] + r.wry[h, 2] + r.wry[h, 3]
        for j in (0, 3, 1, 2):
            target = 4 * h + j
            d = lax.rem(target - z + NZ, NZ)
            copy = remote(r.wty.at[h, j], r.wrz.at[d], r.ws.at[2], r.wr.at[2], device(x, y, target, c))
            pl.when(target != z)(copy.start)
    all_x.wait_recv()
    r.gx[...] = r.sx[0] + r.rx[1] + r.rx[2] + r.rx[3]
    all_q_z.wait_recv()
    total = r.qty[z]
    for d in range(1, NZ):
        total = total + r.qrz[d]
    r.gw[0] = total
    for copy in [own, grads, give_q, give_kv, all_q_y, all_q_z, all_x] + first:
        copy.wait_send()
    settle(r.xg.at[pl.ds(0, 3), pl.ds(0, 128)], r.xs, r.xr.at[0, 0], at.px[1]).wait_send()
    settle(r.xg.at[pl.ds(0, 3), pl.ds(0, 128)], r.fs, r.fr.at[0, 0], sibling).wait_send()
    for group in earlier + later + [norms, adjoint_norms]:
        group.close()
    all_z = settle(r.wrz.at[pl.ds(1, NZ - 1)], r.ws.at[2], r.wr.at[2], at.pz[1])
    all_z.wait_recv()
    total = r.wty[lax.div(z, 4), lax.rem(z, 4)]
    for d in range(1, NZ):
        total = total + r.wrz[d]
    r.gw[1] = total[:, :L]
    r.gw[2] = total[:, L:]
    all_z.wait_send()


def fused(inputs, weights, out_grads):
    dma = pltpu.SemaphoreType.DMA

    def vm(*shape, dtype=F32):
        return pltpu.VMEM(shape, dtype)

    scratch = dict(
        w=vm(3, 1024, L),
        wh=vm(3, 1024, L, dtype=BF16),
        wl=vm(3, 1024, L, dtype=BF16),
        xg=vm(NX, T, 256),
        xh=vm(NX, T, 256, dtype=BF16),
        xl=vm(NX, T, 256, dtype=BF16),
        gg=vm(T, L),
        qq=vm(T, L),
        kk=vm(T, L),
        vv=vm(T, L),
        cols=vm(L, T, dtype=BF16),
        rows=vm(T, 3 * E, dtype=BF16),
        feats=vm(LAST + 1, T, 2 * L, dtype=BF16),
        dots=vm(T, T),
        wgh=vm(T, T, dtype=BF16),
        wgl=vm(T, T, dtype=BF16),
        numer=vm(T, L),
        inverse=vm(T, L),
        normed=vm(T, L),
        total=vm(T, L),
        scores=vm(T, T),
        gn=vm(T, L),
        gd=vm(T, L),
        one=vm(T, L),
        dq=vm(T, L),
        dk=vm(T, L),
        dv=vm(T, L),
        two=vm(T, L),
        gdh=vm(T, T, dtype=BF16),
        gdl=vm(T, T, dtype=BF16),
        dqo=vm(T, L),
        kv=vm(T, L),
        kvo=vm(T, L),
        gh=vm(3, T, L, dtype=BF16),
        gl=vm(3, T, L, dtype=BF16),
        turned=vm(256, T, dtype=BF16),
        xth=vm(512, T, dtype=BF16),
        xtl=vm(512, T, dtype=BF16),
        dwq=vm(NY, NZ, 16, L),
        qry=vm(NY, NZ, 16, L),
        qty=vm(NZ, 16, L),
        qrz=vm(NZ, 16, L),
        dw=vm(2, NY, 4, 16, 2 * L),
        wry=vm(2, NY, 4, 16, 2 * L),
        wty=vm(2, 4, 16, 2 * L),
        wrz=vm(NZ, 16, 2 * L),
        sx=vm(NX, 128, 256),
        rx=vm(NX, 128, 256),
    )
    sems = dict(
        wsem=dma,
        xs=dma,
        xr=dma((2, NX)),
        fs=dma,
        fr=dma((2, NX)),
        cs=dma((4,)),
        cr=dma((4,)),
        qs=dma((2,)),
        qr=dma((2,)),
        ws=dma((3,)),
        wr=dma((3,)),
        os=dma((2,)),
    )
    bufs = [
        [
            [
                vm(NY, rows, L),
                vm(NY, rows, L),
                vm(NY, rows, L),
                vm(rows, L),
                vm(NZ, piece, L),
                vm(NZ, piece, L),
                vm(rows, L),
                vm(NY, rows, L),
                vm(NY, rows, L),
            ]
            for rows, piece, _ in CHUNKS
        ]
        for _ in range(2)
    ]
    small = [vm(*shape, 32, L) for _ in range(2) for shape in ((), (NY,), (), (NZ,))]
    scan_sems = [dma((2, len(CHUNKS), 4)), dma((2, len(CHUNKS), 4)), dma((2, 2)), dma((2, 2))]
    flat = list(scratch.values()) + list(sems.values()) + [b for s in bufs for h in s for b in h] + small + scan_sems
    names = ["x_in", "w_in", "g_in", "gx", "gw"] + list(scratch) + list(sems)

    def kernel(*refs):
        named, rest = refs[: len(names)], refs[len(names) :]
        count = len(CHUNKS)
        held = [[[rest[(s * count + h) * 9 + i] for h in range(count)] for s in range(2)] for i in range(9)]
        rest = rest[18 * count :]
        fused_kernel(
            names + ["bufs", "small", "sems", "small_sems"], *named, held, (rest[:4], rest[4:8]), rest[8:10], rest[10:]
        )

    return pl.pallas_call(
        kernel,
        out_shape=(jax.ShapeDtypeStruct((128, 256), F32), jax.ShapeDtypeStruct((3, 16, L), F32)),
        in_specs=[VMEM, pl.BlockSpec(memory_space=pl.ANY), VMEM],
        out_specs=(VMEM, VMEM),
        scratch_shapes=flat,
        compiler_params=pltpu.CompilerParams(collective_id=0, has_side_effects=True, vmem_limit_bytes=LIMIT),
        name="fused",
    )(inputs, weights, out_grads)


def finish_kernel(gx, gw, dx, dw):
    dx[...] = gx[...]
    dw[...] = gw[...]


def per_device(inputs, proj_weights, out_grads):
    gx, gw = fused(inputs, proj_weights.transpose(1, 0, 2), out_grads)
    dx, dw = pl.pallas_call(
        finish_kernel,
        out_shape=(jax.ShapeDtypeStruct((128, 256), F32), jax.ShapeDtypeStruct((3, 16, L), F32)),
        in_specs=[VMEM, VMEM],
        out_specs=(VMEM, VMEM),
        name="finish",
    )(gx, gw)
    return dx, dw.transpose(1, 0, 2)


def solution(mesh):
    return jax.shard_map(
        per_device,
        mesh=mesh,
        in_specs=(P("seq", "head"), P(None, None, "head"), P("seq", "head")),
        out_specs=(P("seq", "head"), P("seq", None, "head")),
        check_vma=False,
    )
```

```python
import functools
import types

import jax
import jax.numpy as jnp
from jax import lax
from jax.experimental import pallas as pl
from jax.experimental.pallas import tpu as pltpu
from jax.sharding import PartitionSpec as P

MESH = pl.DeviceIdType.MESH
F32, BF16 = jnp.float32, jnp.bfloat16
E = 64
L = 128
T = 256
NX, NY, NZ = 4, 4, 8
LAST = 16
CHUNKS = ((64, 8, 8), (64, 8, 8), (80, 16, 5), (64, 8, 8))
WITH_LAST = 2
VMEM = pl.BlockSpec(memory_space=pltpu.VMEM)
LIMIT = 56 * 2**20


def place():
    seq = lax.axis_index("seq")
    return lax.axis_index("head"), lax.rem(lax.div(seq, 2), NY), lax.div(seq, 2 * NY), lax.rem(seq, 2)


def device(x, y, z, c):
    return (z * (2 * NY) + y * 2 + c, x)


def remote(src, dst, send, recv, peer):
    return pltpu.make_async_remote_copy(
        src_ref=src, dst_ref=dst, send_sem=send, recv_sem=recv, device_id=peer, device_id_type=MESH
    )


def settle(ref, send, recv, peer):
    return remote(ref, ref, send, recv, peer)


def split(value):
    high = value.astype(BF16)
    return high, (value - high.astype(F32)).astype(BF16)


NN = (((1,), (0,)), ((), ()))
NT = (((1,), (1,)), ((), ()))
TN = (((0,), (0,)), ((), ()))


def dot(a, b, dims):
    return lax.dot_general(a, b, dims, preferred_element_type=F32)


def dot3(a, b, dims):
    return dot(a[0], b[0], dims) + (dot(a[0], b[1], dims) + dot(a[1], b[0], dims))


def lower():
    return lax.broadcasted_iota(jnp.int32, (1, L), 1) < E


def roll(value, shift):
    return pltpu.roll(value, shift, 1)


def shifted(double, block):
    return jnp.where(lower(), roll(double, E - 2 * block), roll(double, E - 1 - 2 * block))


def query_scale(block):
    distance = 2 * block + jnp.where(lower(), 0, 1)
    once = jnp.where(distance > 32, 0.0, 1.0 / E)
    return jnp.where((distance > 0) & (distance < 32), 2.0 / E, once)


def unshifted(term, block):
    low = lower()
    return roll(jnp.where(low, term, 0.0), 2 * block) + roll(jnp.where(low, 0.0, term), 2 * block + 1)


def folded(value):
    return value + roll(value, E)


def columns_of(double):
    high, low = split(double.T)
    return jnp.concatenate([high[:E], low[:E]], axis=0)


def state_block(columns, feats):
    product = dot(columns, feats, NN)
    product = product[:, :L] + product[:, L:]
    return product[:E] + product[E:]


def feature_pair(features):
    return jnp.concatenate(split(features), axis=1)


def rows_of(double):
    high, low = split(double)
    return jnp.concatenate([high[:, :E], low[:, :E], high[:, :E]], axis=1)


def apply_state(pair, parts):
    rows = jnp.concatenate(parts, axis=0)
    return dot(pair, jnp.concatenate([rows, rows], axis=1), NT)


def apply_rows(rows, parts):
    high, low = parts
    return dot(rows, jnp.concatenate([high, high, low], axis=0), NN)


class Chunk:
    def __init__(self, at, chunk, reverse, bufs, sems):
        self.rows, self.piece, self.owners = CHUNKS[chunk]
        self.at, self.reverse = at, reverse
        self.st, self.ry, self.py, self.tot, self.rz, self.pz, self.ez, self.oy, self.out = bufs
        send, recv = [[sem.at[int(reverse), chunk, stage] for stage in range(4)] for sem in sems]
        y, z = at.y, at.z
        self.first = [None] + [
            remote(self.st.at[lax.rem(y + d, NY)], self.ry.at[d], send[0], recv[0], at.py[d]) for d in range(1, NY)
        ]
        self.second, self.third = [None], [None]
        for d in range(1, NZ):
            target = lax.rem(z + d, NZ)
            self.second.append(remote(self.tot.at[self.part(target)], self.rz.at[d], send[1], recv[1], at.pz[d]))
            self.third.append(remote(self.pz.at[target], self.ez.at[self.part(z)], send[2], recv[2], at.pz[d]))
        self.fourth = [None] + [
            remote(self.oy.at[d], self.out.at[y], send[3], recv[3], at.py[d]) for d in range(1, NY)
        ]
        self.send, self.recv = send, recv

    def all_of(self, stage, pieces=NZ - 1):
        ref = self.ry.at[pl.ds(1, NY - 1)] if stage in (0, 3) else self.rz.at[pl.ds(0, pieces)]
        return settle(ref, self.send[stage], self.recv[stage], self.at.py[1])

    def part(self, index):
        return pl.ds(pl.multiple_of(lax.min(index, self.owners - 1) * self.piece, 8), self.piece)

    def owner(self, index, act, otherwise=None):
        if self.owners == NZ:
            act()
        else:
            pl.when(index < self.owners)(act)
            if otherwise is not None:
                pl.when(index >= self.owners)(otherwise)

    def ordered(self, n):
        return range(n - 1, -1, -1) if self.reverse else range(n)

    def totals(self):
        y, z = self.at.y, self.at.z
        self.all_of(0).wait_recv()
        running = jnp.zeros((self.rows, L), F32)
        for index in self.ordered(NY):
            self.py[index] = running
            running = running + self.ry[lax.rem(y + NY - index, NY)]
        self.tot[...] = running
        for d in (4, 3, 5, 2, 6, 1, 7):
            self.owner(lax.rem(z + d, NZ), self.second[d].start)

    def prefixes(self):
        z = self.at.z

        def act():
            self.rz[0] = self.tot[self.part(z)]
            self.all_of(1).wait_recv()
            running = jnp.zeros((self.piece, L), F32)
            for index in self.ordered(NZ):
                self.pz[index] = running
                running = running + self.rz[lax.rem(z + NZ - index, NZ)]
            for d in (4, 3, 5, 2, 6, 1, 7):
                self.third[d].start()
            self.ez[self.part(z)] = self.pz[z]

        self.owner(z, act)

    def spread(self):
        y, z = self.at.y, self.at.z
        self.owner(
            z,
            lambda: self.all_of(2, self.owners - 1).wait_recv(),
            lambda: self.all_of(2, self.owners).wait_recv(),
        )
        for d in (2, 1, 3):
            self.oy[d] = self.ez[...] + self.py[lax.rem(y + d, NY)]
            self.fourth[d].start()
        self.out[y] = self.ez[...] + self.py[y]

    def close(self):
        self.all_of(0).wait_send()
        self.owner(
            self.at.z,
            lambda: self.all_of(1, self.owners - 1).wait_send(),
            lambda: self.all_of(1, self.owners).wait_send(),
        )
        self.owner(self.at.z, lambda: self.all_of(2).wait_send())
        self.all_of(3).wait_send()


class Norms:
    def __init__(self, at, reverse, bufs, sems):
        self.at, self.reverse = at, reverse
        self.own, self.ry, self.tot, self.rz = bufs
        send, recv = [[sem.at[int(reverse), stage] for stage in range(2)] for sem in sems]
        self.first = [remote(self.own, self.ry.at[d], send[0], recv[0], at.py[d]) for d in (2, 1, 3)]
        self.second = [remote(self.tot, self.rz.at[d], send[1], recv[1], at.pz[d]) for d in (4, 3, 5, 2, 6, 1, 7)]
        self.all_first = settle(self.ry.at[pl.ds(1, NY - 1)], send[0], recv[0], at.py[1])
        self.all_second = settle(self.rz.at[pl.ds(1, NZ - 1)], send[1], recv[1], at.pz[1])

    def counts(self, d, index):
        return d > index if self.reverse else d <= index

    def start(self, matrix):
        self.own[...] = jnp.where(lower(), matrix[:32], matrix[32:])
        for copy in self.first:
            copy.start()

    def relay(self):
        self.all_first.wait_recv()
        self.tot[...] = self.own[...] + self.ry[1] + self.ry[2] + self.ry[3]
        for copy in self.second:
            copy.start()

    def result(self):
        self.all_second.wait_recv()
        total = jnp.zeros((32, L), F32)
        for d in range(1, NZ):
            total = total + jnp.where(self.counts(d, self.at.z), self.rz[d], 0.0)
        for d in range(1, NY):
            total = total + jnp.where(self.counts(d, self.at.y), self.ry[d], 0.0)
        turned = roll(total, E)
        low = lower()
        return split(jnp.concatenate([jnp.where(low, total, turned), jnp.where(low, turned, total)], axis=0))

    def close(self):
        self.all_first.wait_send()
        self.all_second.wait_send()


def fill(at, chunk, h, make):
    if h == WITH_LAST:
        rows = make(LAST)
        for q in range(NY):
            chunk.st[q, E:] = rows[q * 16 : (q + 1) * 16]
        chunk.ry[0, E:] = chunk.st[at.y, E:]
    for d in (2, 1, 3, 0):
        q = lax.rem(at.y + d, NY)
        block = make(4 * h + q)
        if d == 0:
            chunk.ry[0, :E] = block
        else:
            chunk.st[q, :E] = block
            chunk.first[d].start()


def tail_of(chunks):
    return split(jnp.concatenate([chunks[WITH_LAST].out[q, E:] for q in range(NY)], axis=0))


def over_blocks(at, chunk, h, step, carry, wait):
    for d in range(NY):
        if wait and d == 1:
            chunk.all_of(3).wait_recv()
        q = lax.rem(at.y + NY - d, NY)
        carry = step(4 * h + q, split(chunk.out[q, :E]), carry)
    return carry


def fused_kernel(names, *refs):
    r = types.SimpleNamespace(**dict(zip(names, refs)))
    x, y, z, c = place()
    at = types.SimpleNamespace(x=x, y=y, z=z, c=c)
    sibling = device(x, y, z, 1 - c)
    at.px = [None] + [device(lax.rem(x + d, NX), y, z, c) for d in range(1, NX)]
    at.py = [None] + [device(x, lax.rem(y + d, NY), z, c) for d in range(1, NY)]
    at.pz = [None] + [device(x, y, lax.rem(z + d, NZ), c) for d in range(1, NZ)]
    low = lower()

    barrier = pltpu.get_barrier_semaphore()
    peers = [sibling] + at.px[1:] + at.py[1:] + at.pz[1:]
    for peer in peers:
        pl.semaphore_signal(barrier, inc=1, device_id=peer, device_id_type=MESH)
    mine = pl.ds(pl.multiple_of(c * 128, 128), 128)
    load_x = pltpu.make_async_copy(r.x_in, r.xg.at[x, mine], r.wsem.at[1])
    load_g = pltpu.make_async_copy(r.g_in, r.gg.at[mine], r.wsem.at[2])
    load = pltpu.make_async_copy(r.w_in, r.w, r.wsem.at[0])
    for copy in (load_x, load_g, load):
        copy.start()
    load.wait()

    def split_weights(b, carry):
        rows = pl.ds(pl.multiple_of(b * 256, 256), 256)
        for i in range(3):
            r.wh[i, rows], r.wl[i, rows] = split(r.w[i, rows])
        return carry

    lax.fori_loop(0, NX, split_weights, 0)
    load_x.wait()
    load_g.wait()
    pl.semaphore_wait(barrier, len(peers))

    over_x = [[None] * NX, [None] * NX]
    forwards = [[None] * NX, [None] * NX]
    halves = [pl.ds(pl.multiple_of(c * 128 + 64 * k, 64), 64) for k in range(2)]
    for k in range(2):
        for d in (2, 1, 3):
            over_x[k][d] = remote(
                r.xg.at[x, halves[k]], r.xg.at[x, halves[k]], r.xs, r.xr.at[k, d], at.px[d]
            )
            over_x[k][d].start()
    own = remote(r.xg.at[x, mine], r.xg.at[x, mine], r.cs.at[0], r.cr.at[0], sibling)
    own.start()
    grads = remote(r.gg.at[mine], r.gg.at[mine], r.cs.at[1], r.cr.at[1], sibling)
    grads.start()

    def project(b, sums):
        rows = pl.ds(pl.multiple_of(b * 256, 256), 256)
        r.xh[b], r.xl[b] = split(r.xg[b])
        feats = (r.xh[b], r.xl[b])
        return [sums[i] + dot3(feats, (r.wh[i, rows], r.wl[i, rows]), NN) for i in range(3)]

    own.wait_recv()
    sums = project(x, [jnp.zeros((T, L), F32) for _ in range(3)])
    for k in range(2):
        for d in (1, 3, 2):
            over_x[k][d].wait_recv()
            landed = r.xg.at[lax.rem(x + NX - d, NX), halves[k]]
            forwards[k][d] = remote(landed, landed, r.fs, r.fr.at[k, d], sibling)
            forwards[k][d].start()
    for d in (1, 3, 2):
        for k in range(2):
            forwards[k][d].wait_recv()
        sums = project(lax.rem(x + NX - d, NX), sums)

    def doubled(both):
        return jnp.where(low == (c == 0), both, roll(both, E))

    r.qq[...] = doubled(sums[0])
    r.kk[...] = doubled(sums[1])
    r.vv[...] = doubled(sums[2])

    scans = []
    for reverse in (False, True):
        bufs = [[buf[int(reverse)][h] for buf in r.bufs] for h in range(len(CHUNKS))]
        scans.append([Chunk(at, h, reverse, bufs[h], r.sems) for h in range(len(CHUNKS))])
    earlier, later = scans

    norms, adjoint_norms = [Norms(at, v, r.small[int(v)], r.small_sems) for v in (False, True)]
    ks = split(r.kk[...])
    norms.start(dot3([v[:, :E] for v in ks], ks, TN))

    r.cols[...] = columns_of(r.vv[...])

    def key_block(block):
        kk = r.kk[...]
        return state_block(r.cols[...], feature_pair(kk * shifted(kk, block)))

    for h in range(4):
        if h == 2:
            norms.relay()
        fill(at, earlier[h], h, key_block)

    def query_feature(block, carry):
        qq = r.qq[...]
        r.feats[block] = feature_pair(qq * shifted(qq, block) * query_scale(block))
        return carry

    for h, chunk in enumerate(earlier):
        chunk.totals()
        lax.fori_loop(4 * h, 4 * h + 4, query_feature, 0)
    query_feature(LAST, 0)
    grads.wait_recv()
    causal = lax.broadcasted_iota(jnp.int32, (T, T), 0) >= lax.broadcasted_iota(jnp.int32, (T, T), 1)
    qs, ks, vs = [split(ref[...]) for ref in (r.qq, r.kk, r.vv)]
    r.dots[...] = dot3([v[:, :E] for v in qs], [v[:, :E] for v in ks], NT)
    weights = jnp.where(causal, r.dots[...] * r.dots[...] * (1.0 / E), 0.0)
    r.wgh[...], r.wgl[...] = split(weights)
    near = 1.0 + jnp.sum(weights, axis=1, keepdims=True)

    r.normed[...] = dot3([v[:, :E] for v in qs], norms.result(), NN)
    denom = near + jnp.sum(r.normed[...] * r.qq[...], axis=1, keepdims=True) * (0.5 / E)
    r.inverse[...] = jnp.broadcast_to(1.0 / denom, (T, L))
    r.gn[...] = doubled(r.gg[...]) * r.inverse[...]
    r.cols[...] = columns_of(r.gn[...])

    def query_block(block):
        return state_block(r.cols[...], r.feats[block])

    for h in range(4):
        fill(at, later[h], h, query_block)
    for chunk in earlier:
        chunk.prefixes()

    def transposed(b, carry):
        for to, value in ((r.xth, r.xh[b]), (r.xtl, r.xl[b])):
            r.turned[...] = value.T
            for i in range(8):
                rows = pl.ds(pl.multiple_of(i * 32 + c * 16, 16), 16)
                to[pl.ds(pl.multiple_of(b * 128 + i * 16, 16), 16)] = r.turned[rows]
        return carry

    lax.fori_loop(0, NX, transposed, 0)
    for h in range(4):
        earlier[h].spread()
        later[h].totals()

    gs = split(r.gn[...])
    r.numer[...] = dot3((r.wgh[...], r.wgl[...]), vs, NN)
    r.dv[...] = dot3((r.wgh[...], r.wgl[...]), gs, TN)
    r.scores[...] = dot3([v[:, :E] for v in gs], [v[:, :E] for v in vs], NT)
    r.rows[...] = rows_of(r.gn[...])

    def forward(block, parts, total):
        return total + apply_state(r.feats[block], parts)

    def backward(block, parts, carry):
        one, two = carry
        qq = r.qq[...]
        grad = apply_rows(r.rows[...], parts) * query_scale(block)
        return one + grad * shifted(qq, block), two + unshifted(grad * qq, block)

    r.one[...] = jnp.zeros((T, L), F32)
    r.two[...] = jnp.zeros((T, L), F32)

    def query_gradient(h):
        carry = (r.one[...], r.two[...])
        r.one[...], r.two[...] = over_blocks(at, earlier[h], h, backward, carry, False)

    r.total[...] = jnp.zeros((T, L), F32)
    for h in range(4):
        r.total[...] = over_blocks(at, earlier[h], h, forward, r.total[...], True)
        if h < 3:
            query_gradient(h)
        if h in (1, 2):
            later[h - 1].prefixes()
    total = r.total[...] + apply_state(r.feats[LAST], tail_of(earlier))
    outputs = r.numer[...] + folded(total)
    r.gd[...] = jnp.sum(r.gn[...] * outputs, axis=1, keepdims=True) * r.inverse[...] * -0.5
    qq = r.qq[...]
    adjoint_norms.start(dot3(split((qq * r.gd[...])[:, :E]), split(qq), TN) * (1.0 / E))
    later[2].prefixes()
    later[3].prefixes()

    query_gradient(3)
    carry = backward(LAST, tail_of(earlier), (r.one[...] + r.normed[...] * r.gd[...] * (1.0 / E), r.two[...]))
    r.one[...], r.two[...] = carry
    qs, ks = [split(ref[...]) for ref in (r.qq, r.kk)]
    grad_scores = jnp.where(causal, r.scores[...] + r.gd[:, :1], 0.0)
    r.gdh[...], r.gdl[...] = split(grad_scores * r.dots[...] * (2.0 / E))
    r.dq[...] = folded(r.one[...] + r.two[...]) + dot3((r.gdh[...], r.gdl[...]), ks, NN)
    give_q = remote(r.dq, r.dqo, r.cs.at[2], r.cr.at[2], sibling)
    give_q.start()
    adjoint_norms.relay()
    for chunk in later:
        chunk.spread()
    r.dk[...] = dot3((r.gdh[...], r.gdl[...]), qs, TN)
    r.rows[...] = rows_of(r.vv[...])
    give_q.wait_recv()
    own_lanes = low == (c == 0)
    r.gh[0], r.gl[0] = split(jnp.where(own_lanes, r.dq[...], r.dqo[...]))
    for h in range(2):
        rows = pl.ds(h * 256, 256)
        grad = dot3((r.xth[rows], r.xtl[rows]), (r.gh[0], r.gl[0]), NN)
        for i in range(16):
            r.dwq[i % NY, 4 * h + i // NY] = grad[i * 16 : (i + 1) * 16]
    q_y = [
        remote(r.dwq.at[lax.rem(y + d, NY)], r.qry.at[d], r.qs.at[0], r.qr.at[0], at.py[d]) for d in (2, 1, 3)
    ]
    all_q_y = settle(r.qry.at[pl.ds(1, NY - 1)], r.qs.at[0], r.qr.at[0], at.py[1])
    all_q_z = settle(r.qrz.at[pl.ds(1, NZ - 1)], r.qs.at[1], r.qr.at[1], at.pz[1])

    def keys(block, parts, carry, mask=None):
        total, one, two = carry
        kk = r.kk[...]
        shift = shifted(kk, block)
        if mask is not None:
            shift, kk = jnp.where(mask, shift, 0.0), jnp.where(mask, kk, 0.0)
        total = total + apply_state(feature_pair(kk * shift), parts)
        grad = apply_rows(r.rows[...], parts)
        return total, one + grad * shift, two + unshifted(grad * kk, block)

    zero = jnp.zeros((T, L), F32)
    carry = (zero, zero, zero)
    for h in range(4):
        if h == 3:
            later[3].all_of(3).wait_recv()
            for copy in q_y:
                copy.start()
        carry = over_blocks(at, later[h], h, keys, carry, h < 3)
    total, one, two = keys(LAST, tail_of(later), carry, low)
    ks = split(r.kk[...])
    normed = dot3([v[:, :E] for v in ks], adjoint_norms.result(), NN)
    dv = r.dv[...] + folded(total)
    dk = r.dk[...] + folded(one + two) + 2.0 * normed
    r.kv[...] = jnp.where(low, dk, dv)
    give_kv = remote(r.kv, r.kvo, r.cs.at[3], r.cr.at[3], sibling)
    give_kv.start()
    give_kv.wait_recv()
    other = r.kvo[...]
    turned = roll(other, E)
    r.gh[1], r.gl[1] = split(jnp.where(own_lanes, dk, jnp.where(c == 0, turned, other)))
    r.gh[2], r.gl[2] = split(jnp.where(own_lanes, dv, jnp.where(c == 0, other, turned)))

    kv = [jnp.concatenate([g[1], g[2]], axis=1) for g in (r.gh, r.gl)]
    first = []
    for h in range(2):
        rows = pl.ds(h * 256, 256)
        grad = dot3((r.xth[rows], r.xtl[rows]), kv, NN)
        for i in range(16):
            r.dw[h, i % NY, i // NY] = grad[i * 16 : (i + 1) * 16]
        for d in (2, 1, 3):
            remote(
                r.dw.at[h, lax.rem(y + d, NY)], r.wry.at[h, d], r.ws.at[h], r.wr.at[h], at.py[d]
            ).start()
        first.append(settle(r.wry.at[h, pl.ds(1, NY - 1)], r.ws.at[h], r.wr.at[h], at.py[1]))

    all_q_y.wait_recv()
    r.qty[...] = r.dwq[y] + r.qry[1] + r.qry[2] + r.qry[3]
    for d in (4, 3, 5, 2, 6, 1, 7):
        remote(r.qty.at[lax.rem(z + d, NZ)], r.qrz.at[d], r.qs.at[1], r.qr.at[1], at.pz[d]).start()

    for d in (2, 1, 3, 0):
        rows = pl.ds(pl.multiple_of(lax.rem(x + d, NX) * 256, 256), 256)
        part = jnp.zeros((128, 256), F32)
        for i in range(3):
            part = part + dot3((r.gh[i, mine], r.gl[i, mine]), (r.wh[i, rows], r.wl[i, rows]), NT)
        r.sx[d] = part
        if d:
            remote(r.sx.at[d], r.rx.at[d], r.os.at[0], r.os.at[1], at.px[d]).start()
    all_x = settle(r.rx.at[pl.ds(1, NX - 1)], r.os.at[0], r.os.at[1], at.px[1])

    for h in range(2):
        first[h].wait_recv()
        r.wty[h] = r.dw[h, y] + r.wry[h, 1] + r.wry[h, 2] + r.wry[h, 3]
        for j in (0, 3, 1, 2):
            target = 4 * h + j
            d = lax.rem(target - z + NZ, NZ)
            copy = remote(r.wty.at[h, j], r.wrz.at[d], r.ws.at[2], r.wr.at[2], device(x, y, target, c))
            pl.when(target != z)(copy.start)
    all_x.wait_recv()
    r.gx[...] = r.sx[0] + r.rx[1] + r.rx[2] + r.rx[3]
    all_q_z.wait_recv()
    total = r.qty[z]
    for d in range(1, NZ):
        total = total + r.qrz[d]
    r.gw[0] = total
    for copy in [own, grads, give_q, give_kv, all_q_y, all_q_z, all_x] + first:
        copy.wait_send()
    settle(r.xg.at[pl.ds(0, 3), pl.ds(0, 128)], r.xs, r.xr.at[0, 0], at.px[1]).wait_send()
    settle(r.xg.at[pl.ds(0, 3), pl.ds(0, 128)], r.fs, r.fr.at[0, 0], sibling).wait_send()
    for group in earlier + later + [norms, adjoint_norms]:
        group.close()
    all_z = settle(r.wrz.at[pl.ds(1, NZ - 1)], r.ws.at[2], r.wr.at[2], at.pz[1])
    all_z.wait_recv()
    total = r.wty[lax.div(z, 4), lax.rem(z, 4)]
    for d in range(1, NZ):
        total = total + r.wrz[d]
    r.gw[1] = total[:, :L]
    r.gw[2] = total[:, L:]
    all_z.wait_send()


def fused(inputs, weights, out_grads):
    dma = pltpu.SemaphoreType.DMA

    def vm(*shape, dtype=F32):
        return pltpu.VMEM(shape, dtype)

    scratch = dict(
        w=vm(3, 1024, L),
        wh=vm(3, 1024, L, dtype=BF16),
        wl=vm(3, 1024, L, dtype=BF16),
        xg=vm(NX, T, 256),
        xh=vm(NX, T, 256, dtype=BF16),
        xl=vm(NX, T, 256, dtype=BF16),
        gg=vm(T, L),
        qq=vm(T, L),
        kk=vm(T, L),
        vv=vm(T, L),
        cols=vm(L, T, dtype=BF16),
        rows=vm(T, 3 * E, dtype=BF16),
        feats=vm(LAST + 1, T, 2 * L, dtype=BF16),
        dots=vm(T, T),
        wgh=vm(T, T, dtype=BF16),
        wgl=vm(T, T, dtype=BF16),
        numer=vm(T, L),
        inverse=vm(T, L),
        normed=vm(T, L),
        total=vm(T, L),
        scores=vm(T, T),
        gn=vm(T, L),
        gd=vm(T, L),
        one=vm(T, L),
        dq=vm(T, L),
        dk=vm(T, L),
        dv=vm(T, L),
        two=vm(T, L),
        gdh=vm(T, T, dtype=BF16),
        gdl=vm(T, T, dtype=BF16),
        dqo=vm(T, L),
        kv=vm(T, L),
        kvo=vm(T, L),
        gh=vm(3, T, L, dtype=BF16),
        gl=vm(3, T, L, dtype=BF16),
        turned=vm(256, T, dtype=BF16),
        xth=vm(512, T, dtype=BF16),
        xtl=vm(512, T, dtype=BF16),
        dwq=vm(NY, NZ, 16, L),
        qry=vm(NY, NZ, 16, L),
        qty=vm(NZ, 16, L),
        qrz=vm(NZ, 16, L),
        dw=vm(2, NY, 4, 16, 2 * L),
        wry=vm(2, NY, 4, 16, 2 * L),
        wty=vm(2, 4, 16, 2 * L),
        wrz=vm(NZ, 16, 2 * L),
        sx=vm(NX, 128, 256),
        rx=vm(NX, 128, 256),
    )
    sems = dict(
        wsem=dma((3,)),
        xs=dma,
        xr=dma((2, NX)),
        fs=dma,
        fr=dma((2, NX)),
        cs=dma((4,)),
        cr=dma((4,)),
        qs=dma((2,)),
        qr=dma((2,)),
        ws=dma((3,)),
        wr=dma((3,)),
        os=dma((2,)),
    )
    bufs = [
        [
            [
                vm(NY, rows, L),
                vm(NY, rows, L),
                vm(NY, rows, L),
                vm(rows, L),
                vm(NZ, piece, L),
                vm(NZ, piece, L),
                vm(rows, L),
                vm(NY, rows, L),
                vm(NY, rows, L),
            ]
            for rows, piece, _ in CHUNKS
        ]
        for _ in range(2)
    ]
    small = [vm(*shape, 32, L) for _ in range(2) for shape in ((), (NY,), (), (NZ,))]
    scan_sems = [dma((2, len(CHUNKS), 4)), dma((2, len(CHUNKS), 4)), dma((2, 2)), dma((2, 2))]
    flat = list(scratch.values()) + list(sems.values()) + [b for s in bufs for h in s for b in h] + small + scan_sems
    names = ["x_in", "w_in", "g_in", "gx", "gw"] + list(scratch) + list(sems)

    def kernel(*refs):
        named, rest = refs[: len(names)], refs[len(names) :]
        count = len(CHUNKS)
        held = [[[rest[(s * count + h) * 9 + i] for h in range(count)] for s in range(2)] for i in range(9)]
        rest = rest[18 * count :]
        fused_kernel(
            names + ["bufs", "small", "sems", "small_sems"], *named, held, (rest[:4], rest[4:8]), rest[8:10], rest[10:]
        )

    return pl.pallas_call(
        kernel,
        out_shape=(jax.ShapeDtypeStruct((128, 256), F32), jax.ShapeDtypeStruct((3, 16, L), F32)),
        in_specs=[pl.BlockSpec(memory_space=pl.ANY)] * 3,
        out_specs=(VMEM, VMEM),
        scratch_shapes=flat,
        compiler_params=pltpu.CompilerParams(collective_id=0, has_side_effects=True, vmem_limit_bytes=LIMIT),
        name="fused",
    )(inputs, weights, out_grads)


def finish_kernel(gx, gw, dx, dw):
    dx[...] = gx[...]
    dw[...] = gw[...]


def per_device(inputs, proj_weights, out_grads):
    gx, gw = fused(inputs, proj_weights.transpose(1, 0, 2), out_grads)
    dx, dw = pl.pallas_call(
        finish_kernel,
        out_shape=(jax.ShapeDtypeStruct((128, 256), F32), jax.ShapeDtypeStruct((3, 16, L), F32)),
        in_specs=[VMEM, VMEM],
        out_specs=(VMEM, VMEM),
        name="finish",
    )(gx, gw)
    return dx, dw.transpose(1, 0, 2)


def solution(mesh):
    return jax.shard_map(
        per_device,
        mesh=mesh,
        in_specs=(P("seq", "head"), P(None, None, "head"), P("seq", "head")),
        out_specs=(P("seq", "head"), P("seq", None, "head")),
        check_vma=False,
    )
```

```python
import functools
import types

import jax
import jax.numpy as jnp
from jax import lax
from jax.experimental import pallas as pl
from jax.experimental.pallas import tpu as pltpu
from jax.sharding import PartitionSpec as P

MESH = pl.DeviceIdType.MESH
F32, BF16 = jnp.float32, jnp.bfloat16
E = 64
L = 128
T = 256
NX, NY, NZ = 4, 4, 8
LAST = 16
CHUNKS = ((64, 8, 8), (64, 8, 8), (80, 16, 5), (64, 8, 8))
WITH_LAST = 2
VMEM = pl.BlockSpec(memory_space=pltpu.VMEM)
LIMIT = 56 * 2**20


def place():
    seq = lax.axis_index("seq")
    return lax.axis_index("head"), lax.rem(lax.div(seq, 2), NY), lax.div(seq, 2 * NY), lax.rem(seq, 2)


def device(x, y, z, c):
    return (z * (2 * NY) + y * 2 + c, x)


def remote(src, dst, send, recv, peer):
    return pltpu.make_async_remote_copy(
        src_ref=src, dst_ref=dst, send_sem=send, recv_sem=recv, device_id=peer, device_id_type=MESH
    )


def settle(ref, send, recv, peer):
    return remote(ref, ref, send, recv, peer)


def split(value):
    high = value.astype(BF16)
    return high, (value - high.astype(F32)).astype(BF16)


NN = (((1,), (0,)), ((), ()))
NT = (((1,), (1,)), ((), ()))
TN = (((0,), (0,)), ((), ()))


def dot(a, b, dims):
    return lax.dot_general(a, b, dims, preferred_element_type=F32)


def dot3(a, b, dims):
    return dot(a[0], b[0], dims) + (dot(a[0], b[1], dims) + dot(a[1], b[0], dims))


def lower():
    return lax.broadcasted_iota(jnp.int32, (1, L), 1) < E


def roll(value, shift):
    return pltpu.roll(value, shift, 1)


def shifted(double, block):
    return jnp.where(lower(), roll(double, E - 2 * block), roll(double, E - 1 - 2 * block))


def query_scale(block):
    distance = 2 * block + jnp.where(lower(), 0, 1)
    once = jnp.where(distance > 32, 0.0, 1.0 / E)
    return jnp.where((distance > 0) & (distance < 32), 2.0 / E, once)


def unshifted(term, block):
    low = lower()
    return roll(jnp.where(low, term, 0.0), 2 * block) + roll(jnp.where(low, 0.0, term), 2 * block + 1)


def folded(value):
    return value + roll(value, E)


def columns_of(double):
    high, low = split(double.T)
    return jnp.concatenate([high[:E], low[:E]], axis=0)


def state_block(columns, feats):
    product = dot(columns, feats, NN)
    product = product[:, :L] + product[:, L:]
    return product[:E] + product[E:]


def feature_pair(features):
    return jnp.concatenate(split(features), axis=1)


def rows_of(double):
    high, low = split(double)
    return jnp.concatenate([high[:, :E], low[:, :E], high[:, :E]], axis=1)


def apply_state(pair, parts):
    rows = jnp.concatenate(parts, axis=0)
    return dot(pair, jnp.concatenate([rows, rows], axis=1), NT)


def apply_rows(rows, parts):
    high, low = parts
    return dot(rows, jnp.concatenate([high, high, low], axis=0), NN)


class Chunk:
    def __init__(self, at, chunk, reverse, bufs, sems):
        self.rows, self.piece, self.owners = CHUNKS[chunk]
        self.at, self.reverse = at, reverse
        self.st, self.ry, self.py, self.tot, self.rz, self.pz, self.ez, self.oy, self.out = bufs
        send, recv = [[sem.at[int(reverse), chunk, stage] for stage in range(4)] for sem in sems]
        y, z = at.y, at.z
        self.first = [None] + [
            remote(self.st.at[lax.rem(y + d, NY)], self.ry.at[d], send[0], recv[0], at.py[d]) for d in range(1, NY)
        ]
        self.second, self.third = [None], [None]
        for d in range(1, NZ):
            target = lax.rem(z + d, NZ)
            self.second.append(remote(self.tot.at[self.part(target)], self.rz.at[d], send[1], recv[1], at.pz[d]))
            self.third.append(remote(self.pz.at[target], self.ez.at[self.part(z)], send[2], recv[2], at.pz[d]))
        self.fourth = [None] + [
            remote(self.oy.at[d], self.out.at[y], send[3], recv[3], at.py[d]) for d in range(1, NY)
        ]
        self.send, self.recv = send, recv

    def all_of(self, stage, pieces=NZ - 1):
        ref = self.ry.at[pl.ds(1, NY - 1)] if stage in (0, 3) else self.rz.at[pl.ds(0, pieces)]
        return settle(ref, self.send[stage], self.recv[stage], self.at.py[1])

    def part(self, index):
        return pl.ds(pl.multiple_of(lax.min(index, self.owners - 1) * self.piece, 8), self.piece)

    def owner(self, index, act, otherwise=None):
        if self.owners == NZ:
            act()
        else:
            pl.when(index < self.owners)(act)
            if otherwise is not None:
                pl.when(index >= self.owners)(otherwise)

    def ordered(self, n):
        return range(n - 1, -1, -1) if self.reverse else range(n)

    def totals(self):
        y, z = self.at.y, self.at.z
        self.all_of(0).wait_recv()
        running = jnp.zeros((self.rows, L), F32)
        for index in self.ordered(NY):
            self.py[index] = running
            running = running + self.ry[lax.rem(y + NY - index, NY)]
        self.tot[...] = running
        for d in (4, 3, 5, 2, 6, 1, 7):
            self.owner(lax.rem(z + d, NZ), self.second[d].start)

    def prefixes(self):
        z = self.at.z

        def act():
            self.rz[0] = self.tot[self.part(z)]
            self.all_of(1).wait_recv()
            running = jnp.zeros((self.piece, L), F32)
            for index in self.ordered(NZ):
                self.pz[index] = running
                running = running + self.rz[lax.rem(z + NZ - index, NZ)]
            for d in (4, 3, 5, 2, 6, 1, 7):
                self.third[d].start()
            self.ez[self.part(z)] = self.pz[z]

        self.owner(z, act)

    def spread(self):
        y, z = self.at.y, self.at.z
        self.owner(
            z,
            lambda: self.all_of(2, self.owners - 1).wait_recv(),
            lambda: self.all_of(2, self.owners).wait_recv(),
        )
        for d in (2, 1, 3):
            self.oy[d] = self.ez[...] + self.py[lax.rem(y + d, NY)]
            self.fourth[d].start()
        self.out[y] = self.ez[...] + self.py[y]

    def close(self):
        self.all_of(0).wait_send()
        self.owner(
            self.at.z,
            lambda: self.all_of(1, self.owners - 1).wait_send(),
            lambda: self.all_of(1, self.owners).wait_send(),
        )
        self.owner(self.at.z, lambda: self.all_of(2).wait_send())
        self.all_of(3).wait_send()


class Norms:
    def __init__(self, at, reverse, bufs, sems):
        self.at, self.reverse = at, reverse
        self.own, self.ry, self.tot, self.rz = bufs
        send, recv = [[sem.at[int(reverse), stage] for stage in range(2)] for sem in sems]
        self.first = [remote(self.own, self.ry.at[d], send[0], recv[0], at.py[d]) for d in (2, 1, 3)]
        self.second = [remote(self.tot, self.rz.at[d], send[1], recv[1], at.pz[d]) for d in (4, 3, 5, 2, 6, 1, 7)]
        self.all_first = settle(self.ry.at[pl.ds(1, NY - 1)], send[0], recv[0], at.py[1])
        self.all_second = settle(self.rz.at[pl.ds(1, NZ - 1)], send[1], recv[1], at.pz[1])

    def counts(self, d, index):
        return d > index if self.reverse else d <= index

    def start(self, matrix):
        self.own[...] = jnp.where(lower(), matrix[:32], matrix[32:])
        for copy in self.first:
            copy.start()

    def relay(self):
        self.all_first.wait_recv()
        self.tot[...] = self.own[...] + self.ry[1] + self.ry[2] + self.ry[3]
        for copy in self.second:
            copy.start()

    def result(self):
        self.all_second.wait_recv()
        total = jnp.zeros((32, L), F32)
        for d in range(1, NZ):
            total = total + jnp.where(self.counts(d, self.at.z), self.rz[d], 0.0)
        for d in range(1, NY):
            total = total + jnp.where(self.counts(d, self.at.y), self.ry[d], 0.0)
        turned = roll(total, E)
        low = lower()
        return split(jnp.concatenate([jnp.where(low, total, turned), jnp.where(low, turned, total)], axis=0))

    def close(self):
        self.all_first.wait_send()
        self.all_second.wait_send()


def fill(at, chunk, h, make):
    if h == WITH_LAST:
        rows = make(LAST)
        for q in range(NY):
            chunk.st[q, E:] = rows[q * 16 : (q + 1) * 16]
        chunk.ry[0, E:] = chunk.st[at.y, E:]
    for d in (2, 1, 3, 0):
        q = lax.rem(at.y + d, NY)
        block = make(4 * h + q)
        if d == 0:
            chunk.ry[0, :E] = block
        else:
            chunk.st[q, :E] = block
            chunk.first[d].start()


def tail_of(chunks):
    return split(jnp.concatenate([chunks[WITH_LAST].out[q, E:] for q in range(NY)], axis=0))


def over_blocks(at, chunk, h, step, carry, wait):
    for d in range(NY):
        if wait and d == 1:
            chunk.all_of(3).wait_recv()
        q = lax.rem(at.y + NY - d, NY)
        carry = step(4 * h + q, split(chunk.out[q, :E]), carry)
    return carry


def fused_kernel(names, *refs):
    r = types.SimpleNamespace(**dict(zip(names, refs)))
    x, y, z, c = place()
    at = types.SimpleNamespace(x=x, y=y, z=z, c=c)
    sibling = device(x, y, z, 1 - c)
    at.px = [None] + [device(lax.rem(x + d, NX), y, z, c) for d in range(1, NX)]
    at.py = [None] + [device(x, lax.rem(y + d, NY), z, c) for d in range(1, NY)]
    at.pz = [None] + [device(x, y, lax.rem(z + d, NZ), c) for d in range(1, NZ)]
    low = lower()

    barrier = pltpu.get_barrier_semaphore()
    peers = [sibling] + at.px[1:] + at.py[1:] + at.pz[1:]
    for peer in peers:
        pl.semaphore_signal(barrier, inc=1, device_id=peer, device_id_type=MESH)
    mine = pl.ds(pl.multiple_of(c * 128, 128), 128)
    load_x = pltpu.make_async_copy(r.x_in, r.xg.at[x, mine], r.wsem.at[1])
    load_g = pltpu.make_async_copy(r.g_in, r.gg.at[mine], r.wsem.at[2])
    load = pltpu.make_async_copy(r.w_in, r.w, r.wsem.at[0])
    for copy in (load_x, load_g, load):
        copy.start()
    load.wait()

    def split_weights(b, carry):
        rows = pl.ds(pl.multiple_of(b * 256, 256), 256)
        for i in range(3):
            r.wh[i, rows], r.wl[i, rows] = split(r.w[i, rows])
        return carry

    lax.fori_loop(0, NX, split_weights, 0)
    load_x.wait()
    load_g.wait()
    pl.semaphore_wait(barrier, len(peers))

    over_x = [[None] * NX, [None] * NX]
    forwards = [[None] * NX, [None] * NX]
    halves = [pl.ds(pl.multiple_of(c * 128 + 64 * k, 64), 64) for k in range(2)]
    for k in range(2):
        for d in (1, 3, 2):
            over_x[k][d] = remote(
                r.xg.at[x, halves[k]], r.xg.at[x, halves[k]], r.xs, r.xr.at[k, d], at.px[d]
            )
            over_x[k][d].start()
    own = remote(r.xg.at[x, mine], r.xg.at[x, mine], r.cs.at[0], r.cr.at[0], sibling)
    own.start()
    grads = remote(r.gg.at[mine], r.gg.at[mine], r.cs.at[1], r.cr.at[1], sibling)
    grads.start()

    def project(b, sums):
        rows = pl.ds(pl.multiple_of(b * 256, 256), 256)
        r.xh[b], r.xl[b] = split(r.xg[b])
        feats = (r.xh[b], r.xl[b])
        return [sums[i] + dot3(feats, (r.wh[i, rows], r.wl[i, rows]), NN) for i in range(3)]

    own.wait_recv()
    sums = project(x, [jnp.zeros((T, L), F32) for _ in range(3)])
    for k in range(2):
        for d in (1, 3, 2):
            over_x[k][d].wait_recv()
            landed = r.xg.at[lax.rem(x + NX - d, NX), halves[k]]
            forwards[k][d] = remote(landed, landed, r.fs, r.fr.at[k, d], sibling)
            forwards[k][d].start()
    for d in (1, 3, 2):
        for k in range(2):
            forwards[k][d].wait_recv()
        sums = project(lax.rem(x + NX - d, NX), sums)

    def doubled(both):
        return jnp.where(low == (c == 0), both, roll(both, E))

    r.qq[...] = doubled(sums[0])
    r.kk[...] = doubled(sums[1])
    r.vv[...] = doubled(sums[2])

    scans = []
    for reverse in (False, True):
        bufs = [[buf[int(reverse)][h] for buf in r.bufs] for h in range(len(CHUNKS))]
        scans.append([Chunk(at, h, reverse, bufs[h], r.sems) for h in range(len(CHUNKS))])
    earlier, later = scans

    norms, adjoint_norms = [Norms(at, v, r.small[int(v)], r.small_sems) for v in (False, True)]
    ks = split(r.kk[...])
    norms.start(dot3([v[:, :E] for v in ks], ks, TN))

    r.cols[...] = columns_of(r.vv[...])

    def key_block(block):
        kk = r.kk[...]
        return state_block(r.cols[...], feature_pair(kk * shifted(kk, block)))

    for h in range(4):
        if h == 2:
            norms.relay()
        fill(at, earlier[h], h, key_block)

    def query_feature(block, carry):
        qq = r.qq[...]
        r.feats[block] = feature_pair(qq * shifted(qq, block) * query_scale(block))
        return carry

    for h, chunk in enumerate(earlier):
        chunk.totals()
        lax.fori_loop(4 * h, 4 * h + 4, query_feature, 0)
    query_feature(LAST, 0)
    grads.wait_recv()
    causal = lax.broadcasted_iota(jnp.int32, (T, T), 0) >= lax.broadcasted_iota(jnp.int32, (T, T), 1)
    qs, ks, vs = [split(ref[...]) for ref in (r.qq, r.kk, r.vv)]
    r.dots[...] = dot3([v[:, :E] for v in qs], [v[:, :E] for v in ks], NT)
    weights = jnp.where(causal, r.dots[...] * r.dots[...] * (1.0 / E), 0.0)
    r.wgh[...], r.wgl[...] = split(weights)
    near = 1.0 + jnp.sum(weights, axis=1, keepdims=True)

    r.normed[...] = dot3([v[:, :E] for v in qs], norms.result(), NN)
    denom = near + jnp.sum(r.normed[...] * r.qq[...], axis=1, keepdims=True) * (0.5 / E)
    r.inverse[...] = jnp.broadcast_to(1.0 / denom, (T, L))
    r.gn[...] = doubled(r.gg[...]) * r.inverse[...]
    r.cols[...] = columns_of(r.gn[...])

    def query_block(block):
        return state_block(r.cols[...], r.feats[block])

    for h in range(4):
        fill(at, later[h], h, query_block)
    for chunk in earlier:
        chunk.prefixes()

    def transposed(b, carry):
        for to, value in ((r.xth, r.xh[b]), (r.xtl, r.xl[b])):
            r.turned[...] = value.T
            for i in range(8):
                rows = pl.ds(pl.multiple_of(i * 32 + c * 16, 16), 16)
                to[pl.ds(pl.multiple_of(b * 128 + i * 16, 16), 16)] = r.turned[rows]
        return carry

    lax.fori_loop(0, NX, transposed, 0)
    for h in range(4):
        earlier[h].spread()
        later[h].totals()

    gs = split(r.gn[...])
    r.numer[...] = dot3((r.wgh[...], r.wgl[...]), vs, NN)
    r.dv[...] = dot3((r.wgh[...], r.wgl[...]), gs, TN)
    r.scores[...] = dot3([v[:, :E] for v in gs], [v[:, :E] for v in vs], NT)
    r.rows[...] = rows_of(r.gn[...])

    def forward(block, parts, total):
        return total + apply_state(r.feats[block], parts)

    def backward(block, parts, carry):
        one, two = carry
        qq = r.qq[...]
        grad = apply_rows(r.rows[...], parts) * query_scale(block)
        return one + grad * shifted(qq, block), two + unshifted(grad * qq, block)

    r.one[...] = jnp.zeros((T, L), F32)
    r.two[...] = jnp.zeros((T, L), F32)

    def query_gradient(h):
        carry = (r.one[...], r.two[...])
        r.one[...], r.two[...] = over_blocks(at, earlier[h], h, backward, carry, False)

    r.total[...] = jnp.zeros((T, L), F32)
    for h in range(4):
        r.total[...] = over_blocks(at, earlier[h], h, forward, r.total[...], True)
        if h < 3:
            query_gradient(h)
        if h in (1, 2):
            later[h - 1].prefixes()
    total = r.total[...] + apply_state(r.feats[LAST], tail_of(earlier))
    outputs = r.numer[...] + folded(total)
    r.gd[...] = jnp.sum(r.gn[...] * outputs, axis=1, keepdims=True) * r.inverse[...] * -0.5
    qq = r.qq[...]
    adjoint_norms.start(dot3(split((qq * r.gd[...])[:, :E]), split(qq), TN) * (1.0 / E))
    later[2].prefixes()
    later[3].prefixes()

    query_gradient(3)
    carry = backward(LAST, tail_of(earlier), (r.one[...] + r.normed[...] * r.gd[...] * (1.0 / E), r.two[...]))
    r.one[...], r.two[...] = carry
    qs, ks = [split(ref[...]) for ref in (r.qq, r.kk)]
    grad_scores = jnp.where(causal, r.scores[...] + r.gd[:, :1], 0.0)
    r.gdh[...], r.gdl[...] = split(grad_scores * r.dots[...] * (2.0 / E))
    r.dq[...] = folded(r.one[...] + r.two[...]) + dot3((r.gdh[...], r.gdl[...]), ks, NN)
    give_q = remote(r.dq, r.dqo, r.cs.at[2], r.cr.at[2], sibling)
    give_q.start()
    adjoint_norms.relay()
    for chunk in later:
        chunk.spread()
    r.dk[...] = dot3((r.gdh[...], r.gdl[...]), qs, TN)
    r.rows[...] = rows_of(r.vv[...])
    give_q.wait_recv()
    own_lanes = low == (c == 0)
    r.gh[0], r.gl[0] = split(jnp.where(own_lanes, r.dq[...], r.dqo[...]))
    for h in range(2):
        rows = pl.ds(h * 256, 256)
        grad = dot3((r.xth[rows], r.xtl[rows]), (r.gh[0], r.gl[0]), NN)
        for i in range(16):
            r.dwq[i % NY, 4 * h + i // NY] = grad[i * 16 : (i + 1) * 16]
    q_y = [
        remote(r.dwq.at[lax.rem(y + d, NY)], r.qry.at[d], r.qs.at[0], r.qr.at[0], at.py[d]) for d in (2, 1, 3)
    ]
    all_q_y = settle(r.qry.at[pl.ds(1, NY - 1)], r.qs.at[0], r.qr.at[0], at.py[1])
    all_q_z = settle(r.qrz.at[pl.ds(1, NZ - 1)], r.qs.at[1], r.qr.at[1], at.pz[1])

    def keys(block, parts, carry, mask=None):
        total, one, two = carry
        kk = r.kk[...]
        shift = shifted(kk, block)
        if mask is not None:
            shift, kk = jnp.where(mask, shift, 0.0), jnp.where(mask, kk, 0.0)
        total = total + apply_state(feature_pair(kk * shift), parts)
        grad = apply_rows(r.rows[...], parts)
        return total, one + grad * shift, two + unshifted(grad * kk, block)

    zero = jnp.zeros((T, L), F32)
    carry = (zero, zero, zero)
    for h in range(4):
        if h == 3:
            later[3].all_of(3).wait_recv()
            for copy in q_y:
                copy.start()
        carry = over_blocks(at, later[h], h, keys, carry, h < 3)
    total, one, two = keys(LAST, tail_of(later), carry, low)
    ks = split(r.kk[...])
    dv = r.dv[...] + folded(total)
    r.kv[0] = dv
    give_v = remote(r.kv.at[0], r.kvo.at[0], r.cs.at[3], r.cr.at[3], sibling)
    give_v.start()
    normed = dot3([v[:, :E] for v in ks], adjoint_norms.result(), NN)
    dk = r.dk[...] + folded(one + two) + 2.0 * normed
    r.kv[1] = dk
    give_k = remote(r.kv.at[1], r.kvo.at[1], r.cs.at[4], r.cr.at[4], sibling)
    give_k.start()
    give_v.wait_recv()
    r.gh[2], r.gl[2] = split(jnp.where(own_lanes, dv, r.kvo[0]))
    give_k.wait_recv()
    r.gh[1], r.gl[1] = split(jnp.where(own_lanes, dk, r.kvo[1]))

    kv = [jnp.concatenate([g[1], g[2]], axis=1) for g in (r.gh, r.gl)]
    first = []
    for h in range(4):
        rows = pl.ds(h * 128, 128)
        grad = dot3((r.xth[rows], r.xtl[rows]), kv, NN)
        for i in range(8):
            r.dw[h, i % NY, i // NY] = grad[i * 16 : (i + 1) * 16]
        for d in (2, 1, 3):
            remote(
                r.dw.at[h, lax.rem(y + d, NY)], r.wry.at[h, d], r.ws.at[h], r.wr.at[h], at.py[d]
            ).start()
        first.append(settle(r.wry.at[h, pl.ds(1, NY - 1)], r.ws.at[h], r.wr.at[h], at.py[1]))

    all_q_y.wait_recv()
    r.qty[...] = r.dwq[y] + r.qry[1] + r.qry[2] + r.qry[3]
    for d in (4, 3, 5, 2, 6, 1, 7):
        remote(r.qty.at[lax.rem(z + d, NZ)], r.qrz.at[d], r.qs.at[1], r.qr.at[1], at.pz[d]).start()

    for d in (2, 1, 3, 0):
        rows = pl.ds(pl.multiple_of(lax.rem(x + d, NX) * 256, 256), 256)
        part = jnp.zeros((128, 256), F32)
        for i in range(3):
            part = part + dot3((r.gh[i, mine], r.gl[i, mine]), (r.wh[i, rows], r.wl[i, rows]), NT)
        r.sx[d] = part
        if d:
            remote(r.sx.at[d], r.rx.at[d], r.os.at[0], r.os.at[1], at.px[d]).start()
    all_x = settle(r.rx.at[pl.ds(1, NX - 1)], r.os.at[0], r.os.at[1], at.px[1])

    for h in range(4):
        first[h].wait_recv()
        r.wty[h] = r.dw[h, y] + r.wry[h, 1] + r.wry[h, 2] + r.wry[h, 3]
        for j in range(2):
            target = 2 * h + j
            d = lax.rem(target - z + NZ, NZ)
            copy = remote(r.wty.at[h, j], r.wrz.at[d], r.ws.at[4], r.wr.at[4], device(x, y, target, c))
            pl.when(target != z)(copy.start)
    all_x.wait_recv()
    r.gx[...] = r.sx[0] + r.rx[1] + r.rx[2] + r.rx[3]
    all_q_z.wait_recv()
    total = r.qty[z]
    for d in range(1, NZ):
        total = total + r.qrz[d]
    r.gw[0] = total
    for copy in [own, grads, give_q, give_k, give_v, all_q_y, all_q_z, all_x] + first:
        copy.wait_send()
    settle(r.xg.at[pl.ds(0, 3), pl.ds(0, 128)], r.xs, r.xr.at[0, 0], at.px[1]).wait_send()
    settle(r.xg.at[pl.ds(0, 3), pl.ds(0, 128)], r.fs, r.fr.at[0, 0], sibling).wait_send()
    for group in earlier + later + [norms, adjoint_norms]:
        group.close()
    all_z = settle(r.wrz.at[pl.ds(1, NZ - 1)], r.ws.at[4], r.wr.at[4], at.pz[1])
    all_z.wait_recv()
    total = r.wty[lax.div(z, 2), lax.rem(z, 2)]
    for d in range(1, NZ):
        total = total + r.wrz[d]
    r.gw[1] = total[:, :L]
    r.gw[2] = total[:, L:]
    all_z.wait_send()


def fused(inputs, weights, out_grads):
    dma = pltpu.SemaphoreType.DMA

    def vm(*shape, dtype=F32):
        return pltpu.VMEM(shape, dtype)

    scratch = dict(
        w=vm(3, 1024, L),
        wh=vm(3, 1024, L, dtype=BF16),
        wl=vm(3, 1024, L, dtype=BF16),
        xg=vm(NX, T, 256),
        xh=vm(NX, T, 256, dtype=BF16),
        xl=vm(NX, T, 256, dtype=BF16),
        gg=vm(T, L),
        qq=vm(T, L),
        kk=vm(T, L),
        vv=vm(T, L),
        cols=vm(L, T, dtype=BF16),
        rows=vm(T, 3 * E, dtype=BF16),
        feats=vm(LAST + 1, T, 2 * L, dtype=BF16),
        dots=vm(T, T),
        wgh=vm(T, T, dtype=BF16),
        wgl=vm(T, T, dtype=BF16),
        numer=vm(T, L),
        inverse=vm(T, L),
        normed=vm(T, L),
        total=vm(T, L),
        scores=vm(T, T),
        gn=vm(T, L),
        gd=vm(T, L),
        one=vm(T, L),
        dq=vm(T, L),
        dk=vm(T, L),
        dv=vm(T, L),
        two=vm(T, L),
        gdh=vm(T, T, dtype=BF16),
        gdl=vm(T, T, dtype=BF16),
        dqo=vm(T, L),
        kv=vm(2, T, L),
        kvo=vm(2, T, L),
        gh=vm(3, T, L, dtype=BF16),
        gl=vm(3, T, L, dtype=BF16),
        turned=vm(256, T, dtype=BF16),
        xth=vm(512, T, dtype=BF16),
        xtl=vm(512, T, dtype=BF16),
        dwq=vm(NY, NZ, 16, L),
        qry=vm(NY, NZ, 16, L),
        qty=vm(NZ, 16, L),
        qrz=vm(NZ, 16, L),
        dw=vm(4, NY, 2, 16, 2 * L),
        wry=vm(4, NY, 2, 16, 2 * L),
        wty=vm(4, 2, 16, 2 * L),
        wrz=vm(NZ, 16, 2 * L),
        sx=vm(NX, 128, 256),
        rx=vm(NX, 128, 256),
    )
    sems = dict(
        wsem=dma((3,)),
        xs=dma,
        xr=dma((2, NX)),
        fs=dma,
        fr=dma((2, NX)),
        cs=dma((5,)),
        cr=dma((5,)),
        qs=dma((2,)),
        qr=dma((2,)),
        ws=dma((5,)),
        wr=dma((5,)),
        os=dma((2,)),
    )
    bufs = [
        [
            [
                vm(NY, rows, L),
                vm(NY, rows, L),
                vm(NY, rows, L),
                vm(rows, L),
                vm(NZ, piece, L),
                vm(NZ, piece, L),
                vm(rows, L),
                vm(NY, rows, L),
                vm(NY, rows, L),
            ]
            for rows, piece, _ in CHUNKS
        ]
        for _ in range(2)
    ]
    small = [vm(*shape, 32, L) for _ in range(2) for shape in ((), (NY,), (), (NZ,))]
    scan_sems = [dma((2, len(CHUNKS), 4)), dma((2, len(CHUNKS), 4)), dma((2, 2)), dma((2, 2))]
    flat = list(scratch.values()) + list(sems.values()) + [b for s in bufs for h in s for b in h] + small + scan_sems
    names = ["x_in", "w_in", "g_in", "gx", "gw"] + list(scratch) + list(sems)

    def kernel(*refs):
        named, rest = refs[: len(names)], refs[len(names) :]
        count = len(CHUNKS)
        held = [[[rest[(s * count + h) * 9 + i] for h in range(count)] for s in range(2)] for i in range(9)]
        rest = rest[18 * count :]
        fused_kernel(
            names + ["bufs", "small", "sems", "small_sems"], *named, held, (rest[:4], rest[4:8]), rest[8:10], rest[10:]
        )

    return pl.pallas_call(
        kernel,
        out_shape=(jax.ShapeDtypeStruct((128, 256), F32), jax.ShapeDtypeStruct((3, 16, L), F32)),
        in_specs=[pl.BlockSpec(memory_space=pl.ANY)] * 3,
        out_specs=(VMEM, VMEM),
        scratch_shapes=flat,
        compiler_params=pltpu.CompilerParams(collective_id=0, has_side_effects=True, vmem_limit_bytes=LIMIT),
        name="fused",
    )(inputs, weights, out_grads)


def finish_kernel(gx, gw, dx, dw):
    dx[...] = gx[...]
    dw[...] = gw[...]


def per_device(inputs, proj_weights, out_grads):
    gx, gw = fused(inputs, proj_weights.transpose(1, 0, 2), out_grads)
    dx, dw = pl.pallas_call(
        finish_kernel,
        out_shape=(jax.ShapeDtypeStruct((128, 256), F32), jax.ShapeDtypeStruct((3, 16, L), F32)),
        in_specs=[VMEM, VMEM],
        out_specs=(VMEM, VMEM),
        name="finish",
    )(gx, gw)
    return dx, dw.transpose(1, 0, 2)


def solution(mesh):
    return jax.shard_map(
        per_device,
        mesh=mesh,
        in_specs=(P("seq", "head"), P(None, None, "head"), P("seq", "head")),
        out_specs=(P("seq", "head"), P("seq", None, "head")),
        check_vma=False,
    )
```

```python
import functools
import types

import jax
import jax.numpy as jnp
from jax import lax
from jax.experimental import pallas as pl
from jax.experimental.pallas import tpu as pltpu
from jax.sharding import PartitionSpec as P

MESH = pl.DeviceIdType.MESH
F32, BF16 = jnp.float32, jnp.bfloat16
E = 64
L = 128
T = 256
NX, NY, NZ = 4, 4, 8
LAST = 16
CHUNKS = ((64, 8, 8), (64, 8, 8), (80, 16, 5), (64, 8, 8))
WITH_LAST = 2
VMEM = pl.BlockSpec(memory_space=pltpu.VMEM)
LIMIT = 56 * 2**20


def place():
    seq = lax.axis_index("seq")
    return lax.axis_index("head"), lax.rem(lax.div(seq, 2), NY), lax.div(seq, 2 * NY), lax.rem(seq, 2)


def device(x, y, z, c):
    return (z * (2 * NY) + y * 2 + c, x)


def remote(src, dst, send, recv, peer):
    return pltpu.make_async_remote_copy(
        src_ref=src, dst_ref=dst, send_sem=send, recv_sem=recv, device_id=peer, device_id_type=MESH
    )


def settle(ref, send, recv, peer):
    return remote(ref, ref, send, recv, peer)


def split(value):
    high = value.astype(BF16)
    return high, (value - high.astype(F32)).astype(BF16)


NN = (((1,), (0,)), ((), ()))
NT = (((1,), (1,)), ((), ()))
TN = (((0,), (0,)), ((), ()))


def dot(a, b, dims):
    return lax.dot_general(a, b, dims, preferred_element_type=F32)


def dot3(a, b, dims):
    return dot(a[0], b[0], dims) + (dot(a[0], b[1], dims) + dot(a[1], b[0], dims))


def lower():
    return lax.broadcasted_iota(jnp.int32, (1, L), 1) < E


def roll(value, shift):
    return pltpu.roll(value, shift, 1)


def shifted(double, block):
    return jnp.where(lower(), roll(double, E - 2 * block), roll(double, E - 1 - 2 * block))


def query_scale(block):
    distance = 2 * block + jnp.where(lower(), 0, 1)
    once = jnp.where(distance > 32, 0.0, 1.0 / E)
    return jnp.where((distance > 0) & (distance < 32), 2.0 / E, once)


def unshifted(term, block):
    low = lower()
    return roll(jnp.where(low, term, 0.0), 2 * block) + roll(jnp.where(low, 0.0, term), 2 * block + 1)


def folded(value):
    return value + roll(value, E)


def columns_of(double):
    high, low = split(double.T)
    return jnp.concatenate([high[:E], low[:E]], axis=0)


def state_block(columns, feats):
    product = dot(columns, feats, NN)
    product = product[:, :L] + product[:, L:]
    return product[:E] + product[E:]


def feature_pair(features):
    return jnp.concatenate(split(features), axis=1)


def rows_of(double):
    high, low = split(double)
    return jnp.concatenate([high[:, :E], low[:, :E], high[:, :E]], axis=1)


def apply_state(pair, parts):
    rows = jnp.concatenate(parts, axis=0)
    return dot(pair, jnp.concatenate([rows, rows], axis=1), NT)


def apply_rows(rows, parts):
    high, low = parts
    return dot(rows, jnp.concatenate([high, high, low], axis=0), NN)


class Chunk:
    def __init__(self, at, chunk, reverse, bufs, sems):
        self.rows, self.piece, self.owners = CHUNKS[chunk]
        self.at, self.reverse = at, reverse
        self.st, self.ry, self.py, self.tot, self.rz, self.pz, self.ez, self.oy, self.out = bufs
        send, recv = [[sem.at[int(reverse), chunk, stage] for stage in range(4)] for sem in sems]
        y, z = at.y, at.z
        self.first = [None] + [
            remote(self.st.at[lax.rem(y + d, NY)], self.ry.at[d], send[0], recv[0], at.py[d]) for d in range(1, NY)
        ]
        self.second, self.third = [None], [None]
        for d in range(1, NZ):
            target = lax.rem(z + d, NZ)
            self.second.append(remote(self.tot.at[self.part(target)], self.rz.at[d], send[1], recv[1], at.pz[d]))
            self.third.append(remote(self.pz.at[target], self.ez.at[self.part(z)], send[2], recv[2], at.pz[d]))
        self.fourth = [None] + [
            remote(self.oy.at[d], self.out.at[y], send[3], recv[3], at.py[d]) for d in range(1, NY)
        ]
        self.send, self.recv = send, recv

    def all_of(self, stage, pieces=NZ - 1):
        ref = self.ry.at[pl.ds(1, NY - 1)] if stage in (0, 3) else self.rz.at[pl.ds(0, pieces)]
        return settle(ref, self.send[stage], self.recv[stage], self.at.py[1])

    def part(self, index):
        return pl.ds(pl.multiple_of(lax.min(index, self.owners - 1) * self.piece, 8), self.piece)

    def owner(self, index, act, otherwise=None):
        if self.owners == NZ:
            act()
        else:
            pl.when(index < self.owners)(act)
            if otherwise is not None:
                pl.when(index >= self.owners)(otherwise)

    def ordered(self, n):
        return range(n - 1, -1, -1) if self.reverse else range(n)

    def totals(self):
        y, z = self.at.y, self.at.z
        self.all_of(0).wait_recv()
        running = jnp.zeros((self.rows, L), F32)
        for index in self.ordered(NY):
            self.py[index] = running
            running = running + self.ry[lax.rem(y + NY - index, NY)]
        self.tot[...] = running
        for d in (4, 3, 5, 2, 6, 1, 7):
            self.owner(lax.rem(z + d, NZ), self.second[d].start)

    def prefixes(self):
        z = self.at.z

        def act():
            self.rz[0] = self.tot[self.part(z)]
            self.all_of(1).wait_recv()
            running = jnp.zeros((self.piece, L), F32)
            for index in self.ordered(NZ):
                self.pz[index] = running
                running = running + self.rz[lax.rem(z + NZ - index, NZ)]
            for d in (4, 3, 5, 2, 6, 1, 7):
                self.third[d].start()
            self.ez[self.part(z)] = self.pz[z]

        self.owner(z, act)

    def spread(self):
        y, z = self.at.y, self.at.z
        self.owner(
            z,
            lambda: self.all_of(2, self.owners - 1).wait_recv(),
            lambda: self.all_of(2, self.owners).wait_recv(),
        )
        for d in (2, 1, 3):
            self.oy[d] = self.ez[...] + self.py[lax.rem(y + d, NY)]
            self.fourth[d].start()
        self.out[y] = self.ez[...] + self.py[y]

    def close(self):
        self.all_of(0).wait_send()
        self.owner(
            self.at.z,
            lambda: self.all_of(1, self.owners - 1).wait_send(),
            lambda: self.all_of(1, self.owners).wait_send(),
        )
        self.owner(self.at.z, lambda: self.all_of(2).wait_send())
        self.all_of(3).wait_send()


class Norms:
    def __init__(self, at, reverse, bufs, sems):
        self.at, self.reverse = at, reverse
        self.own, self.ry, self.tot, self.rz = bufs
        send, recv = [[sem.at[int(reverse), stage] for stage in range(2)] for sem in sems]
        self.first = [remote(self.own, self.ry.at[d], send[0], recv[0], at.py[d]) for d in (2, 1, 3)]
        self.second = [remote(self.tot, self.rz.at[d], send[1], recv[1], at.pz[d]) for d in (4, 3, 5, 2, 6, 1, 7)]
        self.all_first = settle(self.ry.at[pl.ds(1, NY - 1)], send[0], recv[0], at.py[1])
        self.all_second = settle(self.rz.at[pl.ds(1, NZ - 1)], send[1], recv[1], at.pz[1])

    def counts(self, d, index):
        return d > index if self.reverse else d <= index

    def start(self, matrix):
        self.own[...] = jnp.where(lower(), matrix[:32], matrix[32:])
        for copy in self.first:
            copy.start()

    def relay(self):
        self.all_first.wait_recv()
        self.tot[...] = self.own[...] + self.ry[1] + self.ry[2] + self.ry[3]
        for copy in self.second:
            copy.start()

    def result(self):
        self.all_second.wait_recv()
        total = jnp.zeros((32, L), F32)
        for d in range(1, NZ):
            total = total + jnp.where(self.counts(d, self.at.z), self.rz[d], 0.0)
        for d in range(1, NY):
            total = total + jnp.where(self.counts(d, self.at.y), self.ry[d], 0.0)
        turned = roll(total, E)
        low = lower()
        return split(jnp.concatenate([jnp.where(low, total, turned), jnp.where(low, turned, total)], axis=0))

    def close(self):
        self.all_first.wait_send()
        self.all_second.wait_send()


def fill(at, chunk, h, make):
    if h == WITH_LAST:
        rows = make(LAST)
        for q in range(NY):
            chunk.st[q, E:] = rows[q * 16 : (q + 1) * 16]
        chunk.ry[0, E:] = chunk.st[at.y, E:]
    for d in (2, 1, 3, 0):
        q = lax.rem(at.y + d, NY)
        block = make(4 * h + q)
        if d == 0:
            chunk.ry[0, :E] = block
        else:
            chunk.st[q, :E] = block
            chunk.first[d].start()


def tail_of(chunks):
    return split(jnp.concatenate([chunks[WITH_LAST].out[q, E:] for q in range(NY)], axis=0))


def over_blocks(at, chunk, h, step, carry, wait):
    for d in range(NY):
        if wait and d == 1:
            chunk.all_of(3).wait_recv()
        q = lax.rem(at.y + NY - d, NY)
        carry = step(4 * h + q, split(chunk.out[q, :E]), carry)
    return carry


def fused_kernel(names, *refs):
    r = types.SimpleNamespace(**dict(zip(names, refs)))
    x, y, z, c = place()
    at = types.SimpleNamespace(x=x, y=y, z=z, c=c)
    sibling = device(x, y, z, 1 - c)
    at.px = [None] + [device(lax.rem(x + d, NX), y, z, c) for d in range(1, NX)]
    at.py = [None] + [device(x, lax.rem(y + d, NY), z, c) for d in range(1, NY)]
    at.pz = [None] + [device(x, y, lax.rem(z + d, NZ), c) for d in range(1, NZ)]
    low = lower()

    barrier = pltpu.get_barrier_semaphore()
    peers = [sibling] + at.px[1:] + at.py[1:] + at.pz[1:]
    for peer in peers:
        pl.semaphore_signal(barrier, inc=1, device_id=peer, device_id_type=MESH)
    mine = pl.ds(pl.multiple_of(c * 128, 128), 128)
    load_x = pltpu.make_async_copy(r.x_in, r.xg.at[x, mine], r.wsem.at[1])
    load_g = pltpu.make_async_copy(r.g_in, r.gg.at[mine], r.wsem.at[2])
    load = pltpu.make_async_copy(r.w_in, r.w, r.wsem.at[0])
    for copy in (load_x, load_g, load):
        copy.start()
    load.wait()

    def split_weights(b, carry):
        rows = pl.ds(pl.multiple_of(b * 256, 256), 256)
        for i in range(3):
            r.wh[i, rows], r.wl[i, rows] = split(r.w[i, rows])
        return carry

    lax.fori_loop(0, NX, split_weights, 0)
    load_x.wait()
    load_g.wait()
    pl.semaphore_wait(barrier, len(peers))

    over_x = [[None] * NX, [None] * NX]
    forwards = [[None] * NX, [None] * NX]
    halves = [pl.ds(pl.multiple_of(c * 128 + 64 * k, 64), 64) for k in range(2)]
    for k in range(2):
        for d in (1, 3, 2):
            over_x[k][d] = remote(
                r.xg.at[x, halves[k]], r.xg.at[x, halves[k]], r.xs, r.xr.at[k, d], at.px[d]
            )
            over_x[k][d].start()
    own = remote(r.xg.at[x, mine], r.xg.at[x, mine], r.cs.at[0], r.cr.at[0], sibling)
    own.start()
    grads = remote(r.gg.at[mine], r.gg.at[mine], r.cs.at[1], r.cr.at[1], sibling)
    grads.start()

    def project(b, sums):
        rows = pl.ds(pl.multiple_of(b * 256, 256), 256)
        r.xh[b], r.xl[b] = split(r.xg[b])
        feats = (r.xh[b], r.xl[b])
        return [sums[i] + dot3(feats, (r.wh[i, rows], r.wl[i, rows]), NN) for i in range(3)]

    own.wait_recv()
    sums = project(x, [jnp.zeros((T, L), F32) for _ in range(3)])
    for k in range(2):
        for d in (1, 3, 2):
            over_x[k][d].wait_recv()
            landed = r.xg.at[lax.rem(x + NX - d, NX), halves[k]]
            forwards[k][d] = remote(landed, landed, r.fs, r.fr.at[k, d], sibling)
            forwards[k][d].start()
    for d in (1, 3, 2):
        for k in range(2):
            forwards[k][d].wait_recv()
        sums = project(lax.rem(x + NX - d, NX), sums)

    def doubled(both):
        return jnp.where(low == (c == 0), both, roll(both, E))

    r.qq[...] = doubled(sums[0])
    r.kk[...] = doubled(sums[1])
    r.vv[...] = doubled(sums[2])

    scans = []
    for reverse in (False, True):
        bufs = [[buf[int(reverse)][h] for buf in r.bufs] for h in range(len(CHUNKS))]
        scans.append([Chunk(at, h, reverse, bufs[h], r.sems) for h in range(len(CHUNKS))])
    earlier, later = scans

    norms, adjoint_norms = [Norms(at, v, r.small[int(v)], r.small_sems) for v in (False, True)]
    ks = split(r.kk[...])
    norms.start(dot3([v[:, :E] for v in ks], ks, TN))

    r.cols[...] = columns_of(r.vv[...])

    def key_block(block):
        kk = r.kk[...]
        return state_block(r.cols[...], feature_pair(kk * shifted(kk, block)))

    for h in range(4):
        if h == 2:
            norms.relay()
        fill(at, earlier[h], h, key_block)

    def query_feature(block, carry):
        qq = r.qq[...]
        r.feats[block] = feature_pair(qq * shifted(qq, block) * query_scale(block))
        return carry

    for h, chunk in enumerate(earlier):
        chunk.totals()
        lax.fori_loop(4 * h, 4 * h + 4, query_feature, 0)
    query_feature(LAST, 0)
    grads.wait_recv()
    causal = lax.broadcasted_iota(jnp.int32, (T, T), 0) >= lax.broadcasted_iota(jnp.int32, (T, T), 1)
    qs, ks, vs = [split(ref[...]) for ref in (r.qq, r.kk, r.vv)]
    r.dots[...] = dot3([v[:, :E] for v in qs], [v[:, :E] for v in ks], NT)
    weights = jnp.where(causal, r.dots[...] * r.dots[...] * (1.0 / E), 0.0)
    r.wgh[...], r.wgl[...] = split(weights)
    near = 1.0 + jnp.sum(weights, axis=1, keepdims=True)

    r.normed[...] = dot3([v[:, :E] for v in qs], norms.result(), NN)
    denom = near + jnp.sum(r.normed[...] * r.qq[...], axis=1, keepdims=True) * (0.5 / E)
    r.inverse[...] = jnp.broadcast_to(1.0 / denom, (T, L))
    r.gn[...] = doubled(r.gg[...]) * r.inverse[...]
    r.cols[...] = columns_of(r.gn[...])

    def query_block(block):
        return state_block(r.cols[...], r.feats[block])

    for h in range(4):
        fill(at, later[h], h, query_block)
    for chunk in earlier:
        chunk.prefixes()

    def transposed(b, carry):
        for to, value in ((r.xth, r.xh[b]), (r.xtl, r.xl[b])):
            r.turned[...] = value.T
            for i in range(8):
                rows = pl.ds(pl.multiple_of(i * 32 + c * 16, 16), 16)
                to[pl.ds(pl.multiple_of(b * 128 + i * 16, 16), 16)] = r.turned[rows]
        return carry

    lax.fori_loop(0, NX, transposed, 0)
    for h in range(4):
        earlier[h].spread()
        later[h].totals()

    gs = split(r.gn[...])
    r.numer[...] = dot3((r.wgh[...], r.wgl[...]), vs, NN)
    r.dv[...] = dot3((r.wgh[...], r.wgl[...]), gs, TN)
    r.scores[...] = dot3([v[:, :E] for v in gs], [v[:, :E] for v in vs], NT)
    r.rows[...] = rows_of(r.gn[...])

    def forward(block, parts, total):
        return total + apply_state(r.feats[block], parts)

    def backward(block, parts, carry):
        one, two = carry
        qq = r.qq[...]
        grad = apply_rows(r.rows[...], parts) * query_scale(block)
        return one + grad * shifted(qq, block), two + unshifted(grad * qq, block)

    r.one[...] = jnp.zeros((T, L), F32)
    r.two[...] = jnp.zeros((T, L), F32)

    def query_gradient(h):
        carry = (r.one[...], r.two[...])
        r.one[...], r.two[...] = over_blocks(at, earlier[h], h, backward, carry, False)

    r.total[...] = jnp.zeros((T, L), F32)
    for h in range(4):
        r.total[...] = over_blocks(at, earlier[h], h, forward, r.total[...], True)
        if h < 3:
            query_gradient(h)
        if h in (1, 2):
            later[h - 1].prefixes()
    total = r.total[...] + apply_state(r.feats[LAST], tail_of(earlier))
    outputs = r.numer[...] + folded(total)
    r.gd[...] = jnp.sum(r.gn[...] * outputs, axis=1, keepdims=True) * r.inverse[...] * -0.5
    qq = r.qq[...]
    adjoint_norms.start(dot3(split((qq * r.gd[...])[:, :E]), split(qq), TN) * (1.0 / E))
    later[2].prefixes()
    later[3].prefixes()

    query_gradient(3)
    later[0].spread()
    later[1].spread()
    carry = backward(LAST, tail_of(earlier), (r.one[...] + r.normed[...] * r.gd[...] * (1.0 / E), r.two[...]))
    r.one[...], r.two[...] = carry
    qs, ks = [split(ref[...]) for ref in (r.qq, r.kk)]
    grad_scores = jnp.where(causal, r.scores[...] + r.gd[:, :1], 0.0)
    r.gdh[...], r.gdl[...] = split(grad_scores * r.dots[...] * (2.0 / E))
    r.dq[...] = folded(r.one[...] + r.two[...]) + dot3((r.gdh[...], r.gdl[...]), ks, NN)
    give_q = remote(r.dq, r.dqo, r.cs.at[2], r.cr.at[2], sibling)
    give_q.start()
    adjoint_norms.relay()
    for chunk in later[2:]:
        chunk.spread()
    r.dk[...] = dot3((r.gdh[...], r.gdl[...]), qs, TN)
    r.rows[...] = rows_of(r.vv[...])
    give_q.wait_recv()
    own_lanes = low == (c == 0)
    r.gh[0], r.gl[0] = split(jnp.where(own_lanes, r.dq[...], r.dqo[...]))
    for h in range(2):
        rows = pl.ds(h * 256, 256)
        grad = dot3((r.xth[rows], r.xtl[rows]), (r.gh[0], r.gl[0]), NN)
        for i in range(16):
            r.dwq[i % NY, 4 * h + i // NY] = grad[i * 16 : (i + 1) * 16]
    q_y = [
        remote(r.dwq.at[lax.rem(y + d, NY)], r.qry.at[d], r.qs.at[0], r.qr.at[0], at.py[d]) for d in (2, 1, 3)
    ]
    all_q_y = settle(r.qry.at[pl.ds(1, NY - 1)], r.qs.at[0], r.qr.at[0], at.py[1])
    all_q_z = settle(r.qrz.at[pl.ds(1, NZ - 1)], r.qs.at[1], r.qr.at[1], at.pz[1])

    def keys(block, parts, carry, mask=None):
        total, one, two = carry
        kk = r.kk[...]
        shift = shifted(kk, block)
        if mask is not None:
            shift, kk = jnp.where(mask, shift, 0.0), jnp.where(mask, kk, 0.0)
        total = total + apply_state(feature_pair(kk * shift), parts)
        grad = apply_rows(r.rows[...], parts)
        return total, one + grad * shift, two + unshifted(grad * kk, block)

    zero = jnp.zeros((T, L), F32)
    carry = (zero, zero, zero)
    for h in range(4):
        if h == 3:
            later[3].all_of(3).wait_recv()
            for copy in q_y:
                copy.start()
        carry = over_blocks(at, later[h], h, keys, carry, h < 3)
    total, one, two = keys(LAST, tail_of(later), carry, low)
    ks = split(r.kk[...])
    dv = r.dv[...] + folded(total)
    r.kv[0] = dv
    give_v = remote(r.kv.at[0], r.kvo.at[0], r.cs.at[3], r.cr.at[3], sibling)
    give_v.start()
    normed = dot3([v[:, :E] for v in ks], adjoint_norms.result(), NN)
    dk = r.dk[...] + folded(one + two) + 2.0 * normed
    r.kv[1] = dk
    give_k = remote(r.kv.at[1], r.kvo.at[1], r.cs.at[4], r.cr.at[4], sibling)
    give_k.start()
    give_v.wait_recv()
    r.gh[2], r.gl[2] = split(jnp.where(own_lanes, dv, r.kvo[0]))
    give_k.wait_recv()
    r.gh[1], r.gl[1] = split(jnp.where(own_lanes, dk, r.kvo[1]))

    kv = [jnp.concatenate([g[1], g[2]], axis=1) for g in (r.gh, r.gl)]
    first = []
    for h in range(4):
        rows = pl.ds(h * 128, 128)
        grad = dot3((r.xth[rows], r.xtl[rows]), kv, NN)
        for i in range(8):
            r.dw[h, i % NY, i // NY] = grad[i * 16 : (i + 1) * 16]
        for d in (2, 1, 3):
            remote(
                r.dw.at[h, lax.rem(y + d, NY)], r.wry.at[h, d], r.ws.at[h], r.wr.at[h], at.py[d]
            ).start()
        first.append(settle(r.wry.at[h, pl.ds(1, NY - 1)], r.ws.at[h], r.wr.at[h], at.py[1]))

    all_q_y.wait_recv()
    r.qty[...] = r.dwq[y] + r.qry[1] + r.qry[2] + r.qry[3]
    for d in (4, 3, 5, 2, 6, 1, 7):
        remote(r.qty.at[lax.rem(z + d, NZ)], r.qrz.at[d], r.qs.at[1], r.qr.at[1], at.pz[d]).start()

    for d in (2, 1, 3, 0):
        rows = pl.ds(pl.multiple_of(lax.rem(x + d, NX) * 256, 256), 256)
        part = jnp.zeros((128, 256), F32)
        for i in range(3):
            part = part + dot3((r.gh[i, mine], r.gl[i, mine]), (r.wh[i, rows], r.wl[i, rows]), NT)
        r.sx[d] = part
        if d:
            remote(r.sx.at[d], r.rx.at[d], r.os.at[0], r.os.at[1], at.px[d]).start()
    all_x = settle(r.rx.at[pl.ds(1, NX - 1)], r.os.at[0], r.os.at[1], at.px[1])

    for h in range(4):
        first[h].wait_recv()
        r.wty[h] = r.dw[h, y] + r.wry[h, 1] + r.wry[h, 2] + r.wry[h, 3]
        for j in range(2):
            target = 2 * h + j
            d = lax.rem(target - z + NZ, NZ)
            copy = remote(r.wty.at[h, j], r.wrz.at[d], r.ws.at[4], r.wr.at[4], device(x, y, target, c))
            pl.when(target != z)(copy.start)
    all_x.wait_recv()
    r.gx[...] = r.sx[0] + r.rx[1] + r.rx[2] + r.rx[3]
    all_q_z.wait_recv()
    total = r.qty[z]
    for d in range(1, NZ):
        total = total + r.qrz[d]
    r.gw[0] = total
    for copy in [own, grads, give_q, give_k, give_v, all_q_y, all_q_z, all_x] + first:
        copy.wait_send()
    settle(r.xg.at[pl.ds(0, 3), pl.ds(0, 128)], r.xs, r.xr.at[0, 0], at.px[1]).wait_send()
    settle(r.xg.at[pl.ds(0, 3), pl.ds(0, 128)], r.fs, r.fr.at[0, 0], sibling).wait_send()
    for group in earlier + later + [norms, adjoint_norms]:
        group.close()
    all_z = settle(r.wrz.at[pl.ds(1, NZ - 1)], r.ws.at[4], r.wr.at[4], at.pz[1])
    all_z.wait_recv()
    total = r.wty[lax.div(z, 2), lax.rem(z, 2)]
    for d in range(1, NZ):
        total = total + r.wrz[d]
    r.gw[1] = total[:, :L]
    r.gw[2] = total[:, L:]
    all_z.wait_send()


def fused(inputs, weights, out_grads):
    dma = pltpu.SemaphoreType.DMA

    def vm(*shape, dtype=F32):
        return pltpu.VMEM(shape, dtype)

    scratch = dict(
        w=vm(3, 1024, L),
        wh=vm(3, 1024, L, dtype=BF16),
        wl=vm(3, 1024, L, dtype=BF16),
        xg=vm(NX, T, 256),
        xh=vm(NX, T, 256, dtype=BF16),
        xl=vm(NX, T, 256, dtype=BF16),
        gg=vm(T, L),
        qq=vm(T, L),
        kk=vm(T, L),
        vv=vm(T, L),
        cols=vm(L, T, dtype=BF16),
        rows=vm(T, 3 * E, dtype=BF16),
        feats=vm(LAST + 1, T, 2 * L, dtype=BF16),
        dots=vm(T, T),
        wgh=vm(T, T, dtype=BF16),
        wgl=vm(T, T, dtype=BF16),
        numer=vm(T, L),
        inverse=vm(T, L),
        normed=vm(T, L),
        total=vm(T, L),
        scores=vm(T, T),
        gn=vm(T, L),
        gd=vm(T, L),
        one=vm(T, L),
        dq=vm(T, L),
        dk=vm(T, L),
        dv=vm(T, L),
        two=vm(T, L),
        gdh=vm(T, T, dtype=BF16),
        gdl=vm(T, T, dtype=BF16),
        dqo=vm(T, L),
        kv=vm(2, T, L),
        kvo=vm(2, T, L),
        gh=vm(3, T, L, dtype=BF16),
        gl=vm(3, T, L, dtype=BF16),
        turned=vm(256, T, dtype=BF16),
        xth=vm(512, T, dtype=BF16),
        xtl=vm(512, T, dtype=BF16),
        dwq=vm(NY, NZ, 16, L),
        qry=vm(NY, NZ, 16, L),
        qty=vm(NZ, 16, L),
        qrz=vm(NZ, 16, L),
        dw=vm(4, NY, 2, 16, 2 * L),
        wry=vm(4, NY, 2, 16, 2 * L),
        wty=vm(4, 2, 16, 2 * L),
        wrz=vm(NZ, 16, 2 * L),
        sx=vm(NX, 128, 256),
        rx=vm(NX, 128, 256),
    )
    sems = dict(
        wsem=dma((3,)),
        xs=dma,
        xr=dma((2, NX)),
        fs=dma,
        fr=dma((2, NX)),
        cs=dma((5,)),
        cr=dma((5,)),
        qs=dma((2,)),
        qr=dma((2,)),
        ws=dma((5,)),
        wr=dma((5,)),
        os=dma((2,)),
    )
    bufs = [
        [
            [
                vm(NY, rows, L),
                vm(NY, rows, L),
                vm(NY, rows, L),
                vm(rows, L),
                vm(NZ, piece, L),
                vm(NZ, piece, L),
                vm(rows, L),
                vm(NY, rows, L),
                vm(NY, rows, L),
            ]
            for rows, piece, _ in CHUNKS
        ]
        for _ in range(2)
    ]
    small = [vm(*shape, 32, L) for _ in range(2) for shape in ((), (NY,), (), (NZ,))]
    scan_sems = [dma((2, len(CHUNKS), 4)), dma((2, len(CHUNKS), 4)), dma((2, 2)), dma((2, 2))]
    flat = list(scratch.values()) + list(sems.values()) + [b for s in bufs for h in s for b in h] + small + scan_sems
    names = ["x_in", "w_in", "g_in", "gx", "gw"] + list(scratch) + list(sems)

    def kernel(*refs):
        named, rest = refs[: len(names)], refs[len(names) :]
        count = len(CHUNKS)
        held = [[[rest[(s * count + h) * 9 + i] for h in range(count)] for s in range(2)] for i in range(9)]
        rest = rest[18 * count :]
        fused_kernel(
            names + ["bufs", "small", "sems", "small_sems"], *named, held, (rest[:4], rest[4:8]), rest[8:10], rest[10:]
        )

    return pl.pallas_call(
        kernel,
        out_shape=(jax.ShapeDtypeStruct((128, 256), F32), jax.ShapeDtypeStruct((3, 16, L), F32)),
        in_specs=[pl.BlockSpec(memory_space=pl.ANY)] * 3,
        out_specs=(VMEM, VMEM),
        scratch_shapes=flat,
        compiler_params=pltpu.CompilerParams(collective_id=0, has_side_effects=True, vmem_limit_bytes=LIMIT),
        name="fused",
    )(inputs, weights, out_grads)


def finish_kernel(gx, gw, dx, dw):
    dx[...] = gx[...]
    dw[...] = gw[...]


def per_device(inputs, proj_weights, out_grads):
    gx, gw = fused(inputs, proj_weights.transpose(1, 0, 2), out_grads)
    dx, dw = pl.pallas_call(
        finish_kernel,
        out_shape=(jax.ShapeDtypeStruct((128, 256), F32), jax.ShapeDtypeStruct((3, 16, L), F32)),
        in_specs=[VMEM, VMEM],
        out_specs=(VMEM, VMEM),
        name="finish",
    )(gx, gw)
    return dx, dw.transpose(1, 0, 2)


def solution(mesh):
    return jax.shard_map(
        per_device,
        mesh=mesh,
        in_specs=(P("seq", "head"), P(None, None, "head"), P("seq", "head")),
        out_specs=(P("seq", "head"), P("seq", None, "head")),
        check_vma=False,
    )
```
